32 devices in a mesh: tm: 4 (over y, x), rows: 8 (over z, core).
Axes of the slice: x: 2, y: 2, z: 4, core: 2. Of those that a mesh axis runs over, the one named last changes fastest.
Arguments:
- frames: bfloat16 [16, 64, 1280, 128], P('tm', 'rows'), may hold values from -30 to 30
- clip_ids: int32 [16], replicated, may hold values from 0 to 3, never falling along the last dimension, each value on 1 to 6 neighbouring positions
- conv_weight: bfloat16 [3, 3, 3, 128, 256], replicated, may hold values from -0.109375 to 0.109375
- norm_gain: float32 [256], replicated, may hold values from 0.1 to 1.9
- norm_bias: float32 [256], replicated, may hold values from -3 to 3
Outputs:
- latent: bfloat16 [16, 32, 640, 256], P('tm', None, 'rows')
The draws below stay inside these ranges and needn't reach their ends.
Inputs may be any that keep to these rules, and one draw needn't show every extreme that they name: `clip_ids`: clip numbers never fall along the frames; each clip spans 1 to 6 frames, one exactly 6.
All inputs are finite; a program needn't handle non-finite values.
Results may differ from the reference program's by a relative error of at most 0.012.
Values may be sent and summed in bfloat16 or wider, within the bound.
No kernel may reach another device: no remote copies, remote signals or barrier semaphores. Data moves between devices by JAX's collectives and lax.ppermute only.
A program may use at most 192 MiB of HBM per device.

```python
import math
import jax
import jax.numpy as jnp
import numpy as np
from jax import lax

CI = 128
CO = 256
GROUPS = 32
WIDTH = 1280
CLIPS = 4
CLIP_MOST = 6
NF = 16
H = 64
HO = 32
WO = 640


def draw_frames(key, part):
    key_values = jax.random.fold_in(key, 11)
    key_channels = jax.random.fold_in(key, 12)
    heights = jnp.arange(H, dtype=jnp.float32) / (H - 1)
    channel_scale = jnp.exp(jax.random.uniform(key_channels, (CI,), jnp.float32, 0.0, 1.1))
    base = jnp.clip(jax.random.normal(key_values, (NF, H, WIDTH, CI), jnp.float32), -5.0, 5.0)
    base = base * (1.0 + 2.0 * heights)[None, :, None, None]
    return (base * channel_scale * 0.5).astype(jnp.bfloat16)


def length_profile(amount, total, bound, skew):
    portions = [(1 << 20) // math.isqrt(standing ** skew) + 1 for standing in range(2, amount + 1)]
    surplus, given = total - bound - (amount - 1), [1] * (amount - 1)
    while surplus > 0:
        movable = [i for i in range(amount - 1) if given[i] < bound]
        mass, remaining = sum([portions[i] for i in movable]), surplus
        for i in movable:
            more = min(bound - given[i], max(1, remaining * portions[i] // mass), surplus)
            given[i] = given[i] + more
            surplus = surplus - more
    return np.array([bound] + given)


def ragged(rng, number_of, total, bound, skew):
    if number_of == 2:
        one = jax.random.randint(rng, (), max(1, total - bound), min(bound, total - 1) + 1)
        return jnp.stack([one, total - one])
    tallies = jnp.asarray(length_profile(number_of, total, bound, skew), jnp.int32)
    pairs = (number_of - 1) // 2
    giver, taker = tallies[1:1 + 2 * pairs:2], tallies[2:2 + 2 * pairs:2]
    margin = jnp.minimum(giver - 1, bound - taker)
    passed = jax.random.randint(jax.random.fold_in(rng, 1), (pairs,), 0, 1 << 20) % (margin + 1)
    tallies = tallies.at[1:1 + 2 * pairs:2].set(giver - passed).at[2:2 + 2 * pairs:2].set(taker + passed)
    return tallies[jax.random.permutation(jax.random.fold_in(rng, 2), number_of)]


def normal_values(own_key, extent, deviation, most, kind=jnp.bfloat16):
    return jnp.clip(deviation * jax.random.normal(own_key, extent, jnp.float32), -most, most).astype(kind)


def setup_inputs(seed: int = 0) -> dict:
    splits = jax.random.split(jax.random.key(seed), 6)
    frames = draw_frames(jax.random.fold_in(splits[5], 71), 0)
    clip_ids = jnp.searchsorted(jnp.cumsum(ragged(splits[1], CLIPS, NF, CLIP_MOST, 2)), jnp.arange(NF), side="right").astype(jnp.int32)
    conv_weight = normal_values(splits[2], (3, 3, 3, CI, CO), (27 * CI) ** -0.5, 0.109375)
    norm_gain = jnp.clip(1.0 + 0.18 * jax.random.normal(splits[3], (CO,), jnp.float32), 0.1, 1.9)
    norm_bias = normal_values(splits[4], (CO,), 0.5, 3.0, jnp.float32)
    return dict(frames=frames, clip_ids=clip_ids, conv_weight=conv_weight, norm_gain=norm_gain, norm_bias=norm_bias)


def plane_conv(image, kernel):
    return lax.conv_general_dilated(image[None], kernel.astype(jnp.float32), (2, 2), ((1, 1), (1, 1)), dimension_numbers=('NHWC', 'HWIO', 'NHWC'))[0]

def reference(frames, clip_ids, conv_weight, norm_gain, norm_bias):

    def one_frame(frame_at):
        running = jnp.zeros((HO, WO, CO), jnp.float32)
        for tap_index in range(3):
            source = frame_at - 2 + tap_index
            safe = jnp.maximum(source, 0).astype(jnp.int32)
            valid = jnp.logical_and(source >= 0, clip_ids[safe] == clip_ids[frame_at])
            image = lax.dynamic_index_in_dim(frames, safe, 0, keepdims=False).astype(jnp.float32)
            image = image * valid.astype(jnp.float32)
            running = running + plane_conv(image, conv_weight[tap_index])
        return running.astype(jnp.bfloat16)
    conv = lax.map(one_frame, jnp.arange(NF, dtype=jnp.int32))
    values = conv.astype(jnp.float32).reshape(NF, HO, WO, GROUPS, CO // GROUPS)
    mean = lax.optimization_barrier(jnp.mean(values, axis=(1, 2, 4)))
    variance = lax.optimization_barrier(jnp.mean(values * values, axis=(1, 2, 4))) - mean * mean
    scaled = (values - mean[:, None, None, :, None]) * lax.rsqrt(variance + 1e-05)[:, None, None, :, None]
    scaled = scaled.reshape(NF, HO, WO, CO) * norm_gain + norm_bias
    return jax.nn.silu(scaled).astype(jnp.bfloat16)
```

```python
import functools

import jax
import jax.numpy as jnp
from jax import lax
from jax.experimental import pallas as pl
from jax.experimental.pallas import tpu as pltpu
from jax.sharding import PartitionSpec as P

GROUPS = 32
EPS = 1e-05
VMEM_BYTES = 40 * 1024 * 1024


def passed_along(array, axis, by):
    length = lax.axis_size(axis)
    pairs = [(i, i + by) for i in range(length) if 0 <= i + by < length]
    return lax.ppermute(array, axis, pairs)


def exchanged(array, axis, flip):
    length = lax.axis_size(axis)
    return lax.ppermute(array, axis, [(i, i ^ flip) for i in range(length)])


def after(array, *earlier):
    return lax.optimization_barrier((array, *earlier))[0]


def rounded_up(rows):
    return -(-rows // 16) * 16


def split_columns(row_ref, slab_ref):
    width, ci = row_ref.shape
    half = width // 2
    slab_ref[:, ci : 2 * ci] = row_ref[pl.ds(0, half, stride=2), :]
    slab_ref[:, 2 * ci :] = row_ref[pl.ds(1, half, stride=2), :]
    slab_ref[16:, 0:ci] = row_ref[pl.ds(31, half - 16, stride=2), :]
    head = row_ref[pl.ds(1, 16, stride=2), :].astype(jnp.float32)
    zero = jnp.zeros((1, ci), jnp.float32)
    slab_ref[0:16, 0:ci] = jnp.concatenate([zero, head[:15]], axis=0).astype(jnp.bfloat16)


def split_three(total):
    high = total.astype(jnp.bfloat16).astype(jnp.float32)
    rest = total - high
    middle = rest.astype(jnp.bfloat16).astype(jnp.float32)
    return [high, middle, rest - middle]


def conv_kernel(plan, clip_ref, place_ref, x_ref, above_ref, w_ref, *refs):
    jobs, parts, part_rows, part_width = (
        plan["jobs"], plan["parts"], plan["part_rows"], plan["part_width"])
    lead, tail, steps = plan["lead"], plan["tail"], plan["steps"]

    def take(number):
        nonlocal refs
        some, refs = refs[:number], refs[number:]
        return some

    add_refs = take(plan["addends"])
    lead_refs = take(parts if lead else 0)
    sums_refs = take(plan["sums_in"])
    out_refs = take(parts if parts else len(jobs))
    sums_out = take(1 if plan["sums_out"] else 0)
    slab_ref, acc_ref, part_ref, stat_ref = refs
    step = pl.program_id(0)
    sources = x_ref.shape[0]
    half = slab_ref.shape[2]
    above = lax.rem(step + 1, 2)
    below = lax.rem(step, 2)
    start = place_ref[0]
    last = clip_ref.shape[0] - 1

    @pl.when(step == 0)
    def _():
        for source in range(sources):
            split_columns(above_ref.at[source, 0], slab_ref.at[source, 1])
        stat_ref[...] = jnp.zeros_like(stat_ref)
        for flip in range(parts if lead else 0):
            out_refs[flip][0:lead] = lead_refs[flip][...]

    for source in range(sources):
        split_columns(x_ref.at[source, 0], slab_ref.at[source, 2])
        split_columns(x_ref.at[source, 1], slab_ref.at[source, below])

    def product(source, tap):
        rows = jnp.concatenate(
            [slab_ref[source, above], slab_ref[source, 2], slab_ref[source, below]], axis=1)
        return jnp.dot(rows, w_ref[tap], preferred_element_type=jnp.float32)

    for at, (target, taps, addend) in enumerate(jobs):
        empty = addend is None
        if addend is not None:
            acc_ref[...] = add_refs[addend][0].astype(jnp.float32)
        for source, tap in taps:
            frame = plan["first"] + source
            if frame == target:
                value = product(source, tap)
                acc_ref[...] = value if empty else acc_ref[...] + value
                empty = False
                continue
            if empty:
                acc_ref[...] = jnp.zeros_like(acc_ref)
                empty = False
            same = clip_ref[start + frame] == clip_ref[jnp.minimum(start + target, last)]

            @pl.when(same)
            def _(source=source, tap=tap):
                acc_ref[...] += product(source, tap)

        if not parts:
            out_refs[at][0] = acc_ref[...].astype(jnp.bfloat16)
            continue
        rounded = acc_ref[...].astype(jnp.bfloat16).astype(jnp.float32)
        tiles = rounded.reshape(half // 8, 8, rounded.shape[1])
        stat_ref[2 * at] += jnp.sum(tiles, axis=0)
        stat_ref[2 * at + 1] += jnp.sum(tiles * tiles, axis=0)
        for part in range(parts):
            piece = rounded[part * part_width : (part + 1) * part_width]
            part_ref[part, 0:part_width] = piece.astype(jnp.bfloat16)
        mine = place_ref[1]
        for flip in range(parts):
            offset = pl.multiple_of(lead + (at * steps + step) * part_rows, 16)
            out_refs[flip][pl.ds(offset, part_rows)] = part_ref[mine ^ flip]

    if sums_out or tail:
        @pl.when(step == steps - 1)
        def _():
            if sums_out:
                sums_out[0][...] = stat_ref[...]
            if tail:
                sums = [sum(ref[at] for ref in sums_refs)
                        for at in range(sums_refs[0].shape[0] if sums_refs else 0)]
                sums += [stat_ref[at] for at in range(2 * len(jobs))]
                rows = []
                for total in sums:
                    rows += split_three(jnp.sum(total, axis=0, keepdims=True))
                blank = jnp.zeros((tail - len(rows), rows[0].shape[1]), jnp.float32)
                closing = jnp.concatenate(rows + [blank], axis=0).astype(jnp.bfloat16)
                body = lead + len(jobs) * steps * part_rows
                for flip in range(parts):
                    out_refs[flip][body : body + tail] = closing


def conv_frames(frames, halo, weight, clip_ids, place, first, sources, jobs, row=0, steps=None,
                addends=(), parts=0, leads=(), sums=(), sums_out=False, tail=0):
    _, band, width, ci = frames.shape
    co = weight.shape[2]
    half = width // 2
    steps = steps or band // 2
    part_width = half // parts if parts else half
    part_rows = rounded_up(part_width)
    lead = leads[0].shape[0] if leads else 0
    plan = dict(jobs=jobs, addends=len(addends), parts=parts, part_rows=part_rows, lead=lead,
                part_width=part_width, first=first, steps=steps, tail=tail,
                sums_in=len(sums), sums_out=sums_out)
    block = first // sources
    above = (frames, 2 * row - 1) if row else (halo, 0)
    in_specs = [
        pl.BlockSpec((sources, 2, width, ci), lambda i, *_: (block, row + i, 0, 0)),
        pl.BlockSpec((sources, 1, width, ci), lambda i, *_: (block, above[1], 0, 0)),
        pl.BlockSpec(weight.shape, lambda i, *_: (0, 0, 0)),
    ]
    in_specs += [pl.BlockSpec((1, None, half, co), lambda i, *_: (0, i, 0, 0)) for _ in addends]
    in_specs += [pl.BlockSpec(a.shape, lambda i, *_: (0, 0)) for a in leads]
    in_specs += [pl.BlockSpec(a.shape, lambda i, *_: (0, 0, 0)) for a in sums]
    if parts:
        message = (lead + len(jobs) * steps * part_rows + tail, co)
        out_shape = [jax.ShapeDtypeStruct(message, jnp.bfloat16) for _ in range(parts)]
        out_specs = [pl.BlockSpec(message, lambda i, *_: (0, 0)) for _ in range(parts)]
    else:
        out_shape = [jax.ShapeDtypeStruct((1, steps, half, co), jnp.bfloat16) for _ in jobs]
        out_specs = [pl.BlockSpec((1, None, half, co), lambda i, *_: (0, i, 0, 0)) for _ in jobs]
    if sums_out:
        shape = (2 * len(jobs), 8, co)
        out_shape.append(jax.ShapeDtypeStruct(shape, jnp.float32))
        out_specs.append(pl.BlockSpec(shape, lambda i, *_: (0, 0, 0)))
    products = sum(len(taps) for _, taps, _ in jobs)
    return pl.pallas_call(
        functools.partial(conv_kernel, plan),
        out_shape=out_shape,
        grid_spec=pltpu.PrefetchScalarGridSpec(
            num_scalar_prefetch=2,
            grid=(steps,),
            in_specs=in_specs,
            out_specs=out_specs,
            scratch_shapes=[
                pltpu.VMEM((sources, 3, half, 3 * ci), jnp.bfloat16),
                pltpu.VMEM((half, co), jnp.float32),
                pltpu.VMEM((max(parts, 1), part_rows, co), jnp.bfloat16),
                pltpu.VMEM((2 * len(jobs), 8, co), jnp.float32),
            ],
        ),
        cost_estimate=pl.CostEstimate(
            flops=2 * products * steps * half * 9 * ci * co,
            bytes_accessed=4 * sources * steps * width * ci + 2 * len(jobs) * steps * half * co,
            transcendentals=0,
        ),
        compiler_params=pltpu.CompilerParams(vmem_limit_bytes=VMEM_BYTES),
    )(clip_ids, place, frames, above[0], weight, *addends, *leads, *sums)


def norm_kernel(plan, place_ref, *refs):
    parts, jobs, entries, held = plan["parts"], plan["jobs"], plan["entries"], plan["held"]
    early_refs = refs[:parts] if plan["early"] else ()
    refs = refs[len(early_refs):]
    data_refs, tail_refs = refs[:parts], refs[parts : 2 * parts]
    gain_ref, bias_ref = refs[2 * parts : 2 * parts + 2]
    out_ref, scale_ref = refs[-2:]
    frame, row = pl.program_id(0), pl.program_id(1)
    part_width, co = out_ref.shape[-2:]

    @pl.when((frame == 0) & (row == 0))
    def _():
        total = tail_refs[0][...].astype(jnp.float32)
        for flip in range(1, parts):
            total = total + tail_refs[flip][...].astype(jnp.float32)
        size = co // GROUPS
        same = (lax.broadcasted_iota(jnp.int32, (co, co), 0) // size
                == lax.broadcasted_iota(jnp.int32, (co, co), 1) // size).astype(jnp.float32)
        grouped = jnp.dot(total, same, precision=lax.Precision.HIGHEST,
                          preferred_element_type=jnp.float32)
        for at in range(jobs):
            def taken(which):
                base = 6 * (held + at) + 3 * which
                return grouped[base : base + 1] + grouped[base + 1 : base + 2] + grouped[base + 2 : base + 3]
            mean = taken(0) / entries
            variance = taken(1) / entries - mean * mean
            scale_ref[at, 0:1] = mean
            scale_ref[at, 1:2] = lax.rsqrt(variance + EPS) * gain_ref[...]

    def write(sources):
        mean = scale_ref[frame, 0:1]
        scale = scale_ref[frame, 1:2]
        bias = bias_ref[...]
        mine = place_ref[1]
        for flip in range(parts):
            values = sources[flip][0:part_width].astype(jnp.float32)
            value = 0.5 * ((values - mean) * scale + bias)
            out_ref[0, mine ^ flip, 0] = (value + value * jnp.tanh(value)).astype(jnp.bfloat16)

    if early_refs:
        @pl.when(row == 0)
        def _():
            write(data_refs)

        @pl.when(row > 0)
        def _():
            write(early_refs)
    else:
        write(data_refs)


def norm_frames(messages, gain, bias, place, first, jobs, shape, held=0, lead=0, tail=16,
                early=(), base=None):
    frames, parts, steps, part_width, co = shape
    part_rows = rounded_up(part_width)
    group = co // GROUPS
    plan = dict(parts=parts, jobs=jobs, entries=float(parts * steps * part_width * parts * group),
                held=held, early=bool(early))
    ahead = lead // part_rows
    if early:
        at = lambda f, i, *_: (f, 0)
    else:
        at = lambda f, i, *_: (ahead + f * steps + i, 0)
    closing = messages[0].shape[0] // tail - 1
    in_specs = (
        [pl.BlockSpec((part_rows, co), lambda f, i, *_: (f * (steps - 1) + jnp.maximum(i - 1, 0), 0))
         for _ in early]
        + [pl.BlockSpec((part_rows, co), at) for _ in messages]
        + [pl.BlockSpec((tail, co), lambda f, i, *_: (closing, 0)) for _ in messages]
        + [pl.BlockSpec((1, co), lambda f, i, *_: (0, 0))] * 2
    )
    operands = [place, *early, *messages, *messages, gain, bias]
    aliases = {}
    if base is not None:
        in_specs.append(pl.BlockSpec(memory_space=pl.ANY))
        aliases = {len(operands): 0}
        operands.append(base)
    return pl.pallas_call(
        functools.partial(norm_kernel, plan),
        out_shape=jax.ShapeDtypeStruct(shape, jnp.bfloat16),
        grid_spec=pltpu.PrefetchScalarGridSpec(
            num_scalar_prefetch=1,
            grid=(jobs, steps),
            in_specs=in_specs,
            out_specs=pl.BlockSpec(
                (1, parts, 1, part_width, co), lambda f, i, *_: (first + f, 0, i, 0, 0)),
            scratch_shapes=[pltpu.VMEM((jobs, 8, co), jnp.float32)],
        ),
        input_output_aliases=aliases,
        cost_estimate=pl.CostEstimate(
            flops=8 * jobs * parts * steps * part_width * co,
            bytes_accessed=4 * jobs * parts * steps * part_width * co,
            transcendentals=jobs * parts * steps * part_width * co,
        ),
        compiler_params=pltpu.CompilerParams(vmem_limit_bytes=VMEM_BYTES),
    )(*operands)


def on_device(frames, clip_ids, conv_weight, norm_gain, norm_bias):
    count, band, width, ci = frames.shape
    co = conv_weight.shape[4]
    parts = lax.axis_size("rows")
    place = jnp.stack([lax.axis_index("tm") * count, lax.axis_index("rows")]).astype(jnp.int32)
    weight = conv_weight.reshape(3, 9 * ci, co)
    gain, bias = norm_gain.reshape(1, co), norm_bias.reshape(1, co)
    steps = band // 2
    shape = (count, parts, steps, width // 2 // parts, co)
    part_rows = rounded_up(shape[3])

    def named(name, function, *args, **keywords):
        with jax.named_scope(name):
            return function(*args, **keywords)

    halo = named("halo", passed_along, frames[:, -1:], "rows", 1)
    run = functools.partial(conv_frames, frames, halo, weight, clip_ids, place)
    far = [flip for flip in range(parts - 1, 0, -1) if 2 * flip >= parts]
    near = [flip for flip in range(parts - 1, 0, -1) if 2 * flip < parts]

    later = [(2, [(0, 0), (1, 1), (2, 2)], None), (3, [(1, 0), (2, 1), (3, 2)], None)]
    *a_sent, a_sums = named("conv_a", run, 0, 4, later, row=1, steps=steps - 1, parts=parts, sums_out=True)
    a_got = {flip: named(f"a{flip}", exchanged, a_sent[flip], "rows", flip) for flip in far}

    run = functools.partial(conv_frames, frames, after(halo, a_sums), weight, clip_ids, place)
    onward = named("conv_hist", run, 2, 2, [(4, [(0, 0), (1, 1)], None), (5, [(1, 0)], None)])
    first_add = named("hist0", passed_along, onward[0], "tm", 1)
    *top, top_sums = named("conv_top", run, 0, 4, later, row=0, steps=1, parts=parts, sums_out=True)
    second_add = named("hist1", passed_along, onward[1], "tm", 1)

    b_sent = named("conv_b", run, 0, 1, [(0, [(0, 2)], 0)], addends=(after(first_add, *[a_got[f] for f in far]),), parts=parts, leads=top,
                   sums=(a_sums, top_sums), tail=32)
    b_got = {flip: named(f"b{flip}", exchanged, b_sent[flip], "rows", flip) for flip in far}
    c_sent = named("conv_c", run, 0, 2, [(1, [(0, 1), (1, 2)], 0)], addends=(after(second_add, *[b_got[f] for f in far]),), parts=parts, tail=16)
    for flip in near:
        a_got[flip] = named(f"a{flip}", exchanged, a_sent[flip], "rows", flip)
        b_got[flip] = named(f"b{flip}", exchanged, b_sent[flip], "rows", flip)
    c_got = {flip: named(f"c{flip}", exchanged, c_sent[flip], "rows", flip) for flip in far + near}

    def whole(sent, got):
        return [sent[0]] + [got[flip] for flip in range(1, parts)]

    a_all, b_all, c_all = whole(a_sent, a_got), whole(b_sent, b_got), whole(c_sent, c_got)
    lead = 2 * part_rows
    out = named("norm_a", norm_frames, b_all, gain, bias, place, 2, 2, shape, tail=32, early=a_all)
    out = named("norm_b", norm_frames, b_all, gain, bias, place, 0, 1, shape, held=2, lead=lead, tail=32, base=out)
    out = named("norm_c", norm_frames, c_all, gain, bias, place, 1, 1, shape, tail=16, base=out)
    return out.reshape(count, parts * steps, shape[3], co)


def solution(mesh):
    in_specs = (P("tm", "rows", None, None), P(), P(), P(), P())
    out_specs = P("tm", None, "rows", None)
    return jax.shard_map(
        on_device, mesh=mesh, in_specs=in_specs, out_specs=out_specs, check_vma=False
    )
```

```python
import functools

import jax
import jax.numpy as jnp
from jax import lax
from jax.experimental import pallas as pl
from jax.experimental.pallas import tpu as pltpu
from jax.sharding import PartitionSpec as P

GROUPS = 32
EPS = 1e-05
VMEM_BYTES = 56 * 1024 * 1024


def passed_along(array, axis, by):
    length = lax.axis_size(axis)
    pairs = [(i, i + by) for i in range(length) if 0 <= i + by < length]
    return lax.ppermute(array, axis, pairs)


def exchanged(array, axis, flip):
    length = lax.axis_size(axis)
    return lax.ppermute(array, axis, [(i, i ^ flip) for i in range(length)])


def after(array, *earlier):
    return lax.optimization_barrier((array, *earlier))[0]


def rounded_up(rows):
    return -(-rows // 16) * 16


def split_columns(row_ref, slab_ref):
    width, ci = row_ref.shape
    half = width // 2
    slab_ref[:, ci : 2 * ci] = row_ref[pl.ds(0, half, stride=2), :]
    slab_ref[:, 2 * ci :] = row_ref[pl.ds(1, half, stride=2), :]
    slab_ref[16:, 0:ci] = row_ref[pl.ds(31, half - 16, stride=2), :]
    head = row_ref[pl.ds(1, 16, stride=2), :].astype(jnp.float32)
    zero = jnp.zeros((1, ci), jnp.float32)
    slab_ref[0:16, 0:ci] = jnp.concatenate([zero, head[:15]], axis=0).astype(jnp.bfloat16)


def split_three(total):
    high = total.astype(jnp.bfloat16).astype(jnp.float32)
    rest = total - high
    middle = rest.astype(jnp.bfloat16).astype(jnp.float32)
    return [high, middle, rest - middle]


def conv_kernel(plan, clip_ref, place_ref, x_ref, above_ref, w_ref, *refs):
    jobs, parts, part_rows, part_width = (
        plan["jobs"], plan["parts"], plan["part_rows"], plan["part_width"])
    lead, tail, steps = plan["lead"], plan["tail"], plan["steps"]

    def take(number):
        nonlocal refs
        some, refs = refs[:number], refs[number:]
        return some

    add_refs = take(plan["addends"])
    lead_refs = take(parts if lead else 0)
    sums_refs = take(plan["sums_in"])
    out_refs = take(parts if parts else len(jobs))
    sums_out = take(1 if plan["sums_out"] else 0)
    sources = x_ref.shape[0]
    slab_refs, refs = refs[:sources], refs[sources:]
    acc_refs, part_ref, stat_ref = refs[: len(jobs)], refs[-2], refs[-1]
    step = pl.program_id(0)
    half = acc_refs[0].shape[0]
    above = lax.rem(step + 1, 2)
    below = lax.rem(step, 2)
    start = place_ref[0]
    last = clip_ref.shape[0] - 1

    @pl.when(step == 0)
    def _():
        for source in range(sources):
            split_columns(above_ref.at[source, 0], slab_refs[source].at[1])
        stat_ref[...] = jnp.zeros_like(stat_ref)
        for flip in range(parts if lead else 0):
            out_refs[flip][0:lead] = lead_refs[flip][...]

    def product(source, tap):
        slab_ref = slab_refs[source]
        rows = jnp.concatenate([slab_ref[above], slab_ref[2], slab_ref[below]], axis=1)
        return jnp.dot(rows, w_ref[tap], preferred_element_type=jnp.float32)

    empty = [True] * len(jobs)
    for at, (target, taps, addend) in enumerate(jobs):
        if addend is not None:
            acc_refs[at][...] = add_refs[addend][0].astype(jnp.float32)
            empty[at] = False
    for source in range(sources):
        split_columns(x_ref.at[source, 0], slab_refs[source].at[2])
        split_columns(x_ref.at[source, 1], slab_refs[source].at[below])
        frame = plan["first"] + source
        for at, (target, taps, _) in enumerate(jobs):
            for tap in [tap for other, tap in taps if other == source]:
                value = product(source, tap)
                if frame != target:
                    same = clip_ref[start + frame] == clip_ref[jnp.minimum(start + target, last)]
                    value = value * same.astype(jnp.float32)
                acc_refs[at][...] = value if empty[at] else acc_refs[at][...] + value
                empty[at] = False

    for at in range(len(jobs)):
        acc_ref = acc_refs[at]
        if not parts:
            out_refs[at][0] = acc_ref[...].astype(jnp.bfloat16)
            continue
        rounded = acc_ref[...].astype(jnp.bfloat16).astype(jnp.float32)
        tiles = rounded.reshape(half // 8, 8, rounded.shape[1])
        stat_ref[2 * at] += jnp.sum(tiles, axis=0)
        stat_ref[2 * at + 1] += jnp.sum(tiles * tiles, axis=0)
        for part in range(parts):
            piece = rounded[part * part_width : (part + 1) * part_width]
            part_ref[at, part, 0:part_width] = piece.astype(jnp.bfloat16)
        mine = place_ref[1]
        for flip in range(parts):
            offset = pl.multiple_of(lead + (at * steps + step) * part_rows, 16)
            out_refs[flip][pl.ds(offset, part_rows)] = part_ref[at, mine ^ flip]

    if sums_out or tail:
        @pl.when(step == steps - 1)
        def _():
            if sums_out:
                sums_out[0][...] = stat_ref[...]
            if tail:
                sums = [sum(ref[at] for ref in sums_refs)
                        for at in range(sums_refs[0].shape[0] if sums_refs else 0)]
                sums += [stat_ref[at] for at in range(2 * len(jobs))]
                rows = []
                for total in sums:
                    rows += split_three(jnp.sum(total, axis=0, keepdims=True))
                blank = jnp.zeros((tail - len(rows), rows[0].shape[1]), jnp.float32)
                closing = jnp.concatenate(rows + [blank], axis=0).astype(jnp.bfloat16)
                body = lead + len(jobs) * steps * part_rows
                for flip in range(parts):
                    out_refs[flip][body : body + tail] = closing


def conv_frames(frames, halo, weight, clip_ids, place, first, sources, jobs, row=0, steps=None,
                addends=(), parts=0, leads=(), sums=(), sums_out=False, tail=0,
                weigh=1):
    _, band, width, ci = frames.shape
    co = weight.shape[2]
    half = width // 2
    steps = steps or band // 2
    part_width = half // parts if parts else half
    part_rows = rounded_up(part_width)
    lead = leads[0].shape[0] if leads else 0
    plan = dict(jobs=jobs, addends=len(addends), parts=parts, part_rows=part_rows, lead=lead,
                part_width=part_width, first=first, steps=steps, tail=tail,
                sums_in=len(sums), sums_out=sums_out)
    block = first // sources
    above = (frames, 2 * row - 1) if row else (halo, 0)
    in_specs = [
        pl.BlockSpec((sources, 2, width, ci), lambda i, *_: (block, row + i, 0, 0)),
        pl.BlockSpec((sources, 1, width, ci), lambda i, *_: (block, above[1], 0, 0)),
        pl.BlockSpec(weight.shape, lambda i, *_: (0, 0, 0)),
    ]
    in_specs += [pl.BlockSpec((1, None, half, co), lambda i, *_: (0, i, 0, 0)) for _ in addends]
    in_specs += [pl.BlockSpec(a.shape, lambda i, *_: (0, 0)) for a in leads]
    in_specs += [pl.BlockSpec(a.shape, lambda i, *_: (0, 0, 0)) for a in sums]
    if parts:
        message = (lead + len(jobs) * steps * part_rows + tail, co)
        out_shape = [jax.ShapeDtypeStruct(message, jnp.bfloat16) for _ in range(parts)]
        out_specs = [pl.BlockSpec(message, lambda i, *_: (0, 0)) for _ in range(parts)]
    else:
        out_shape = [jax.ShapeDtypeStruct((1, steps, half, co), jnp.bfloat16) for _ in jobs]
        out_specs = [pl.BlockSpec((1, None, half, co), lambda i, *_: (0, i, 0, 0)) for _ in jobs]
    if sums_out:
        shape = (2 * len(jobs), 8, co)
        out_shape.append(jax.ShapeDtypeStruct(shape, jnp.float32))
        out_specs.append(pl.BlockSpec(shape, lambda i, *_: (0, 0, 0)))
    products = sum(len(taps) for _, taps, _ in jobs)
    return pl.pallas_call(
        functools.partial(conv_kernel, plan),
        out_shape=out_shape,
        grid_spec=pltpu.PrefetchScalarGridSpec(
            num_scalar_prefetch=2,
            grid=(steps,),
            in_specs=in_specs,
            out_specs=out_specs,
            scratch_shapes=[
                *[pltpu.VMEM((3, half, 3 * ci), jnp.bfloat16) for _ in range(sources)],
                *[pltpu.VMEM((half, co), jnp.float32) for _ in jobs],
                pltpu.VMEM((len(jobs), max(parts, 1), part_rows, co), jnp.bfloat16),
                pltpu.VMEM((2 * len(jobs), 8, co), jnp.float32),
            ],
        ),
        cost_estimate=pl.CostEstimate(
            flops=2 * weigh * products * steps * half * 9 * ci * co,
            bytes_accessed=weigh * (4 * sources * steps * width * ci + 2 * len(jobs) * steps * half * co),
            transcendentals=0,
        ),
        compiler_params=pltpu.CompilerParams(vmem_limit_bytes=VMEM_BYTES),
    )(clip_ids, place, frames, above[0], weight, *addends, *leads, *sums)


def norm_kernel(plan, place_ref, *refs):
    parts, jobs, entries, held = plan["parts"], plan["jobs"], plan["entries"], plan["held"]
    early_refs = refs[:parts] if plan["early"] else ()
    refs = refs[len(early_refs):]
    data_refs, tail_refs = refs[:parts], refs[parts : 2 * parts]
    gain_ref, bias_ref = refs[2 * parts : 2 * parts + 2]
    out_ref, scale_ref = refs[-2:]
    frame, row = pl.program_id(0), pl.program_id(1)
    part_width, co = out_ref.shape[-2:]

    @pl.when((frame == 0) & (row == 0))
    def _():
        total = tail_refs[0][...].astype(jnp.float32)
        for flip in range(1, parts):
            total = total + tail_refs[flip][...].astype(jnp.float32)
        size = co // GROUPS
        same = (lax.broadcasted_iota(jnp.int32, (co, co), 0) // size
                == lax.broadcasted_iota(jnp.int32, (co, co), 1) // size).astype(jnp.float32)
        grouped = jnp.dot(total, same, precision=lax.Precision.HIGHEST,
                          preferred_element_type=jnp.float32)
        for at in range(jobs):
            def taken(which):
                base = 6 * (held + at) + 3 * which
                return grouped[base : base + 1] + grouped[base + 1 : base + 2] + grouped[base + 2 : base + 3]
            mean = taken(0) / entries
            variance = taken(1) / entries - mean * mean
            scale_ref[at, 0:1] = mean
            scale_ref[at, 1:2] = lax.rsqrt(variance + EPS) * gain_ref[...]

    def write(sources):
        mean = scale_ref[frame, 0:1]
        scale = scale_ref[frame, 1:2]
        bias = bias_ref[...]
        mine = place_ref[1]
        for flip in range(parts):
            values = sources[flip][0:part_width].astype(jnp.float32)
            value = 0.5 * ((values - mean) * scale + bias)
            out_ref[0, mine ^ flip, 0] = (value + value * jnp.tanh(value)).astype(jnp.bfloat16)

    if early_refs:
        @pl.when(row == 0)
        def _():
            write(data_refs)

        @pl.when(row > 0)
        def _():
            write(early_refs)
    else:
        write(data_refs)


def norm_frames(messages, gain, bias, place, first, jobs, shape, held=0, lead=0, tail=16,
                early=(), base=None):
    frames, parts, steps, part_width, co = shape
    part_rows = rounded_up(part_width)
    group = co // GROUPS
    plan = dict(parts=parts, jobs=jobs, entries=float(parts * steps * part_width * parts * group),
                held=held, early=bool(early))
    ahead = lead // part_rows
    if early:
        at = lambda f, i, *_: (f, 0)
    else:
        at = lambda f, i, *_: (ahead + f * steps + i, 0)
    closing = messages[0].shape[0] // tail - 1
    in_specs = (
        [pl.BlockSpec((part_rows, co), lambda f, i, *_: (f * (steps - 1) + jnp.maximum(i - 1, 0), 0))
         for _ in early]
        + [pl.BlockSpec((part_rows, co), at) for _ in messages]
        + [pl.BlockSpec((tail, co), lambda f, i, *_: (closing, 0)) for _ in messages]
        + [pl.BlockSpec((1, co), lambda f, i, *_: (0, 0))] * 2
    )
    operands = [place, *early, *messages, *messages, gain, bias]
    aliases = {}
    if base is not None:
        in_specs.append(pl.BlockSpec(memory_space=pl.ANY))
        aliases = {len(operands): 0}
        operands.append(base)
    return pl.pallas_call(
        functools.partial(norm_kernel, plan),
        out_shape=jax.ShapeDtypeStruct(shape, jnp.bfloat16),
        grid_spec=pltpu.PrefetchScalarGridSpec(
            num_scalar_prefetch=1,
            grid=(jobs, steps),
            in_specs=in_specs,
            out_specs=pl.BlockSpec(
                (1, parts, 1, part_width, co), lambda f, i, *_: (first + f, 0, i, 0, 0)),
            scratch_shapes=[pltpu.VMEM((jobs, 8, co), jnp.float32)],
        ),
        input_output_aliases=aliases,
        cost_estimate=pl.CostEstimate(
            flops=8 * jobs * parts * steps * part_width * co,
            bytes_accessed=4 * jobs * parts * steps * part_width * co,
            transcendentals=jobs * parts * steps * part_width * co,
        ),
        compiler_params=pltpu.CompilerParams(vmem_limit_bytes=VMEM_BYTES),
    )(*operands)


def on_device(frames, clip_ids, conv_weight, norm_gain, norm_bias):
    count, band, width, ci = frames.shape
    co = conv_weight.shape[4]
    parts = lax.axis_size("rows")
    place = jnp.stack([lax.axis_index("tm") * count, lax.axis_index("rows")]).astype(jnp.int32)
    weight = conv_weight.reshape(3, 9 * ci, co)
    gain, bias = norm_gain.reshape(1, co), norm_bias.reshape(1, co)
    steps = band // 2
    shape = (count, parts, steps, width // 2 // parts, co)
    part_rows = rounded_up(shape[3])

    def named(name, function, *args, **keywords):
        with jax.named_scope(name):
            return function(*args, **keywords)

    halo = named("halo", passed_along, frames[:, -1:], "rows", 1)
    run = functools.partial(conv_frames, frames, halo, weight, clip_ids, place)
    far = [flip for flip in range(parts - 1, 0, -1) if 2 * flip >= parts]
    near = [flip for flip in range(parts - 1, 0, -1) if 2 * flip < parts]

    later = [(2, [(0, 0), (1, 1), (2, 2)], None), (3, [(1, 0), (2, 1), (3, 2)], None)]
    *a_sent, a_sums = named("conv_a", run, 0, 4, later, row=1, steps=steps - 1, parts=parts, sums_out=True)
    a_got = {flip: named(f"a{flip}", exchanged, a_sent[flip], "rows", flip) for flip in far}

    run = functools.partial(conv_frames, frames, after(halo, a_sums), weight, clip_ids, place)
    onward = named("conv_hist", run, 2, 2, [(4, [(0, 0), (1, 1)], None), (5, [(1, 0)], None)], weigh=1)
    first_add = named("hist0", passed_along, onward[0], "tm", 1)
    *top, top_sums = named("conv_top", run, 0, 4, later, row=0, steps=1, parts=parts, sums_out=True, weigh=20)
    second_add = named("hist1", passed_along, after(onward[1], first_add), "tm", 1)

    b_sent = named("conv_b", run, 0, 1, [(0, [(0, 2)], 0)], addends=(first_add,), parts=parts, leads=top,
                   sums=(a_sums, top_sums), tail=32, weigh=20)
    b_got = {flip: named(f"b{flip}", exchanged, after(b_sent[flip], a_got[flip]), "rows", flip) for flip in far}
    c_sent = named("conv_c", run, 0, 2, [(1, [(0, 1), (1, 2)], 0)], addends=(second_add,), parts=parts, tail=16, weigh=20)
    c_got = {flip: named(f"c{flip}", exchanged, after(c_sent[flip], b_got[flip]), "rows", flip) for flip in far}
    for flip in near:
        a_got[flip] = named(f"a{flip}", exchanged, after(a_sent[flip], c_sent[0]), "rows", flip)
        b_got[flip] = named(f"b{flip}", exchanged, after(b_sent[flip], c_sent[0]), "rows", flip)
        c_got[flip] = named(f"c{flip}", exchanged, after(c_sent[flip], b_got[flip]), "rows", flip)

    def whole(sent, got):
        return [sent[0]] + [got[flip] for flip in range(1, parts)]

    a_all, b_all, c_all = whole(a_sent, a_got), whole(b_sent, b_got), whole(c_sent, c_got)
    lead = 2 * part_rows
    out = named("norm_a", norm_frames, b_all, gain, bias, place, 2, 2, shape, tail=32, early=a_all)
    out = named("norm_b", norm_frames, b_all, gain, bias, place, 0, 1, shape, held=2, lead=lead, tail=32, base=out)
    out = named("norm_c", norm_frames, c_all, gain, bias, place, 1, 1, shape, tail=16, base=out)
    return out.reshape(count, parts * steps, shape[3], co)


def solution(mesh):
    in_specs = (P("tm", "rows", None, None), P(), P(), P(), P())
    out_specs = P("tm", None, "rows", None)
    return jax.shard_map(
        on_device, mesh=mesh, in_specs=in_specs, out_specs=out_specs, check_vma=False
    )
```

```python
import functools

import jax
import jax.numpy as jnp
from jax import lax
from jax.experimental import pallas as pl
from jax.experimental.pallas import tpu as pltpu
from jax.sharding import PartitionSpec as P

GROUPS = 32
EPS = 1e-05
STAT_ROWS = 16
VMEM_BYTES = 60 * 1024 * 1024


def passed_along(array, axis, by):
    length = lax.axis_size(axis)
    pairs = [(i, i + by) for i in range(length) if 0 <= i + by < length]
    return lax.ppermute(array, axis, pairs)


def exchanged(array, axis, flip):
    length = lax.axis_size(axis)
    return lax.ppermute(array, axis, [(i, i ^ flip) for i in range(length)])


def after(array, *earlier):
    return lax.optimization_barrier((array, *earlier))[0]


def rounded_up(rows):
    return -(-rows // 16) * 16


def split_columns(row_ref, slab_ref):
    width, ci = row_ref.shape
    half = width // 2
    slab_ref[:, 0:ci] = row_ref[pl.ds(0, half, stride=2), :]
    slab_ref[:, ci:] = row_ref[pl.ds(1, half, stride=2), :]


def split_three(total):
    high = total.astype(jnp.bfloat16).astype(jnp.float32)
    rest = total - high
    middle = rest.astype(jnp.bfloat16).astype(jnp.float32)
    return [high, middle, rest - middle]


def conv_kernel(plan, clip_ref, place_ref, x_ref, above_ref, w_ref, *refs):
    jobs, parts, part_rows, part_width = (
        plan["jobs"], plan["parts"], plan["part_rows"], plan["part_width"])
    lead, steps, tap_first = plan["lead"], plan["steps"], plan["tap_first"]

    def take(number):
        nonlocal refs
        some, refs = refs[:number], refs[number:]
        return some

    add_refs = take(plan["addends"])
    sums_refs = take(plan["sums_in"])
    take(plan["kept"])
    out_refs = take(parts if parts else len(jobs))
    sums_out = take(1 if plan["sums_out"] else 0)
    sources, ci = x_ref.shape[0], x_ref.shape[3]
    slab_refs, main_refs, left_refs = take(sources), take(len(jobs)), take(len(jobs))
    part_ref, stat_ref = refs
    step = pl.program_id(0)
    half, co = main_refs[0].shape
    above = lax.rem(step + 1, 2)
    below = lax.rem(step, 2)
    start = place_ref[0]
    last = clip_ref.shape[0] - 1

    @pl.when(step == 0)
    def _():
        for source in range(sources):
            split_columns(above_ref.at[source, 0], slab_refs[source].at[1])
        for left_ref in left_refs:
            left_ref[0:8] = jnp.zeros((8, co), jnp.float32)
        stat_ref[...] = jnp.zeros_like(stat_ref)

    def products(source, tap):
        slab_ref, tap = slab_refs[source], tap - tap_first
        rows = [slab_ref[above], slab_ref[2], slab_ref[below]]
        main = jnp.dot(
            jnp.concatenate(rows, axis=1),
            jnp.concatenate([w_ref[tap, (3 * a + 1) * ci : (3 * a + 3) * ci] for a in range(3)], axis=0),
            preferred_element_type=jnp.float32)
        left = jnp.dot(
            jnp.concatenate([row[:, ci:] for row in rows], axis=1),
            jnp.concatenate([w_ref[tap, 3 * a * ci : (3 * a + 1) * ci] for a in range(3)], axis=0),
            preferred_element_type=jnp.float32)
        return main, left

    empty = [True] * len(jobs)
    for source in range(sources):
        split_columns(x_ref.at[source, 0], slab_refs[source].at[2])
        split_columns(x_ref.at[source, 1], slab_refs[source].at[below])
        frame = plan["first"] + source
        for at, (target, taps, addend) in enumerate(jobs):
            for tap in [tap for other, tap in taps if other == source]:
                main, left = products(source, tap)
                if frame != target:
                    same = clip_ref[start + frame] == clip_ref[jnp.minimum(start + target, last)]
                    same = same.astype(jnp.float32)
                    main, left = main * same, left * same
                if empty[at]:
                    if addend is not None:
                        main = main + add_refs[addend][0].astype(jnp.float32)
                    main_refs[at][...] = main
                    left_refs[at][8:] = left
                else:
                    main_refs[at][...] += main
                    left_refs[at][8:] += left
                empty[at] = False

    for at in range(len(jobs)):
        total = main_refs[at][...] + left_refs[at][7 : 7 + half]
        if not parts:
            out_refs[at][0] = total.astype(jnp.bfloat16)
            continue
        rounded = total.astype(jnp.bfloat16).astype(jnp.float32)
        tiles = rounded.reshape(half // 8, 8, co)
        stat_ref[2 * at] += jnp.sum(tiles, axis=0)
        stat_ref[2 * at + 1] += jnp.sum(tiles * tiles, axis=0)
        for part in range(parts):
            piece = rounded[part * part_width : (part + 1) * part_width]
            part_ref[at, part, 0:part_width] = piece.astype(jnp.bfloat16)
        mine = place_ref[1]
        for flip in range(parts):
            offset = pl.multiple_of(lead + (at * steps + step) * part_rows, 16)
            out_refs[flip][pl.ds(offset, part_rows)] = part_ref[at, mine ^ flip]

    if parts:
        @pl.when(step == steps - 1)
        def _():
            if sums_out:
                sums_out[0][...] = stat_ref[...]
                return
            rows = []
            for at in range(2 * len(jobs)):
                total = stat_ref[at]
                for ref in sums_refs:
                    total = total + ref[at]
                rows += split_three(jnp.sum(total, axis=0, keepdims=True))
            blank = jnp.zeros((STAT_ROWS - len(rows), co), jnp.float32)
            closing = jnp.concatenate(rows + [blank], axis=0).astype(jnp.bfloat16)
            for flip in range(parts):
                out_refs[flip][0:STAT_ROWS] = closing


def conv_frames(frames, halo, weight, clip_ids, place, first, sources, jobs, row=0, steps=None,
                addends=(), parts=0, sums=(), sums_out=False, lead=0, kept=(), weigh=1):
    _, band, width, ci = frames.shape
    co = weight.shape[2]
    half = width // 2
    steps = steps or band // 2
    part_width = half // parts if parts else half
    part_rows = rounded_up(part_width)
    taps = sorted({tap for _, some, _ in jobs for _, tap in some})
    tap_first, tap_count = 0, 3
    if len(taps) == 1 or taps == [0, 1]:
        tap_first, tap_count = taps[0], len(taps)
    plan = dict(jobs=jobs, addends=len(addends), parts=parts, part_rows=part_rows, lead=lead,
                part_width=part_width, first=first, steps=steps, kept=len(kept),
                sums_in=len(sums), sums_out=sums_out, tap_first=tap_first)
    block = first // sources
    above = (frames, 2 * row - 1) if row else (halo, 0)
    in_specs = [
        pl.BlockSpec((sources, 2, width, ci), lambda i, *_: (block, row + i, 0, 0)),
        pl.BlockSpec((sources, 1, width, ci), lambda i, *_: (block, above[1], 0, 0)),
        pl.BlockSpec((tap_count, 9 * ci, co), lambda i, *_: (tap_first // tap_count, 0, 0)),
    ]
    in_specs += [pl.BlockSpec((1, None, half, co), lambda i, *_: (0, i, 0, 0)) for _ in addends]
    in_specs += [pl.BlockSpec(a.shape, lambda i, *_: (0, 0, 0)) for a in sums]
    in_specs += [pl.BlockSpec(memory_space=pl.ANY) for _ in kept]
    operands = [clip_ids, place, frames, above[0], weight, *addends, *sums, *kept]
    aliases = {len(operands) - len(kept) + at: at for at in range(len(kept))}
    if parts:
        rows = lead + len(jobs) * steps * part_rows
        shape = kept[0].shape if kept else (rows, co)
        out_shape = [jax.ShapeDtypeStruct(shape, jnp.bfloat16) for _ in range(parts)]
        out_specs = [pl.BlockSpec((rows, co), lambda i, *_: (0, 0)) for _ in range(parts)]
    else:
        out_shape = [jax.ShapeDtypeStruct((1, steps, half, co), jnp.bfloat16) for _ in jobs]
        out_specs = [pl.BlockSpec((1, None, half, co), lambda i, *_: (0, i, 0, 0)) for _ in jobs]
    if sums_out:
        shape = (2 * len(jobs), 8, co)
        out_shape.append(jax.ShapeDtypeStruct(shape, jnp.float32))
        out_specs.append(pl.BlockSpec(shape, lambda i, *_: (0, 0, 0)))
    products = sum(len(some) for _, some, _ in jobs)
    return pl.pallas_call(
        functools.partial(conv_kernel, plan),
        out_shape=out_shape,
        grid_spec=pltpu.PrefetchScalarGridSpec(
            num_scalar_prefetch=2,
            grid=(steps,),
            in_specs=in_specs,
            out_specs=out_specs,
            scratch_shapes=[
                *[pltpu.VMEM((3, half, 2 * ci), jnp.bfloat16) for _ in range(sources)],
                *[pltpu.VMEM((half, co), jnp.float32) for _ in jobs],
                *[pltpu.VMEM((8 + half, co), jnp.float32) for _ in jobs],
                pltpu.VMEM((len(jobs), max(parts, 1), part_rows, co), jnp.bfloat16),
                pltpu.VMEM((2 * len(jobs), 8, co), jnp.float32),
            ],
        ),
        input_output_aliases=aliases,
        cost_estimate=pl.CostEstimate(
            flops=2 * weigh * products * steps * half * 9 * ci * co,
            bytes_accessed=weigh * (4 * sources * steps * width * ci + 2 * len(jobs) * steps * half * co),
            transcendentals=0,
        ),
        compiler_params=pltpu.CompilerParams(vmem_limit_bytes=VMEM_BYTES),
    )(*operands)


def norm_kernel(plan, place_ref, *refs):
    parts, jobs, steps, rows = plan["parts"], plan["jobs"], plan["steps"], plan["rows"]
    lead, part_rows = plan["lead"], plan["part_rows"]
    data_refs, (gain_ref, bias_ref) = refs[:parts], refs[parts : parts + 2]
    out_ref, scale_ref = refs[-2:]
    frame, step = pl.program_id(0), pl.program_id(1)
    part_width, co = out_ref.shape[-2:]

    @pl.when((frame == 0) & (step == 0))
    def _():
        total = data_refs[0][0:STAT_ROWS].astype(jnp.float32)
        for flip in range(1, parts):
            total = total + data_refs[flip][0:STAT_ROWS].astype(jnp.float32)
        size = co // GROUPS
        same = (lax.broadcasted_iota(jnp.int32, (co, co), 0) // size
                == lax.broadcasted_iota(jnp.int32, (co, co), 1) // size).astype(jnp.float32)
        grouped = jnp.dot(total, same, precision=lax.Precision.HIGHEST,
                          preferred_element_type=jnp.float32)
        for at in range(jobs):
            def taken(which):
                base = 6 * at + 3 * which
                return grouped[base : base + 1] + grouped[base + 1 : base + 2] + grouped[base + 2 : base + 3]
            mean = taken(0) / plan["entries"]
            variance = taken(1) / plan["entries"] - mean * mean
            scale_ref[at, 0:1] = mean
            scale_ref[at, 1:2] = lax.rsqrt(variance + EPS) * gain_ref[...]

    mean = scale_ref[frame, 0:1]
    scale = scale_ref[frame, 1:2]
    bias = bias_ref[...]
    mine = place_ref[1]
    for at in range(rows):
        row = step * rows + at
        if plan["top_first"]:
            place = jnp.where(row == 0, frame, jobs + frame * (steps - 1) + row - 1)
        else:
            place = frame * steps + row
        offset = pl.multiple_of(lead + place * part_rows, 16)
        for flip in range(parts):
            values = data_refs[flip][pl.ds(offset, part_rows)][0:part_width].astype(jnp.float32)
            value = 0.5 * ((values - mean) * scale + bias)
            out_ref[0, mine ^ flip, at] = (value + value * jnp.tanh(value)).astype(jnp.bfloat16)


def norm_frames(messages, gain, bias, place, first, jobs, shape, top_first=False, base=None):
    frames, parts, steps, part_width, co = shape
    rows = 2 if steps % 2 == 0 else 1
    plan = dict(parts=parts, jobs=jobs, steps=steps, rows=rows, lead=STAT_ROWS,
                part_rows=rounded_up(part_width), top_first=top_first,
                entries=float(parts * steps * part_width * parts * (co // GROUPS)))
    in_specs = (
        [pl.BlockSpec(message.shape, lambda f, i, *_: (0, 0)) for message in messages]
        + [pl.BlockSpec((1, co), lambda f, i, *_: (0, 0))] * 2
    )
    operands = [place, *messages, gain, bias]
    aliases = {}
    if base is not None:
        in_specs.append(pl.BlockSpec(memory_space=pl.ANY))
        aliases = {len(operands): 0}
        operands.append(base)
    return pl.pallas_call(
        functools.partial(norm_kernel, plan),
        out_shape=jax.ShapeDtypeStruct(shape, jnp.bfloat16),
        grid_spec=pltpu.PrefetchScalarGridSpec(
            num_scalar_prefetch=1,
            grid=(jobs, steps // rows),
            in_specs=in_specs,
            out_specs=pl.BlockSpec(
                (1, parts, rows, part_width, co), lambda f, i, *_: (first + f, 0, i, 0, 0)),
            scratch_shapes=[pltpu.VMEM((jobs, 8, co), jnp.float32)],
        ),
        input_output_aliases=aliases,
        cost_estimate=pl.CostEstimate(
            flops=8 * jobs * parts * steps * part_width * co,
            bytes_accessed=4 * jobs * parts * steps * part_width * co,
            transcendentals=jobs * parts * steps * part_width * co,
        ),
        compiler_params=pltpu.CompilerParams(vmem_limit_bytes=VMEM_BYTES),
    )(*operands)


def on_device(frames, clip_ids, conv_weight, norm_gain, norm_bias):
    count, band, width, ci = frames.shape
    co = conv_weight.shape[4]
    parts = lax.axis_size("rows")
    place = jnp.stack([lax.axis_index("tm") * count, lax.axis_index("rows")]).astype(jnp.int32)
    weight = conv_weight.reshape(3, 9 * ci, co)
    gain, bias = norm_gain.reshape(1, co), norm_bias.reshape(1, co)
    steps = band // 2
    shape = (count, parts, steps, width // 2 // parts, co)
    part_rows = rounded_up(shape[3])
    top_rows = STAT_ROWS + 2 * part_rows

    def named(name, function, *args, **keywords):
        with jax.named_scope(name):
            return function(*args, **keywords)

    halo = named("halo", passed_along, frames[:, -1:], "rows", 1)
    far = [flip for flip in range(parts - 1, 0, -1) if 2 * flip >= parts]
    near = [flip for flip in range(parts - 1, 0, -1) if 2 * flip < parts]

    later = [(2, [(0, 0), (1, 1), (2, 2)], None), (3, [(1, 0), (2, 1), (3, 2)], None)]
    run = functools.partial(conv_frames, frames, halo, weight, clip_ids, place)
    *a_sent, a_sums = named("conv_a", run, 0, 4, later, row=1, steps=steps - 1, parts=parts,
                            sums_out=True, lead=top_rows, weigh=1)
    a_sent = named("conv_top", run, 0, 4, later, steps=1, parts=parts, sums=(a_sums,),
                   lead=STAT_ROWS, kept=a_sent, weigh=1)
    run = functools.partial(conv_frames, frames, after(halo, a_sent[0]), weight, clip_ids, place)
    onward, = named("conv_hist0", run, 2, 2, [(4, [(0, 0), (1, 1)], None)])
    first_add = named("hist0", passed_along, onward, "tm", 1)
    run = functools.partial(conv_frames, frames, after(halo, onward), weight, clip_ids, place)
    onward, = named("conv_hist1", run, 3, 1, [(5, [(0, 0)], None)], weigh=40)
    second_add = named("hist1", passed_along, after(onward, first_add), "tm", 1)
    b_sent = named("conv_b", run, 0, 1, [(0, [(0, 2)], 0)], addends=(after(first_add, onward),), parts=parts,
                   lead=STAT_ROWS, weigh=20)
    c_sent = named("conv_c", run, 0, 2, [(1, [(0, 1), (1, 2)], 0)], addends=(second_add,), parts=parts,
                   lead=STAT_ROWS, weigh=20)

    a_got, b_got, c_got = {}, {}, {}
    chain = []
    for name, sent, got in (("a", a_sent, a_got), ("b", b_sent, b_got), ("c", c_sent, c_got)):
        for flip in far:
            earlier = chain[-4:][:1] if len(chain) >= 4 else []
            got[flip] = named(f"{name}{flip}", exchanged, after(sent[flip], *earlier), "rows", flip)
            chain.append(got[flip])
    for name, sent, got, earlier in (("a", a_sent, a_got, a_sums), ("b", b_sent, b_got, c_sent[0]), ("c", c_sent, c_got, c_sent[0])):
        for flip in near:
            got[flip] = named(f"{name}{flip}", exchanged, after(sent[flip], earlier), "rows", flip)

    def whole(sent, got):
        return [sent[0]] + [got[flip] for flip in range(1, parts)]

    a_all, b_all, c_all = whole(a_sent, a_got), whole(b_sent, b_got), whole(c_sent, c_got)
    out = named("norm_a", norm_frames, a_all, gain, bias, place, 2, 2, shape, top_first=True)
    out = named("norm_b", norm_frames, b_all, gain, bias, place, 0, 1, shape, base=out)
    out = named("norm_c", norm_frames, c_all, gain, bias, place, 1, 1, shape, base=out)
    return out.reshape(count, parts * steps, shape[3], co)


def solution(mesh):
    in_specs = (P("tm", "rows", None, None), P(), P(), P(), P())
    out_specs = P("tm", None, "rows", None)
    return jax.shard_map(
        on_device, mesh=mesh, in_specs=in_specs, out_specs=out_specs, check_vma=False
    )
```

```python
import functools

import jax
import jax.numpy as jnp
from jax import lax
from jax.experimental import pallas as pl
from jax.experimental.pallas import tpu as pltpu
from jax.sharding import PartitionSpec as P

GROUPS = 32
EPS = 1e-05
STAT_ROWS = 16


def passed_along(array, axis, by):
    length = lax.axis_size(axis)
    pairs = [(i, i + by) for i in range(length) if 0 <= i + by < length]
    return lax.ppermute(array, axis, pairs)


def exchanged(array, axis, flip):
    length = lax.axis_size(axis)
    return lax.ppermute(array, axis, [(i, i ^ flip) for i in range(length)])


def after(array, *earlier):
    return lax.optimization_barrier((array, *earlier))[0]


def rounded_up(rows):
    return -(-rows // 16) * 16


def split_columns(row_ref, slab_ref):
    width, ci = row_ref.shape
    half = width // 2
    slab_ref[:, 0:ci] = row_ref[pl.ds(0, half, stride=2), :]
    slab_ref[:, ci:] = row_ref[pl.ds(1, half, stride=2), :]


def split_three(total):
    high = total.astype(jnp.bfloat16).astype(jnp.float32)
    rest = total - high
    middle = rest.astype(jnp.bfloat16).astype(jnp.float32)
    return [high, middle, rest - middle]


def conv_kernel(plan, clip_ref, x_ref, above_ref, w_ref, *refs):
    jobs, parts, part_rows, part_width = (
        plan["jobs"], plan["parts"], plan["part_rows"], plan["part_width"])
    lead, steps, tap_first = plan["lead"], plan["steps"], plan["tap_first"]

    def take(number):
        nonlocal refs
        some, refs = refs[:number], refs[number:]
        return some

    add_refs = take(plan["addends"])
    sums_refs = take(plan["sums_in"])
    take(plan["kept"])
    out_refs = take(parts if parts else len(jobs))
    sums_out = take(1 if plan["sums_out"] else 0)
    sources, ci = x_ref.shape[0], x_ref.shape[3]
    slab_refs, main_refs, left_refs = take(sources), take(len(jobs)), take(len(jobs))
    part_ref, stat_ref, closing_ref, part_sem, tail_sem = refs
    step = pl.program_id(0)
    half, co = main_refs[0].shape
    above = lax.rem(step + 1, 2)
    below = lax.rem(step, 2)
    start = lax.axis_index("tm") * plan["count"]
    last = clip_ref.shape[0] - 1

    @pl.when(step == 0)
    def _():
        for source in range(sources):
            split_columns(above_ref.at[source, 0], slab_refs[source].at[1])
        for left_ref in left_refs:
            left_ref[0:8] = jnp.zeros((8, co), jnp.float32)
        stat_ref[...] = jnp.zeros_like(stat_ref)

    def piece_copies(at, slot, step):
        mine = lax.axis_index("rows")
        offset = pl.multiple_of(lead + (at * steps + step) * part_rows, 16)
        return [
            pltpu.make_async_copy(part_ref.at[slot, at, mine ^ flip],
                                  out.at[pl.ds(offset, part_rows)], part_sem.at[slot, at, flip])
            for flip, out in enumerate(out_refs)
        ]

    def products(source, tap):
        slab_ref, tap = slab_refs[source], tap - tap_first
        rows = [slab_ref[above], slab_ref[2], slab_ref[below]]
        main = jnp.dot(
            jnp.concatenate(rows, axis=1),
            jnp.concatenate([w_ref[tap, (3 * a + 1) * ci : (3 * a + 3) * ci] for a in range(3)], axis=0),
            preferred_element_type=jnp.float32)
        left = jnp.dot(
            jnp.concatenate([row[:, ci:] for row in rows], axis=1),
            jnp.concatenate([w_ref[tap, 3 * a * ci : (3 * a + 1) * ci] for a in range(3)], axis=0),
            preferred_element_type=jnp.float32)
        return main, left

    empty = [True] * len(jobs)
    for source in range(sources):
        split_columns(x_ref.at[source, 0], slab_refs[source].at[2])
        split_columns(x_ref.at[source, 1], slab_refs[source].at[below])
        frame = plan["first"] + source
        for at, (target, taps, addend) in enumerate(jobs):
            for tap in [tap for other, tap in taps if other == source]:
                main, left = products(source, tap)
                if frame != target:
                    same = clip_ref[start + frame] == clip_ref[jnp.minimum(start + target, last)]
                    same = same.astype(jnp.float32)
                    main, left = main * same, left * same
                if empty[at]:
                    if addend is not None:
                        main = main + add_refs[addend][0].astype(jnp.float32)
                    main_refs[at][...] = main
                    left_refs[at][8:] = left
                else:
                    main_refs[at][...] += main
                    left_refs[at][8:] += left
                empty[at] = False

    for at in range(len(jobs)):
        total = main_refs[at][...] + left_refs[at][7 : 7 + half]
        if not parts:
            out_refs[at][0] = total.astype(jnp.bfloat16)
            continue
        rounded = total.astype(jnp.bfloat16).astype(jnp.float32)
        tiles = rounded.reshape(half // 8, 8, co)
        stat_ref[2 * at] += jnp.sum(tiles, axis=0)
        stat_ref[2 * at + 1] += jnp.sum(tiles * tiles, axis=0)
        slot = lax.rem(step, 2)

        @pl.when(step >= 2)
        def _(at=at, slot=slot):
            for copy in piece_copies(at, slot, step):
                copy.wait()

        for part in range(parts):
            piece = rounded[part * part_width : (part + 1) * part_width]
            part_ref[slot, at, part, 0:part_width] = piece.astype(jnp.bfloat16)
        for copy in piece_copies(at, slot, step):
            copy.start()

    if parts:
        @pl.when(step == steps - 1)
        def _():
            closing = []
            if sums_out:
                sums_out[0][...] = stat_ref[...]
            else:
                rows = []
                for at in range(2 * len(jobs)):
                    total = stat_ref[at]
                    for ref in sums_refs:
                        total = total + ref[at]
                    rows += split_three(jnp.sum(total, axis=0, keepdims=True))
                blank = jnp.zeros((STAT_ROWS - len(rows), co), jnp.float32)
                closing_ref[...] = jnp.concatenate(rows + [blank], axis=0).astype(jnp.bfloat16)
                closing = [
                    pltpu.make_async_copy(closing_ref, out.at[0:STAT_ROWS], tail_sem.at[flip])
                    for flip, out in enumerate(out_refs)
                ]
            for copy in closing:
                copy.start()
            for at in range(len(jobs)):
                for back in range(min(steps, 2)):
                    for copy in piece_copies(at, lax.rem(step - back, 2), step - back):
                        copy.wait()
            for copy in closing:
                copy.wait()


def conv_frames(frames, halo, weight, clip_ids, first, sources, jobs, row=0, steps=None,
                addends=(), parts=0, sums=(), sums_out=False, lead=0, kept=(), weigh=1, vmem=60):
    _, band, width, ci = frames.shape
    co = weight.shape[2]
    half = width // 2
    steps = steps or band // 2
    part_width = half // parts if parts else half
    part_rows = rounded_up(part_width)
    taps = sorted({tap for _, some, _ in jobs for _, tap in some})
    tap_first, tap_count = 0, 3
    if len(taps) == 1 or taps == [0, 1]:
        tap_first, tap_count = taps[0], len(taps)
    plan = dict(jobs=jobs, addends=len(addends), parts=parts, part_rows=part_rows, lead=lead,
                part_width=part_width, first=first, steps=steps, kept=len(kept),
                sums_in=len(sums), sums_out=sums_out, tap_first=tap_first, count=frames.shape[0])
    block = first // sources
    above = (frames, 2 * row - 1) if row else (halo, 0)
    in_specs = [
        pl.BlockSpec((sources, 2, width, ci), lambda i, *_: (block, row + i, 0, 0)),
        pl.BlockSpec((sources, 1, width, ci), lambda i, *_: (block, above[1], 0, 0)),
        pl.BlockSpec((tap_count, 9 * ci, co), lambda i, *_: (tap_first // tap_count, 0, 0)),
    ]
    in_specs += [pl.BlockSpec((1, None, half, co), lambda i, *_: (0, i, 0, 0)) for _ in addends]
    in_specs += [pl.BlockSpec(a.shape, lambda i, *_: (0, 0, 0)) for a in sums]
    in_specs += [pl.BlockSpec(memory_space=pl.ANY) for _ in kept]
    operands = [clip_ids, frames, above[0], weight, *addends, *sums, *kept]
    aliases = {len(operands) - len(kept) + at: at for at in range(len(kept))}
    if parts:
        rows = lead + len(jobs) * steps * part_rows
        shape = kept[0].shape if kept else (rows, co)
        out_shape = [jax.ShapeDtypeStruct(shape, jnp.bfloat16) for _ in range(parts)]
        out_specs = [pl.BlockSpec(memory_space=pl.ANY) for _ in range(parts)]
    else:
        out_shape = [jax.ShapeDtypeStruct((1, steps, half, co), jnp.bfloat16) for _ in jobs]
        out_specs = [pl.BlockSpec((1, None, half, co), lambda i, *_: (0, i, 0, 0)) for _ in jobs]
    if sums_out:
        shape = (2 * len(jobs), 8, co)
        out_shape.append(jax.ShapeDtypeStruct(shape, jnp.float32))
        out_specs.append(pl.BlockSpec(shape, lambda i, *_: (0, 0, 0)))
    products = sum(len(some) for _, some, _ in jobs)
    return pl.pallas_call(
        functools.partial(conv_kernel, plan),
        out_shape=out_shape,
        grid_spec=pltpu.PrefetchScalarGridSpec(
            num_scalar_prefetch=1,
            grid=(steps,),
            in_specs=in_specs,
            out_specs=out_specs,
            scratch_shapes=[
                *[pltpu.VMEM((3, half, 2 * ci), jnp.bfloat16) for _ in range(sources)],
                *[pltpu.VMEM((half, co), jnp.float32) for _ in jobs],
                *[pltpu.VMEM((8 + half, co), jnp.float32) for _ in jobs],
                pltpu.VMEM((2, len(jobs), max(parts, 1), part_rows, co), jnp.bfloat16),
                pltpu.VMEM((2 * len(jobs), 8, co), jnp.float32),
                pltpu.VMEM((STAT_ROWS, co), jnp.bfloat16),
                pltpu.SemaphoreType.DMA((2, len(jobs), max(parts, 1))),
                pltpu.SemaphoreType.DMA((max(parts, 1),)),
            ],
        ),
        input_output_aliases=aliases,
        cost_estimate=pl.CostEstimate(
            flops=2 * weigh * products * steps * half * 9 * ci * co,
            bytes_accessed=weigh * (4 * sources * steps * width * ci + 2 * len(jobs) * steps * half * co),
            transcendentals=0,
        ),
        compiler_params=pltpu.CompilerParams(vmem_limit_bytes=vmem * 1024 * 1024),
    )(*operands)


def norm_kernel(plan, *refs):
    parts, jobs, steps, rows = plan["parts"], plan["jobs"], plan["steps"], plan["rows"]
    lead, part_rows = plan["lead"], plan["part_rows"]
    data_refs, (gain_ref, bias_ref) = refs[:parts], refs[parts : parts + 2]
    out_ref, done_ref, scale_ref = refs[-3:]
    frame, step = pl.program_id(0), pl.program_id(1)
    part_width, co = out_ref.shape[-2:]

    @pl.when((frame == 0) & (step == 0))
    def _():
        scale_ref[...] = jnp.zeros_like(scale_ref)
        total = data_refs[0][0:STAT_ROWS].astype(jnp.float32)
        for flip in range(1, parts):
            total = total + data_refs[flip][0:STAT_ROWS].astype(jnp.float32)
        size = co // GROUPS
        same = (lax.broadcasted_iota(jnp.int32, (co, co), 0) // size
                == lax.broadcasted_iota(jnp.int32, (co, co), 1) // size).astype(jnp.float32)
        grouped = jnp.dot(total, same, precision=lax.Precision.HIGHEST,
                          preferred_element_type=jnp.float32)
        for at in range(jobs):
            def taken(which):
                base = 6 * at + 3 * which
                return grouped[base : base + 1] + grouped[base + 1 : base + 2] + grouped[base + 2 : base + 3]
            mean = taken(0) / plan["entries"]
            variance = taken(1) / plan["entries"] - mean * mean
            scale_ref[at, 0:1] = mean
            scale_ref[at, 1:2] = lax.rsqrt(variance + EPS) * gain_ref[...]

    done_ref[...] = scale_ref[0]
    mean = scale_ref[frame, 0:1]
    scale = scale_ref[frame, 1:2]
    bias = bias_ref[...]
    mine = lax.axis_index("rows")
    for at in range(rows):
        row = step * rows + at
        if plan["top_first"]:
            place = jnp.where(row == 0, frame, jobs + frame * (steps - 1) + row - 1)
        else:
            place = frame * steps + row
        offset = pl.multiple_of(lead + place * part_rows, 16)
        for flip in range(parts):
            values = data_refs[flip][pl.ds(offset, part_rows)][0:part_width].astype(jnp.float32)
            value = 0.5 * ((values - mean) * scale + bias)
            out_ref[0, mine ^ flip, at] = (value + value * jnp.tanh(value)).astype(jnp.bfloat16)


def norm_frames(messages, gain, bias, first, jobs, shape, top_first=False, base=None, vmem=20):
    frames, parts, steps, part_width, co = shape
    rows = 2 if steps % 2 == 0 else 1
    plan = dict(parts=parts, jobs=jobs, steps=steps, rows=rows, lead=STAT_ROWS,
                part_rows=rounded_up(part_width), top_first=top_first,
                entries=float(parts * steps * part_width * parts * (co // GROUPS)))
    in_specs = (
        [pl.BlockSpec(message.shape, lambda f, i, *_: (0, 0)) for message in messages]
        + [pl.BlockSpec((1, co), lambda f, i, *_: (0, 0))] * 2
    )
    operands = [*messages, gain, bias]
    aliases = {}
    if base is not None:
        in_specs.append(pl.BlockSpec(memory_space=pl.ANY))
        aliases = {len(operands): 0}
        operands.append(base)
    return pl.pallas_call(
        functools.partial(norm_kernel, plan),
        out_shape=[jax.ShapeDtypeStruct(shape, jnp.bfloat16), jax.ShapeDtypeStruct((8, co), jnp.float32)],
        grid_spec=pltpu.PrefetchScalarGridSpec(
            num_scalar_prefetch=0,
            grid=(jobs, steps // rows),
            in_specs=in_specs,
            out_specs=[
                pl.BlockSpec((1, parts, rows, part_width, co), lambda f, i, *_: (first + f, 0, i, 0, 0)),
                pl.BlockSpec((8, co), lambda f, i, *_: (0, 0)),
            ],
            scratch_shapes=[pltpu.VMEM((jobs, 8, co), jnp.float32)],
        ),
        input_output_aliases=aliases,
        cost_estimate=pl.CostEstimate(
            flops=8 * jobs * parts * steps * part_width * co,
            bytes_accessed=4 * jobs * parts * steps * part_width * co,
            transcendentals=jobs * parts * steps * part_width * co,
        ),
        compiler_params=pltpu.CompilerParams(vmem_limit_bytes=vmem * 1024 * 1024),
    )(*operands)


def on_device(frames, clip_ids, conv_weight, norm_gain, norm_bias):
    count, band, width, ci = frames.shape
    co = conv_weight.shape[4]
    parts = lax.axis_size("rows")
    weight = conv_weight.reshape(3, 9 * ci, co)
    gain, bias = norm_gain.reshape(1, co), norm_bias.reshape(1, co)
    steps = band // 2
    shape = (count, parts, steps, width // 2 // parts, co)
    part_rows = rounded_up(shape[3])
    top_rows = STAT_ROWS + 2 * part_rows

    def named(name, function, *args, **keywords):
        with jax.named_scope(name):
            return function(*args, **keywords)

    def whole(sent, got):
        return [sent[0]] + [got[flip] for flip in range(1, parts)]

    chain = []

    def send_far(name, sent, *earlier):
        got = {}
        for flip in [flip for flip in range(parts - 1, 0, -1) if 2 * flip >= parts]:
            before = chain[-4:][:1] if len(chain) >= 4 else []
            got[flip] = named(f"{name}{flip}", exchanged, after(sent[flip], *before, *earlier), "rows", flip)
            chain.append(got[flip])
        return got

    def send_near(name, sent, single, *earlier):
        got = {}
        for flip in near:
            got[flip] = named(f"{name}{flip}", exchanged, after(sent[flip], *earlier), "rows", flip)
            if single:
                earlier = (got[flip],)
        return got

    near = [flip for flip in range(1, parts) if 2 * flip < parts]
    halo = named("halo", passed_along, frames[:, -1:], "rows", 1)

    later = [(2, [(0, 0), (1, 1), (2, 2)], None), (3, [(1, 0), (2, 1), (3, 2)], None)]
    run = functools.partial(conv_frames, frames, halo, weight, clip_ids)
    *a_sent, a_sums = named("conv_a", run, 0, 4, later, row=1, steps=steps - 1, parts=parts,
                            sums_out=True, lead=top_rows, vmem=63)
    a_sent = named("conv_top", run, 0, 4, later, steps=1, parts=parts, sums=(a_sums,),
                   lead=STAT_ROWS, kept=a_sent, weigh=1, vmem=63)
    a_got = send_far("a", a_sent)
    run = functools.partial(conv_frames, frames, after(halo, a_sent[0]), weight, clip_ids)
    ahead, = named("conv_hist0", run, 2, 2, [(4, [(0, 0), (1, 1)], None)])
    first_add = named("hist0", passed_along, ahead, "tm", 1)
    run = functools.partial(conv_frames, frames, after(halo, ahead), weight, clip_ids)
    onward, = named("conv_hist1", run, 3, 1, [(5, [(0, 0)], None)], weigh=40)
    second_add = named("hist1", passed_along, after(onward, first_add), "tm", 1)
    a_got.update(send_near("a", a_sent, True, a_sums))
    b_sent = named("conv_b", run, 0, 1, [(0, [(0, 2)], 0)],
                   addends=(after(first_add, onward, *[a_got[flip] for flip in near]),), parts=parts,
                   lead=STAT_ROWS, weigh=20, vmem=24)
    b_got = send_far("b", b_sent)
    c_sent = named("conv_c", run, 0, 2, [(1, [(0, 1), (1, 2)], 0)], addends=(second_add,), parts=parts,
                   lead=STAT_ROWS, weigh=20, vmem=24)
    out, a_done = named("norm_a", norm_frames, whole(a_sent, a_got), gain, bias, 2, 2, shape, top_first=True, vmem=20)
    b_got.update(send_near("b", b_sent, False, c_sent[0]))
    c_got = send_far("c", c_sent, a_done)
    out, b_done = named("norm_b", norm_frames, whole(b_sent, b_got), gain, bias, 0, 1, shape, base=out, vmem=20)
    c_got.update(send_near("c", c_sent, False, b_done))
    out, _ = named("norm_c", norm_frames, whole(c_sent, c_got), gain, bias, 1, 1, shape, base=out, vmem=64)
    return out.reshape(count, parts * steps, shape[3], co)


def solution(mesh):
    in_specs = (P("tm", "rows", None, None), P(), P(), P(), P())
    out_specs = P("tm", None, "rows", None)
    return jax.shard_map(
        on_device, mesh=mesh, in_specs=in_specs, out_specs=out_specs, check_vma=False
    )
```

```python
import functools

import jax
import jax.numpy as jnp
from jax import lax
from jax.experimental import pallas as pl
from jax.experimental.pallas import tpu as pltpu
from jax.sharding import PartitionSpec as P

GROUPS = 32
EPS = 1e-05
STAT_ROWS = 16


def passed_along(array, axis, by):
    length = lax.axis_size(axis)
    pairs = [(i, i + by) for i in range(length) if 0 <= i + by < length]
    return lax.ppermute(array, axis, pairs)


def exchanged(array, axis, flip):
    length = lax.axis_size(axis)
    return lax.ppermute(array, axis, [(i, i ^ flip) for i in range(length)])


def after(array, *earlier):
    return lax.optimization_barrier((array, *earlier))[0]


def rounded_up(rows):
    return -(-rows // 16) * 16


def split_columns(row_ref, slab_ref):
    width, ci = row_ref.shape
    half = width // 2
    slab_ref[:, 0:ci] = row_ref[pl.ds(0, half, stride=2), :]
    slab_ref[:, ci:] = row_ref[pl.ds(1, half, stride=2), :]


def split_three(total):
    high = total.astype(jnp.bfloat16).astype(jnp.float32)
    rest = total - high
    middle = rest.astype(jnp.bfloat16).astype(jnp.float32)
    return [high, middle, rest - middle]


def conv_kernel(plan, clip_ref, *refs):
    jobs, plains, parts, part_rows, part_width = (
        plan["jobs"], plan["plains"], plan["parts"], plan["part_rows"], plan["part_width"])
    lead, steps, sources, taps = plan["lead"], plan["steps"], plan["sources"], plan["taps"]

    def take(number):
        nonlocal refs
        some, refs = refs[:number], refs[number:]
        return some

    x_refs, above_refs, w_refs = take(sources), take(sources), take(len(taps))
    add_refs = take(plan["addends"])
    sums_refs = take(plan["sums_in"])
    take(plan["kept"])
    out_refs = take(parts)
    plain_refs = take(len(plains))
    sums_out = take(1 if plan["sums_out"] else 0)
    works = jobs + plains
    slab_refs, main_refs, left_refs = take(sources), take(len(works)), take(len(works))
    part_ref, stat_ref, closing_ref, part_sem, tail_sem = refs
    step = pl.program_id(0)
    ci = x_refs[0].shape[3]
    half, co = main_refs[0].shape
    above = lax.rem(step + 1, 2)
    below = lax.rem(step, 2)
    start = lax.axis_index("tm") * plan["count"]
    last = clip_ref.shape[0] - 1

    @pl.when(step == 0)
    def _():
        for source in range(sources):
            split_columns(above_refs[source].at[0, 0], slab_refs[source].at[1])
        for left_ref in left_refs:
            left_ref[0:8] = jnp.zeros((8, co), jnp.float32)
        stat_ref[...] = jnp.zeros_like(stat_ref)

    def piece_copies(at, slot, step):
        mine = lax.axis_index("rows")
        offset = pl.multiple_of(lead + (at * steps + step) * part_rows, 16)
        return [
            pltpu.make_async_copy(part_ref.at[slot, at, mine ^ flip],
                                  out.at[pl.ds(offset, part_rows)], part_sem.at[slot, at, flip])
            for flip, out in enumerate(out_refs)
        ]

    def products(source, tap):
        slab_ref, w_ref = slab_refs[source], w_refs[taps.index(tap)]
        rows = [slab_ref[above], slab_ref[2], slab_ref[below]]
        main = jnp.dot(
            jnp.concatenate(rows, axis=1),
            jnp.concatenate([w_ref[0, (3 * a + 1) * ci : (3 * a + 3) * ci] for a in range(3)], axis=0),
            preferred_element_type=jnp.float32)
        left = jnp.dot(
            jnp.concatenate([row[:, ci:] for row in rows], axis=1),
            jnp.concatenate([w_ref[0, 3 * a * ci : (3 * a + 1) * ci] for a in range(3)], axis=0),
            preferred_element_type=jnp.float32)
        return main, left

    empty = [True] * len(works)
    for source in range(sources):
        split_columns(x_refs[source].at[0, 0], slab_refs[source].at[2])
        split_columns(x_refs[source].at[0, 1], slab_refs[source].at[below])
        frame = plan["first"] + source
        for at, (target, pairs, addend) in enumerate(works):
            for tap in [tap for other, tap in pairs if other == source]:
                main, left = products(source, tap)
                if frame != target:
                    same = clip_ref[start + frame] == clip_ref[jnp.minimum(start + target, last)]
                    same = same.astype(jnp.float32)
                    main, left = main * same, left * same
                if empty[at]:
                    if addend is not None:
                        main = main + add_refs[addend][0].astype(jnp.float32)
                    main_refs[at][...] = main
                    left_refs[at][8:] = left
                else:
                    main_refs[at][...] += main
                    left_refs[at][8:] += left
                empty[at] = False

    for at in range(len(works)):
        total = main_refs[at][...] + left_refs[at][7 : 7 + half]
        if at >= len(jobs):
            plain_refs[at - len(jobs)][0] = total.astype(jnp.bfloat16)
            continue
        rounded = total.astype(jnp.bfloat16).astype(jnp.float32)
        tiles = rounded.reshape(half // 8, 8, co)
        stat_ref[2 * at] += jnp.sum(tiles, axis=0)
        stat_ref[2 * at + 1] += jnp.sum(tiles * tiles, axis=0)
        slot = lax.rem(step, 2)

        @pl.when(step >= 2)
        def _(at=at, slot=slot):
            for copy in piece_copies(at, slot, step):
                copy.wait()

        for part in range(parts):
            piece = rounded[part * part_width : (part + 1) * part_width]
            part_ref[slot, at, part, 0:part_width] = piece.astype(jnp.bfloat16)
        for copy in piece_copies(at, slot, step):
            copy.start()

    @pl.when(step == steps - 1)
    def _():
        closing = []
        if sums_out:
            sums_out[0][...] = stat_ref[...]
        else:
            rows = []
            for at in range(2 * len(jobs)):
                total = stat_ref[at]
                for ref in sums_refs:
                    total = total + ref[at]
                rows += split_three(jnp.sum(total, axis=0, keepdims=True))
            blank = jnp.zeros((STAT_ROWS - len(rows), co), jnp.float32)
            closing_ref[...] = jnp.concatenate(rows + [blank], axis=0).astype(jnp.bfloat16)
            closing = [
                pltpu.make_async_copy(closing_ref, out.at[0:STAT_ROWS], tail_sem.at[flip])
                for flip, out in enumerate(out_refs)
            ]
        for copy in closing:
            copy.start()
        for at in range(len(jobs)):
            for back in range(min(steps, 2)):
                for copy in piece_copies(at, lax.rem(step - back, 2), step - back):
                    copy.wait()
        for copy in closing:
            copy.wait()


def conv_frames(frames, halo, weight, clip_ids, parts, first, sources, jobs, plains=(), row=0,
                steps=None, addends=(), sums=(), sums_out=False, lead=0, kept=(), weigh=1, vmem=56):
    _, band, width, ci = frames.shape
    co = weight.shape[2]
    half = width // 2
    steps = steps or band // 2
    part_width = half // parts
    part_rows = rounded_up(part_width)
    works = list(jobs) + list(plains)
    taps = sorted({tap for _, pairs, _ in works for _, tap in pairs})
    plan = dict(jobs=list(jobs), plains=list(plains), addends=len(addends), parts=parts,
                part_rows=part_rows, lead=lead, part_width=part_width, first=first, steps=steps,
                kept=len(kept), sums_in=len(sums), sums_out=sums_out, sources=sources, taps=taps,
                count=frames.shape[0])
    above, above_row = (frames, 2 * row - 1) if row else (halo, 0)
    plain_spec = pl.BlockSpec((1, None, half, co), lambda i, *_: (0, row + i, 0, 0))
    frame_spec = lambda source: pl.BlockSpec((1, 2, width, ci), lambda i, *_: (source, row + i, 0, 0))
    above_spec = lambda source: pl.BlockSpec((1, 1, width, ci), lambda i, *_: (source, above_row, 0, 0))
    tap_spec = lambda tap: pl.BlockSpec((1, 9 * ci, co), lambda i, *_: (tap, 0, 0))
    in_specs = [frame_spec(first + source) for source in range(sources)]
    in_specs += [above_spec(first + source) for source in range(sources)]
    in_specs += [tap_spec(tap) for tap in taps]
    in_specs += [plain_spec for _ in addends]
    in_specs += [pl.BlockSpec(a.shape, lambda i, *_: (0, 0, 0)) for a in sums]
    in_specs += [pl.BlockSpec(memory_space=pl.ANY) for _ in kept]
    operands = [clip_ids, *[frames] * sources, *[above] * sources, *[weight] * len(taps),
                *addends, *sums, *kept]
    aliases = {len(operands) - len(kept) + at: at for at in range(len(kept))}
    rows = lead + len(jobs) * steps * part_rows
    shape = kept[0].shape if kept else (rows, co)
    out_shape = [jax.ShapeDtypeStruct(shape, jnp.bfloat16) for _ in range(parts)]
    out_specs = [pl.BlockSpec(memory_space=pl.ANY) for _ in range(parts)]
    out_shape += [jax.ShapeDtypeStruct((1, band // 2, half, co), jnp.bfloat16) for _ in plains]
    out_specs += [plain_spec for _ in plains]
    if sums_out:
        shape = (2 * len(jobs), 8, co)
        out_shape.append(jax.ShapeDtypeStruct(shape, jnp.float32))
        out_specs.append(pl.BlockSpec(shape, lambda i, *_: (0, 0, 0)))
    products = sum(len(pairs) for _, pairs, _ in works)
    return pl.pallas_call(
        functools.partial(conv_kernel, plan),
        out_shape=out_shape,
        grid_spec=pltpu.PrefetchScalarGridSpec(
            num_scalar_prefetch=1,
            grid=(steps,),
            in_specs=in_specs,
            out_specs=out_specs,
            scratch_shapes=[
                *[pltpu.VMEM((3, half, 2 * ci), jnp.bfloat16) for _ in range(sources)],
                *[pltpu.VMEM((half, co), jnp.float32) for _ in works],
                *[pltpu.VMEM((8 + half, co), jnp.float32) for _ in works],
                pltpu.VMEM((2, len(jobs), parts, part_rows, co), jnp.bfloat16),
                pltpu.VMEM((2 * len(jobs), 8, co), jnp.float32),
                pltpu.VMEM((STAT_ROWS, co), jnp.bfloat16),
                pltpu.SemaphoreType.DMA((2, len(jobs), parts)),
                pltpu.SemaphoreType.DMA((parts,)),
            ],
        ),
        input_output_aliases=aliases,
        cost_estimate=pl.CostEstimate(
            flops=2 * weigh * products * steps * half * 9 * ci * co,
            bytes_accessed=weigh * (4 * sources * steps * width * ci + 2 * len(works) * steps * half * co),
            transcendentals=0,
        ),
        compiler_params=pltpu.CompilerParams(vmem_limit_bytes=vmem * 1024 * 1024),
    )(*operands)


def norm_kernel(plan, *refs):
    parts, jobs, steps, rows = plan["parts"], plan["jobs"], plan["steps"], plan["rows"]
    lead, part_rows = plan["lead"], plan["part_rows"]
    data_refs, (gain_ref, bias_ref) = refs[:parts], refs[parts : parts + 2]
    out_ref, done_ref, scale_ref = refs[-3:]
    frame, step = pl.program_id(0), pl.program_id(1)
    part_width, co = out_ref.shape[-2:]

    @pl.when((frame == 0) & (step == 0))
    def _():
        scale_ref[...] = jnp.zeros_like(scale_ref)
        total = data_refs[0][0:STAT_ROWS].astype(jnp.float32)
        for flip in range(1, parts):
            total = total + data_refs[flip][0:STAT_ROWS].astype(jnp.float32)
        size = co // GROUPS
        same = (lax.broadcasted_iota(jnp.int32, (co, co), 0) // size
                == lax.broadcasted_iota(jnp.int32, (co, co), 1) // size).astype(jnp.float32)
        grouped = jnp.dot(total, same, precision=lax.Precision.HIGHEST,
                          preferred_element_type=jnp.float32)
        for at in range(jobs):
            def taken(which):
                base = 6 * at + 3 * which
                return grouped[base : base + 1] + grouped[base + 1 : base + 2] + grouped[base + 2 : base + 3]
            mean = taken(0) / plan["entries"]
            variance = taken(1) / plan["entries"] - mean * mean
            scale_ref[at, 0:1] = mean
            scale_ref[at, 1:2] = lax.rsqrt(variance + EPS) * gain_ref[...]

    done_ref[...] = scale_ref[0]
    mean = scale_ref[frame, 0:1]
    scale = scale_ref[frame, 1:2]
    bias = bias_ref[...]
    mine = lax.axis_index("rows")
    for at in range(rows):
        row = step * rows + at
        if plan["top_first"]:
            place = jnp.where(row == 0, frame, jobs + frame * (steps - 1) + row - 1)
        else:
            place = frame * steps + row
        offset = pl.multiple_of(lead + place * part_rows, 16)
        for flip in range(parts):
            values = data_refs[flip][pl.ds(offset, part_rows)][0:part_width].astype(jnp.float32)
            value = 0.5 * ((values - mean) * scale + bias)
            out_ref[0, mine ^ flip, at] = (value + value * jnp.tanh(value)).astype(jnp.bfloat16)


def norm_frames(messages, gain, bias, first, jobs, shape, top_first=False, base=None, vmem=20):
    frames, parts, steps, part_width, co = shape
    rows = 2 if steps % 2 == 0 else 1
    plan = dict(parts=parts, jobs=jobs, steps=steps, rows=rows, lead=STAT_ROWS,
                part_rows=rounded_up(part_width), top_first=top_first,
                entries=float(parts * steps * part_width * parts * (co // GROUPS)))
    in_specs = (
        [pl.BlockSpec(message.shape, lambda f, i, *_: (0, 0)) for message in messages]
        + [pl.BlockSpec((1, co), lambda f, i, *_: (0, 0))] * 2
    )
    operands = [*messages, gain, bias]
    aliases = {}
    if base is not None:
        in_specs.append(pl.BlockSpec(memory_space=pl.ANY))
        aliases = {len(operands): 0}
        operands.append(base)
    return pl.pallas_call(
        functools.partial(norm_kernel, plan),
        out_shape=[jax.ShapeDtypeStruct(shape, jnp.bfloat16), jax.ShapeDtypeStruct((8, co), jnp.float32)],
        grid_spec=pltpu.PrefetchScalarGridSpec(
            num_scalar_prefetch=0,
            grid=(jobs, steps // rows),
            in_specs=in_specs,
            out_specs=[
                pl.BlockSpec((1, parts, rows, part_width, co), lambda f, i, *_: (first + f, 0, i, 0, 0)),
                pl.BlockSpec((8, co), lambda f, i, *_: (0, 0)),
            ],
            scratch_shapes=[pltpu.VMEM((jobs, 8, co), jnp.float32)],
        ),
        input_output_aliases=aliases,
        cost_estimate=pl.CostEstimate(
            flops=8 * jobs * parts * steps * part_width * co,
            bytes_accessed=4 * jobs * parts * steps * part_width * co,
            transcendentals=jobs * parts * steps * part_width * co,
        ),
        compiler_params=pltpu.CompilerParams(vmem_limit_bytes=vmem * 1024 * 1024),
    )(*operands)


def on_device(frames, clip_ids, conv_weight, norm_gain, norm_bias):
    count, band, width, ci = frames.shape
    co = conv_weight.shape[4]
    parts = lax.axis_size("rows")
    weight = conv_weight.reshape(3, 9 * ci, co)
    gain, bias = norm_gain.reshape(1, co), norm_bias.reshape(1, co)
    steps = band // 2
    shape = (count, parts, steps, width // 2 // parts, co)
    part_rows = rounded_up(shape[3])
    top_rows = STAT_ROWS + 2 * part_rows

    def named(name, function, *args, **keywords):
        with jax.named_scope(name):
            return function(*args, **keywords)

    def whole(sent, got):
        return [sent[0]] + [got[flip] for flip in range(1, parts)]

    near = [flip for flip in range(1, parts) if 2 * flip < parts]
    chain = []

    def send_far(name, sent, *earlier):
        got = {}
        for flip in [flip for flip in range(parts - 1, 0, -1) if 2 * flip >= parts]:
            before = chain[-4:][:1] if len(chain) >= 4 else []
            got[flip] = named(f"{name}{flip}", exchanged, after(sent[flip], *before, *earlier), "rows", flip)
            chain.append(got[flip])
        return got

    def send_near(name, sent, single, *earlier):
        got = {}
        for flip in near:
            got[flip] = named(f"{name}{flip}", exchanged, after(sent[flip], *earlier), "rows", flip)
            if single:
                earlier = (got[flip],)
        return got

    halo = named("halo", passed_along, frames[:, -1:], "rows", 1)
    later = [(2, [(0, 0), (1, 1), (2, 2)], None), (3, [(1, 0), (2, 1), (3, 2)], None)]
    onward = [(4, [(2, 0), (3, 1)], None), (5, [(3, 0)], None)]
    run = functools.partial(conv_frames, frames, halo, weight, clip_ids, parts)
    *kept, a_sums = named("conv_a", run, 0, 4, later, onward, row=1, steps=steps - 1,
                          sums_out=True, lead=top_rows, weigh=1, vmem=56)
    *a_sent, first_on, second_on = named("conv_top", run, 0, 4, later, onward, steps=1, sums=(a_sums,),
                                         lead=STAT_ROWS, kept=kept, weigh=1, vmem=56)
    first_add = named("hist0", passed_along, first_on, "tm", 1)
    second_add = named("hist1", passed_along, after(second_on, first_add), "tm", 1)
    a_got = send_far("a", a_sent)
    a_got.update(send_near("a", a_sent, True, a_sums))
    b_sent = named("conv_b", run, 0, 1, [(0, [(0, 2)], 0)], addends=(after(first_add, a_sums),),
                   lead=STAT_ROWS, weigh=20, vmem=56)
    b_got = send_far("b", b_sent)
    c_sent = named("conv_c", run, 0, 2, [(1, [(0, 1), (1, 2)], 0)], addends=(after(second_add, a_sums),),
                   lead=STAT_ROWS, weigh=20, vmem=56)
    out, a_done = named("norm_a", norm_frames, whole(a_sent, a_got), gain, bias, 2, 2, shape, top_first=True, vmem=20)
    b_got.update(send_near("b", b_sent, False, c_sent[0]))
    c_got = send_near("c", c_sent, False, c_sent[0])
    c_got.update(send_far("c", c_sent, c_sent[0]))
    out, b_done = named("norm_b", norm_frames, whole(b_sent, b_got), gain, bias, 0, 1, shape, base=out, vmem=20)
    out, _ = named("norm_c", norm_frames, whole(c_sent, c_got), gain, bias, 1, 1, shape, base=out, vmem=20)
    return out.reshape(count, parts * steps, shape[3], co)


def solution(mesh):
    in_specs = (P("tm", "rows", None, None), P(), P(), P(), P())
    out_specs = P("tm", None, "rows", None)
    return jax.shard_map(
        on_device, mesh=mesh, in_specs=in_specs, out_specs=out_specs, check_vma=False
    )
```

```python
import functools

import jax
import jax.numpy as jnp
from jax import lax
from jax.experimental import pallas as pl
from jax.experimental.pallas import tpu as pltpu
from jax.sharding import PartitionSpec as P

GROUPS = 32
EPS = 1e-05
STAT_ROWS = 16


def passed_along(array, axis, by):
    length = lax.axis_size(axis)
    pairs = [(i, i + by) for i in range(length) if 0 <= i + by < length]
    return lax.ppermute(array, axis, pairs)


def exchanged(array, axis, flip):
    length = lax.axis_size(axis)
    return lax.ppermute(array, axis, [(i, i ^ flip) for i in range(length)])


def after(array, *earlier):
    return lax.optimization_barrier((array, *earlier))[0]


def rounded_up(rows):
    return -(-rows // 16) * 16


def split_columns(row_ref, slab_ref):
    width, ci = row_ref.shape
    half = width // 2
    slab_ref[:, 0:ci] = row_ref[pl.ds(0, half, stride=2), :]
    slab_ref[:, ci:] = row_ref[pl.ds(1, half, stride=2), :]


def split_three(total):
    high = total.astype(jnp.bfloat16).astype(jnp.float32)
    rest = total - high
    middle = rest.astype(jnp.bfloat16).astype(jnp.float32)
    return [high, middle, rest - middle]


def conv_kernel(plan, clip_ref, *refs):
    jobs, plains, parts, part_rows, part_width = (
        plan["jobs"], plan["plains"], plan["parts"], plan["part_rows"], plan["part_width"])
    leads, steps, sources, taps = plan["leads"], plan["steps"], plan["sources"], plan["taps"]

    def take(number):
        nonlocal refs
        some, refs = refs[:number], refs[number:]
        return some

    x_refs, above_refs, w_refs = take(sources), take(sources), take(len(taps))
    add_refs = take(plan["addends"])
    sums_refs = take(plan["sums_in"])
    take(plan["kept"])
    out_refs = take(parts)
    plain_refs = take(len(plains))
    sums_out = take(1 if plan["sums_out"] else 0)
    works = jobs + plains
    slab_refs, main_refs, left_refs = take(sources), take(len(works)), take(len(works))
    part_ref, stat_ref, closing_ref, part_sem, tail_sem = refs
    step = pl.program_id(0)
    ci = x_refs[0].shape[3]
    half, co = main_refs[0].shape
    above = lax.rem(step + 1, 2)
    below = lax.rem(step, 2)
    start = lax.axis_index("tm") * plan["count"]
    last = clip_ref.shape[0] - 1

    @pl.when(step == 0)
    def _():
        for source in range(sources):
            split_columns(above_refs[source].at[0, 0], slab_refs[source].at[1])
        for left_ref in left_refs:
            left_ref[0:8] = jnp.zeros((8, co), jnp.float32)
        stat_ref[...] = jnp.zeros_like(stat_ref)

    def piece_copies(at, slot, step):
        mine = lax.axis_index("rows")
        place = (at * steps + step) * part_rows
        return [
            pltpu.make_async_copy(
                part_ref.at[slot, at, mine ^ flip],
                out.at[pl.ds(pl.multiple_of(leads[flip] + place, 16), part_rows)],
                part_sem.at[slot, at, flip])
            for flip, out in enumerate(out_refs)
        ]

    def products(source, tap):
        slab_ref, w_ref = slab_refs[source], w_refs[taps.index(tap)]
        rows = [slab_ref[above], slab_ref[2], slab_ref[below]]
        main = jnp.dot(
            jnp.concatenate(rows, axis=1),
            jnp.concatenate([w_ref[0, (3 * a + 1) * ci : (3 * a + 3) * ci] for a in range(3)], axis=0),
            preferred_element_type=jnp.float32)
        left = jnp.dot(
            jnp.concatenate([row[:, ci:] for row in rows], axis=1),
            jnp.concatenate([w_ref[0, 3 * a * ci : (3 * a + 1) * ci] for a in range(3)], axis=0),
            preferred_element_type=jnp.float32)
        return main, left

    empty = [True] * len(works)
    for source in range(sources):
        split_columns(x_refs[source].at[0, 0], slab_refs[source].at[2])
        split_columns(x_refs[source].at[0, 1], slab_refs[source].at[below])
        frame = plan["first"] + source
        for at, (target, pairs, addend) in enumerate(works):
            for tap in [tap for other, tap in pairs if other == source]:
                main, left = products(source, tap)
                if frame != target:
                    same = clip_ref[start + frame] == clip_ref[jnp.minimum(start + target, last)]
                    same = same.astype(jnp.float32)
                    main, left = main * same, left * same
                if empty[at]:
                    if addend is not None:
                        main = main + add_refs[addend][0].astype(jnp.float32)
                    main_refs[at][...] = main
                    left_refs[at][8:] = left
                else:
                    main_refs[at][...] += main
                    left_refs[at][8:] += left
                empty[at] = False

    for at in range(len(works)):
        total = main_refs[at][...] + left_refs[at][7 : 7 + half]
        if at >= len(jobs):
            plain_refs[at - len(jobs)][0] = total.astype(jnp.bfloat16)
            continue
        rounded = total.astype(jnp.bfloat16).astype(jnp.float32)
        tiles = rounded.reshape(half // 8, 8, co)
        stat_ref[2 * at] += jnp.sum(tiles, axis=0)
        stat_ref[2 * at + 1] += jnp.sum(tiles * tiles, axis=0)
        slot = lax.rem(step, 2)

        @pl.when(step >= 2)
        def _(at=at, slot=slot):
            for copy in piece_copies(at, slot, step):
                copy.wait()

        for part in range(parts):
            piece = rounded[part * part_width : (part + 1) * part_width]
            part_ref[slot, at, part, 0:part_width] = piece.astype(jnp.bfloat16)
        for copy in piece_copies(at, slot, step):
            copy.start()

    if not jobs:
        return

    @pl.when(step == steps - 1)
    def _():
        closing = []
        if sums_out:
            sums_out[0][...] = stat_ref[...]
        else:
            rows = []
            for at in range(2 * len(jobs)):
                total = stat_ref[at]
                for ref in sums_refs:
                    total = total + ref[at]
                rows += split_three(jnp.sum(total, axis=0, keepdims=True))
            blank = jnp.zeros((STAT_ROWS - len(rows), co), jnp.float32)
            closing_ref[...] = jnp.concatenate(rows + [blank], axis=0).astype(jnp.bfloat16)
            closing = [
                pltpu.make_async_copy(closing_ref, out.at[0:STAT_ROWS], tail_sem.at[flip])
                for flip, out in enumerate(out_refs)
            ]
        for copy in closing:
            copy.start()
        for at in range(len(jobs)):
            for back in range(min(steps, 2)):
                for copy in piece_copies(at, lax.rem(step - back, 2), step - back):
                    copy.wait()
        for copy in closing:
            copy.wait()


def conv_frames(frames, halo, weight, clip_ids, parts, first, sources, jobs, plains=(), row=0,
                steps=None, addends=(), sums=(), sums_out=False, leads=(), kept=None, weigh=1, vmem=56):
    _, band, width, ci = frames.shape
    co = weight.shape[2]
    half = width // 2
    steps = steps or band // 2
    part_width = half // parts
    part_rows = rounded_up(part_width)
    works = list(jobs) + list(plains)
    kept = kept or {}
    leads = leads or [STAT_ROWS] * parts
    messages = parts if jobs else 0
    taps = sorted({tap for _, pairs, _ in works for _, tap in pairs})
    plan = dict(jobs=list(jobs), plains=list(plains), addends=len(addends), parts=messages,
                part_rows=part_rows, leads=list(leads), part_width=part_width, first=first,
                steps=steps, kept=len(kept), sums_in=len(sums), sums_out=sums_out, sources=sources, taps=taps,
                count=frames.shape[0])
    above, above_row = (frames, 2 * row - 1) if row else (halo, 0)
    plain_spec = pl.BlockSpec((1, None, half, co), lambda i, *_: (0, row + i, 0, 0))
    frame_spec = lambda source: pl.BlockSpec((1, 2, width, ci), lambda i, *_: (source, row + i, 0, 0))
    above_spec = lambda source: pl.BlockSpec((1, 1, width, ci), lambda i, *_: (source, above_row, 0, 0))
    tap_spec = lambda tap: pl.BlockSpec((1, 9 * ci, co), lambda i, *_: (tap, 0, 0))
    in_specs = [frame_spec(first + source) for source in range(sources)]
    in_specs += [above_spec(first + source) for source in range(sources)]
    in_specs += [tap_spec(tap) for tap in taps]
    in_specs += [plain_spec for _ in addends]
    in_specs += [pl.BlockSpec(a.shape, lambda i, *_: (0, 0, 0)) for a in sums]
    in_specs += [pl.BlockSpec(memory_space=pl.ANY) for _ in kept]
    operands = [clip_ids, *[frames] * sources, *[above] * sources, *[weight] * len(taps),
                *addends, *sums, *kept.values()]
    aliases = {len(operands) - len(kept) + at: flip for at, flip in enumerate(kept)}
    rows = len(jobs) * steps * part_rows
    out_shape = [jax.ShapeDtypeStruct(kept[flip].shape if flip in kept else (leads[flip] + rows, co),
                                      jnp.bfloat16) for flip in range(messages)]
    out_specs = [pl.BlockSpec(memory_space=pl.ANY) for _ in range(messages)]
    out_shape += [jax.ShapeDtypeStruct((1, band // 2, half, co), jnp.bfloat16) for _ in plains]
    out_specs += [plain_spec for _ in plains]
    if sums_out:
        shape = (2 * len(jobs), 8, co)
        out_shape.append(jax.ShapeDtypeStruct(shape, jnp.float32))
        out_specs.append(pl.BlockSpec(shape, lambda i, *_: (0, 0, 0)))
    products = sum(len(pairs) for _, pairs, _ in works)
    return pl.pallas_call(
        functools.partial(conv_kernel, plan),
        out_shape=out_shape,
        grid_spec=pltpu.PrefetchScalarGridSpec(
            num_scalar_prefetch=1,
            grid=(steps,),
            in_specs=in_specs,
            out_specs=out_specs,
            scratch_shapes=[
                *[pltpu.VMEM((3, half, 2 * ci), jnp.bfloat16) for _ in range(sources)],
                *[pltpu.VMEM((half, co), jnp.float32) for _ in works],
                *[pltpu.VMEM((8 + half, co), jnp.float32) for _ in works],
                pltpu.VMEM((2, max(len(jobs), 1), parts, part_rows, co), jnp.bfloat16),
                pltpu.VMEM((2 * max(len(jobs), 1), 8, co), jnp.float32),
                pltpu.VMEM((STAT_ROWS, co), jnp.bfloat16),
                pltpu.SemaphoreType.DMA((2, max(len(jobs), 1), parts)),
                pltpu.SemaphoreType.DMA((parts,)),
            ],
        ),
        input_output_aliases=aliases,
        cost_estimate=pl.CostEstimate(
            flops=2 * weigh * products * steps * half * 9 * ci * co,
            bytes_accessed=weigh * (4 * sources * steps * width * ci + 2 * len(works) * steps * half * co),
            transcendentals=0,
        ),
        compiler_params=pltpu.CompilerParams(vmem_limit_bytes=vmem * 1024 * 1024),
    )(*operands)


def norm_kernel(plan, *refs):
    parts, jobs, steps, rows = plan["parts"], plan["jobs"], plan["steps"], plan["rows"]
    part_rows, apart = plan["part_rows"], plan["apart"]
    data_refs, rest_refs = refs[:parts], refs[parts : parts + len(apart)]
    gain_ref, bias_ref = refs[parts + len(apart) : parts + len(apart) + 2]
    out_ref, done_ref, scale_ref = refs[-3:]
    frame, step = pl.program_id(0), pl.program_id(1)
    part_width, co = out_ref.shape[-2:]

    @pl.when((frame == 0) & (step == 0))
    def _():
        scale_ref[...] = jnp.zeros_like(scale_ref)
        total = data_refs[0][0:STAT_ROWS].astype(jnp.float32)
        for flip in range(1, parts):
            total = total + data_refs[flip][0:STAT_ROWS].astype(jnp.float32)
        size = co // GROUPS
        same = (lax.broadcasted_iota(jnp.int32, (co, co), 0) // size
                == lax.broadcasted_iota(jnp.int32, (co, co), 1) // size).astype(jnp.float32)
        grouped = jnp.dot(total, same, precision=lax.Precision.HIGHEST,
                          preferred_element_type=jnp.float32)
        for at in range(jobs):
            def taken(which):
                base = 6 * at + 3 * which
                return grouped[base : base + 1] + grouped[base + 1 : base + 2] + grouped[base + 2 : base + 3]
            mean = taken(0) / plan["entries"]
            variance = taken(1) / plan["entries"] - mean * mean
            scale_ref[at, 0:1] = mean
            scale_ref[at, 1:2] = lax.rsqrt(variance + EPS) * gain_ref[...]

    done_ref[...] = scale_ref[0]
    mean = scale_ref[frame, 0:1]
    scale = scale_ref[frame, 1:2]
    bias = bias_ref[...]
    mine = lax.axis_index("rows")
    top_rows = STAT_ROWS + jobs * part_rows

    def write(flip, at, ref, offset):
        values = ref[pl.ds(pl.multiple_of(offset, 16), part_rows)][0:part_width].astype(jnp.float32)
        value = 0.5 * ((values - mean) * scale + bias)
        out_ref[0, mine ^ flip, at] = (value + value * jnp.tanh(value)).astype(jnp.bfloat16)

    for at in range(rows):
        row = step * rows + at
        for flip in range(parts):
            if not plan["top_first"]:
                write(flip, at, data_refs[flip], STAT_ROWS + (frame * steps + row) * part_rows)
                continue
            rest, base = data_refs[flip], top_rows
            if flip in apart:
                rest, base = rest_refs[apart.index(flip)], 0
            below = base + (frame * (steps - 1) + row - 1) * part_rows
            if at > 0:
                write(flip, at, rest, below)
                continue

            @pl.when(row == 0)
            def _(flip=flip):
                write(flip, 0, data_refs[flip], STAT_ROWS + frame * part_rows)

            @pl.when(row > 0)
            def _(flip=flip, rest=rest, below=below):
                write(flip, 0, rest, below)


def norm_frames(messages, gain, bias, first, jobs, shape, top_first=False, rest=None, base=None,
                vmem=20):
    frames, parts, steps, part_width, co = shape
    rows = 2 if steps % 2 == 0 else 1
    rest = rest or {}
    plan = dict(parts=parts, jobs=jobs, steps=steps, rows=rows, apart=list(rest),
                part_rows=rounded_up(part_width), top_first=top_first,
                entries=float(parts * steps * part_width * parts * (co // GROUPS)))
    in_specs = (
        [pl.BlockSpec(message.shape, lambda f, i, *_: (0, 0)) for message in [*messages, *rest.values()]]
        + [pl.BlockSpec((1, co), lambda f, i, *_: (0, 0))] * 2
    )
    operands = [*messages, *rest.values(), gain, bias]
    aliases = {}
    if base is not None:
        in_specs.append(pl.BlockSpec(memory_space=pl.ANY))
        aliases = {len(operands): 0}
        operands.append(base)
    return pl.pallas_call(
        functools.partial(norm_kernel, plan),
        out_shape=[jax.ShapeDtypeStruct(shape, jnp.bfloat16), jax.ShapeDtypeStruct((8, co), jnp.float32)],
        grid_spec=pltpu.PrefetchScalarGridSpec(
            num_scalar_prefetch=0,
            grid=(jobs, steps // rows),
            in_specs=in_specs,
            out_specs=[
                pl.BlockSpec((1, parts, rows, part_width, co), lambda f, i, *_: (first + f, 0, i, 0, 0)),
                pl.BlockSpec((8, co), lambda f, i, *_: (0, 0)),
            ],
            scratch_shapes=[pltpu.VMEM((jobs, 8, co), jnp.float32)],
        ),
        input_output_aliases=aliases,
        cost_estimate=pl.CostEstimate(
            flops=8 * jobs * parts * steps * part_width * co,
            bytes_accessed=4 * jobs * parts * steps * part_width * co,
            transcendentals=jobs * parts * steps * part_width * co,
        ),
        compiler_params=pltpu.CompilerParams(vmem_limit_bytes=vmem * 1024 * 1024),
    )(*operands)


def on_device(frames, clip_ids, conv_weight, norm_gain, norm_bias):
    count, band, width, ci = frames.shape
    co = conv_weight.shape[4]
    parts = lax.axis_size("rows")
    weight = conv_weight.reshape(3, 9 * ci, co)
    gain, bias = norm_gain.reshape(1, co), norm_bias.reshape(1, co)
    steps = band // 2
    shape = (count, parts, steps, width // 2 // parts, co)
    part_rows = rounded_up(shape[3])
    top_rows = STAT_ROWS + 2 * part_rows

    def named(name, function, *args, **keywords):
        with jax.named_scope(name):
            return function(*args, **keywords)

    def whole(sent, got):
        return [sent[0]] + [got[flip] for flip in range(1, parts)]

    near = [flip for flip in range(1, parts) if 2 * flip < parts]
    far = [flip for flip in range(parts - 1, 0, -1) if 2 * flip >= parts]
    chain = []

    def send_far(name, sent):
        got = {}
        for flip in far:
            before = chain[-4:][:1] if len(chain) >= 4 else []
            got[flip] = named(f"{name}{flip}", exchanged, after(sent[flip], *before), "rows", flip)
            chain.append(got[flip])
        return got

    def send_near(name, sent, *earlier):
        return {flip: named(f"{name}{flip}", exchanged, after(sent[flip], *earlier), "rows", flip)
                for flip in near}

    halo = named("halo", passed_along, frames[:, -1:], "rows", 1)
    run = functools.partial(conv_frames, frames, halo, weight, clip_ids, parts)
    later = [(2, [(0, 0), (1, 1), (2, 2)], None), (3, [(1, 0), (2, 1), (3, 2)], None)]
    leads = [0 if flip in far else top_rows for flip in range(parts)]
    *a_sent, a_sums = named("conv_a", run, 0, 4, later, row=1, steps=steps - 1, sums_out=True,
                            leads=leads, vmem=56)
    a_got = send_far("a", a_sent)
    run = functools.partial(conv_frames, frames, after(halo, a_sums), weight, clip_ids, parts)
    ahead, = named("conv_hist0", run, 2, 2, [], [(4, [(0, 0), (1, 1)], None)], vmem=56)
    first_add = named("hist0", passed_along, ahead, "tm", 1)
    run = functools.partial(conv_frames, frames, after(halo, ahead), weight, clip_ids, parts)
    kept = {flip: a_sent[flip] for flip in range(parts) if flip not in far}
    t_sent = named("conv_top", run, 0, 4, later, steps=1, sums=(a_sums,), kept=kept, weigh=20, vmem=56)
    t_got = send_far("t", t_sent)
    run = functools.partial(conv_frames, frames, after(halo, ahead), weight, clip_ids, parts)
    onward, = named("conv_hist1", run, 3, 1, [], [(5, [(0, 0)], None)], weigh=20, vmem=56)
    second_add = named("hist1", passed_along, after(onward, first_add), "tm", 1)
    b_sent = named("conv_b", run, 0, 1, [(0, [(0, 2)], 0)], addends=(after(first_add, a_sums),),
                   weigh=20, vmem=56)
    b_got = send_far("b", b_sent)
    c_sent = named("conv_c", run, 0, 2, [(1, [(0, 1), (1, 2)], 0)], addends=(second_add,),
                   weigh=20, vmem=56)
    c_got = send_far("c", c_sent)
    t_got.update(send_near("t", t_sent, t_got[far[0]]))
    b_got.update(send_near("b", b_sent, c_sent[0]))
    c_got.update(send_near("c", c_sent, c_sent[0]))
    out, _ = named("norm_a", norm_frames, whole(t_sent, t_got), gain, bias, 2, 2, shape, top_first=True,
                   rest=a_got, vmem=20)
    out, _ = named("norm_b", norm_frames, whole(b_sent, b_got), gain, bias, 0, 1, shape, base=out, vmem=20)
    out, _ = named("norm_c", norm_frames, whole(c_sent, c_got), gain, bias, 1, 1, shape, base=out, vmem=20)
    return out.reshape(count, parts * steps, shape[3], co)


def solution(mesh):
    in_specs = (P("tm", "rows", None, None), P(), P(), P(), P())
    out_specs = P("tm", None, "rows", None)
    return jax.shard_map(
        on_device, mesh=mesh, in_specs=in_specs, out_specs=out_specs, check_vma=False
    )
```

```python
import functools

import jax
import jax.numpy as jnp
from jax import lax
from jax.experimental import pallas as pl
from jax.experimental.pallas import tpu as pltpu
from jax.sharding import PartitionSpec as P

GROUPS = 32
EPS = 1e-05
STAT_ROWS = 16


def passed_along(array, axis, by):
    length = lax.axis_size(axis)
    pairs = [(i, i + by) for i in range(length) if 0 <= i + by < length]
    return lax.ppermute(array, axis, pairs)


def exchanged(array, axis, flip):
    length = lax.axis_size(axis)
    return lax.ppermute(array, axis, [(i, i ^ flip) for i in range(length)])


def after(array, *earlier):
    return lax.optimization_barrier((array, *earlier))[0]


def rounded_up(rows):
    return -(-rows // 16) * 16


def split_columns(row_ref, slab_ref):
    width, ci = row_ref.shape
    half = width // 2
    slab_ref[:, 0:ci] = row_ref[pl.ds(0, half, stride=2), :]
    slab_ref[:, ci:] = row_ref[pl.ds(1, half, stride=2), :]


def split_three(total):
    high = total.astype(jnp.bfloat16).astype(jnp.float32)
    rest = total - high
    middle = rest.astype(jnp.bfloat16).astype(jnp.float32)
    return [high, middle, rest - middle]


def conv_kernel(plan, clip_ref, *refs):
    jobs, plains, parts, part_rows, part_width = (
        plan["jobs"], plan["plains"], plan["parts"], plan["part_rows"], plan["part_width"])
    layout, steps, sources, taps = plan["layout"], plan["steps"], plan["sources"], plan["taps"]

    def take(number):
        nonlocal refs
        some, refs = refs[:number], refs[number:]
        return some

    x_refs, above_refs, w_refs = take(sources), take(sources), take(len(taps))
    add_refs = take(plan["addends"])
    sums_refs = take(plan["sums_in"])
    take(plan["kept"])
    out_refs = take(parts)
    plain_refs = take(len(plains))
    sums_out = take(1 if plan["sums_out"] else 0)
    works = jobs + plains
    slab_refs, main_refs, left_refs = take(sources), take(len(works)), take(len(works))
    part_ref, stat_ref, closing_ref, part_sem, tail_sem = refs
    step = pl.program_id(0)
    ci = plan["ci"]
    half, co = plan["half"], plan["co"]
    above = lax.rem(step + 1, 2)
    below = lax.rem(step, 2)
    start = lax.axis_index("tm") * plan["count"]
    last = clip_ref.shape[0] - 1

    @pl.when(step == 0)
    def _():
        for source in range(sources):
            split_columns(above_refs[source].at[0, 0], slab_refs[source].at[1])
        for left_ref in left_refs:
            left_ref[0:8] = jnp.zeros((8, co), jnp.float32)
        stat_ref[...] = jnp.zeros_like(stat_ref)

    def piece_copies(at, slot, step):
        mine = lax.axis_index("rows")
        place = (at * steps + step) * part_rows
        return [
            pltpu.make_async_copy(
                part_ref.at[slot, at, mine ^ flip],
                out.at[pl.ds(pl.multiple_of(layout[flip][1] + place, 16), part_rows)],
                part_sem.at[slot, at, flip])
            for flip, out in enumerate(out_refs)
        ]

    def products(source, tap):
        slab_ref, w_ref = slab_refs[source], w_refs[taps.index(tap)]
        rows = [slab_ref[above], slab_ref[2], slab_ref[below]]
        main = jnp.dot(
            jnp.concatenate(rows, axis=1),
            jnp.concatenate([w_ref[0, (3 * a + 1) * ci : (3 * a + 3) * ci] for a in range(3)], axis=0),
            preferred_element_type=jnp.float32)
        left = jnp.dot(
            jnp.concatenate([row[:, ci:] for row in rows], axis=1),
            jnp.concatenate([w_ref[0, 3 * a * ci : (3 * a + 1) * ci] for a in range(3)], axis=0),
            preferred_element_type=jnp.float32)
        return main, left

    empty = [True] * len(works)
    for source in range(sources):
        split_columns(x_refs[source].at[0, 0], slab_refs[source].at[2])
        split_columns(x_refs[source].at[0, 1], slab_refs[source].at[below])
        frame = plan["first"] + source
        for at, (target, pairs, _) in enumerate(works):
            for tap in [tap for other, tap in pairs if other == source]:
                main, left = products(source, tap)
                if frame != target:
                    same = clip_ref[start + frame] == clip_ref[jnp.minimum(start + target, last)]
                    same = same.astype(jnp.float32)
                    main, left = main * same, left * same
                if empty[at]:
                    main_refs[at][...] = main
                    left_refs[at][8:] = left
                else:
                    main_refs[at][...] += main
                    left_refs[at][8:] += left
                empty[at] = False

    for at, (_, pairs, added) in enumerate(works):
        total = main_refs[at][...] + left_refs[at][7 : 7 + half] if pairs else 0.0
        for addend in added:
            total = total + add_refs[addend][0].astype(jnp.float32)
        if at >= len(jobs):
            plain_refs[at - len(jobs)][0] = total.astype(plain_refs[0].dtype)
            continue
        rounded = total.astype(jnp.bfloat16).astype(jnp.float32)
        tiles = rounded.reshape(half // 8, 8, co)
        stat_ref[2 * at] += jnp.sum(tiles, axis=0)
        stat_ref[2 * at + 1] += jnp.sum(tiles * tiles, axis=0)
        slot = lax.rem(step, 2)

        @pl.when(step >= 2)
        def _(at=at, slot=slot):
            for copy in piece_copies(at, slot, step):
                copy.wait()

        for part in range(parts):
            piece = rounded[part * part_width : (part + 1) * part_width]
            part_ref[slot, at, part, 0:part_width] = piece.astype(jnp.bfloat16)
        for copy in piece_copies(at, slot, step):
            copy.start()

    if not jobs:
        return

    @pl.when(step == steps - 1)
    def _():
        closing = []
        if sums_out:
            sums_out[0][...] = stat_ref[...]
        else:
            rows = []
            for at in range(2 * len(jobs)):
                total = stat_ref[at]
                for ref in sums_refs:
                    total = total + ref[at]
                rows += split_three(jnp.sum(total, axis=0, keepdims=True))
            blank = jnp.zeros((STAT_ROWS - len(rows), co), jnp.float32)
            closing_ref[...] = jnp.concatenate(rows + [blank], axis=0).astype(jnp.bfloat16)
            closing = [
                pltpu.make_async_copy(
                    closing_ref, out.at[layout[flip][0] : layout[flip][0] + STAT_ROWS], tail_sem.at[flip])
                for flip, out in enumerate(out_refs)
            ]
        for copy in closing:
            copy.start()
        for at in range(len(jobs)):
            for back in range(min(steps, 2)):
                for copy in piece_copies(at, lax.rem(step - back, 2), step - back):
                    copy.wait()
        for copy in closing:
            copy.wait()


def conv_frames(frames, halo, weight, clip_ids, parts, first, sources, jobs, plains=(), row=0,
                steps=None, addends=(), sums=(), sums_out=False, layout=None, kept=None, exact=False,
                weigh=1, vmem=56):
    _, band, width, ci = frames.shape
    co = weight.shape[2]
    half = width // 2
    steps = steps or band // 2
    part_width = half // parts
    part_rows = rounded_up(part_width)
    works = list(jobs) + list(plains)
    kept = kept or {}
    messages = parts if jobs else 0
    taps = sorted({tap for _, pairs, _ in works for _, tap in pairs})
    plan = dict(jobs=list(jobs), plains=list(plains), addends=len(addends), parts=messages,
                part_rows=part_rows, layout=layout, part_width=part_width, first=first,
                steps=steps, kept=len(kept), sums_in=len(sums), sums_out=sums_out, sources=sources, taps=taps,
                count=frames.shape[0],
                half=half, co=co, ci=ci)
    above, above_row = (frames, 2 * row - 1) if row else (halo, 0)
    plain_spec = pl.BlockSpec((1, None, half, co), lambda i, *_: (0, row + i, 0, 0))
    frame_spec = lambda source: pl.BlockSpec((1, 2, width, ci), lambda i, *_: (source, row + i, 0, 0))
    above_spec = lambda source: pl.BlockSpec((1, 1, width, ci), lambda i, *_: (source, above_row, 0, 0))
    tap_spec = lambda tap: pl.BlockSpec((1, 9 * ci, co), lambda i, *_: (tap, 0, 0))
    in_specs = [frame_spec(first + source) for source in range(sources)]
    in_specs += [above_spec(first + source) for source in range(sources)]
    in_specs += [tap_spec(tap) for tap in taps]
    in_specs += [plain_spec for _ in addends]
    in_specs += [pl.BlockSpec(a.shape, lambda i, *_: (0, 0, 0)) for a in sums]
    in_specs += [pl.BlockSpec(memory_space=pl.ANY) for _ in kept]
    operands = [clip_ids, *[frames] * sources, *[above] * sources, *[weight] * len(taps),
                *addends, *sums, *kept.values()]
    aliases = {len(operands) - len(kept) + at: flip for at, flip in enumerate(kept)}
    out_shape = [jax.ShapeDtypeStruct((layout[flip][2], co), jnp.bfloat16) for flip in range(messages)]
    out_specs = [pl.BlockSpec(memory_space=pl.ANY) for _ in range(messages)]
    plain_type = jnp.float32 if exact else jnp.bfloat16
    out_shape += [jax.ShapeDtypeStruct((1, band // 2, half, co), plain_type) for _ in plains]
    out_specs += [plain_spec for _ in plains]
    if sums_out:
        shape = (2 * len(jobs), 8, co)
        out_shape.append(jax.ShapeDtypeStruct(shape, jnp.float32))
        out_specs.append(pl.BlockSpec(shape, lambda i, *_: (0, 0, 0)))
    products = sum(len(pairs) for _, pairs, _ in works)
    return pl.pallas_call(
        functools.partial(conv_kernel, plan),
        out_shape=out_shape,
        grid_spec=pltpu.PrefetchScalarGridSpec(
            num_scalar_prefetch=1,
            grid=(steps,),
            in_specs=in_specs,
            out_specs=out_specs,
            scratch_shapes=[
                *[pltpu.VMEM((3, half, 2 * ci), jnp.bfloat16) for _ in range(sources)],
                *[pltpu.VMEM((half, co), jnp.float32) for _ in works],
                *[pltpu.VMEM((8 + half, co), jnp.float32) for _ in works],
                pltpu.VMEM((2, max(len(jobs), 1), parts, part_rows, co), jnp.bfloat16),
                pltpu.VMEM((2 * max(len(jobs), 1), 8, co), jnp.float32),
                pltpu.VMEM((STAT_ROWS, co), jnp.bfloat16),
                pltpu.SemaphoreType.DMA((2, max(len(jobs), 1), parts)),
                pltpu.SemaphoreType.DMA((parts,)),
            ],
        ),
        input_output_aliases=aliases,
        cost_estimate=pl.CostEstimate(
            flops=2 * weigh * products * steps * half * 9 * ci * co,
            bytes_accessed=weigh * (4 * sources * steps * width * ci + 2 * len(works) * steps * half * co),
            transcendentals=0,
        ),
        compiler_params=pltpu.CompilerParams(vmem_limit_bytes=vmem * 1024 * 1024),
    )(*operands)


def norm_kernel(plan, *refs):
    parts, jobs, steps, rows = plan["parts"], plan["jobs"], plan["steps"], plan["rows"]
    part_rows, apart, bases = plan["part_rows"], plan["apart"], plan["bases"]
    data_refs, rest_refs = refs[:parts], refs[parts : parts + len(apart)]
    gain_ref, bias_ref = refs[parts + len(apart) : parts + len(apart) + 2]
    out_ref, done_ref, scale_ref = refs[-3:]
    frame, step = pl.program_id(0), pl.program_id(1)
    part_width, co = out_ref.shape[-2:]

    @pl.when((frame == 0) & (step == 0))
    def _():
        scale_ref[...] = jnp.zeros_like(scale_ref)
        total = 0.0
        for flip, base in enumerate(bases):
            total = total + data_refs[flip][base : base + STAT_ROWS].astype(jnp.float32)
        size = co // GROUPS
        same = (lax.broadcasted_iota(jnp.int32, (co, co), 0) // size
                == lax.broadcasted_iota(jnp.int32, (co, co), 1) // size).astype(jnp.float32)
        grouped = jnp.dot(total, same, precision=lax.Precision.HIGHEST,
                          preferred_element_type=jnp.float32)
        for at in range(jobs):
            def taken(which):
                base = 6 * at + 3 * which
                return grouped[base : base + 1] + grouped[base + 1 : base + 2] + grouped[base + 2 : base + 3]
            mean = taken(0) / plan["entries"]
            variance = taken(1) / plan["entries"] - mean * mean
            scale_ref[at, 0:1] = mean
            scale_ref[at, 1:2] = lax.rsqrt(variance + EPS) * gain_ref[...]

    done_ref[...] = scale_ref[0]
    mean = scale_ref[frame, 0:1]
    scale = scale_ref[frame, 1:2]
    bias = bias_ref[...]
    mine = lax.axis_index("rows")
    top_rows = STAT_ROWS + jobs * part_rows

    def write(flip, at, ref, offset):
        values = ref[pl.ds(pl.multiple_of(offset, 16), part_rows)][0:part_width].astype(jnp.float32)
        value = 0.5 * ((values - mean) * scale + bias)
        out_ref[0, mine ^ flip, at] = (value + value * jnp.tanh(value)).astype(jnp.bfloat16)

    for at in range(rows):
        row = step * rows + at
        for flip in range(parts):
            if not plan["top_first"]:
                write(flip, at, data_refs[flip], bases[flip] + STAT_ROWS + (frame * steps + row) * part_rows)
                continue
            rest, base = data_refs[flip], top_rows
            if flip in apart:
                rest, base = rest_refs[apart.index(flip)], 0
            below = base + (frame * (steps - 1) + row - 1) * part_rows
            if at > 0:
                write(flip, at, rest, below)
                continue

            @pl.when(row == 0)
            def _(flip=flip):
                write(flip, 0, data_refs[flip], STAT_ROWS + frame * part_rows)

            @pl.when(row > 0)
            def _(flip=flip, rest=rest, below=below):
                write(flip, 0, rest, below)


def norm_frames(messages, gain, bias, first, jobs, shape, top_first=False, rest=None, bases=None,
                base=None, vmem=20):
    frames, parts, steps, part_width, co = shape
    rows = 2 if steps % 2 == 0 else 1
    rest = rest or {}
    plan = dict(parts=parts, jobs=jobs, steps=steps, rows=rows, apart=list(rest),
                bases=bases or [0] * parts,
                part_rows=rounded_up(part_width), top_first=top_first,
                entries=float(parts * steps * part_width * parts * (co // GROUPS)))
    in_specs = (
        [pl.BlockSpec(message.shape, lambda f, i, *_: (0, 0)) for message in [*messages, *rest.values()]]
        + [pl.BlockSpec((1, co), lambda f, i, *_: (0, 0))] * 2
    )
    operands = [*messages, *rest.values(), gain, bias]
    aliases = {}
    if base is not None:
        in_specs.append(pl.BlockSpec(memory_space=pl.ANY))
        aliases = {len(operands): 0}
        operands.append(base)
    return pl.pallas_call(
        functools.partial(norm_kernel, plan),
        out_shape=[jax.ShapeDtypeStruct(shape, jnp.bfloat16), jax.ShapeDtypeStruct((8, co), jnp.float32)],
        grid_spec=pltpu.PrefetchScalarGridSpec(
            num_scalar_prefetch=0,
            grid=(jobs, steps // rows),
            in_specs=in_specs,
            out_specs=[
                pl.BlockSpec((1, parts, rows, part_width, co), lambda f, i, *_: (first + f, 0, i, 0, 0)),
                pl.BlockSpec((8, co), lambda f, i, *_: (0, 0)),
            ],
            scratch_shapes=[pltpu.VMEM((jobs, 8, co), jnp.float32)],
        ),
        input_output_aliases=aliases,
        cost_estimate=pl.CostEstimate(
            flops=8 * jobs * parts * steps * part_width * co,
            bytes_accessed=4 * jobs * parts * steps * part_width * co,
            transcendentals=jobs * parts * steps * part_width * co,
        ),
        compiler_params=pltpu.CompilerParams(vmem_limit_bytes=vmem * 1024 * 1024),
    )(*operands)


def on_device(frames, clip_ids, conv_weight, norm_gain, norm_bias):
    count, band, width, ci = frames.shape
    co = conv_weight.shape[4]
    parts = lax.axis_size("rows")
    weight = conv_weight.reshape(3, 9 * ci, co)
    gain, bias = norm_gain.reshape(1, co), norm_bias.reshape(1, co)
    steps = band // 2
    shape = (count, parts, steps, width // 2 // parts, co)
    part_rows = rounded_up(shape[3])
    top_rows = STAT_ROWS + 2 * part_rows
    all_rows = top_rows + 2 * (steps - 1) * part_rows
    one_rows = STAT_ROWS + steps * part_rows

    def named(name, function, *args, **keywords):
        with jax.named_scope(name):
            return function(*args, **keywords)

    def whole(sent, got):
        return [sent[0]] + [got[flip] for flip in range(1, parts)]

    near = [flip for flip in range(1, parts) if 2 * flip < parts]
    far = [flip for flip in range(parts - 1, 0, -1) if 2 * flip >= parts]
    chain = []

    def send_far(name, sent):
        got = {}
        for flip in far:
            before = chain[-4:][:1] if len(chain) >= 4 else []
            got[flip] = named(f"{name}{flip}", exchanged, after(sent[flip], *before), "rows", flip)
            chain.append(got[flip])
        return got

    def send_near(name, sent, single, *earlier):
        got = {}
        for flip in near:
            got[flip] = named(f"{name}{flip}", exchanged, after(sent[flip], *earlier), "rows", flip)
            if single:
                earlier = (got[flip],)
        return got

    def layout(far_one, near_one):
        return [far_one if flip in far else near_one for flip in range(parts)]

    halo = named("halo", passed_along, frames[:, -1:], "rows", 1)
    run = functools.partial(conv_frames, frames, halo, weight, clip_ids, parts)
    later = [(2, [(0, 0), (1, 1), (2, 2)], ()), (3, [(1, 0), (2, 1), (3, 2)], ())]
    near_rows = all_rows + one_rows
    *a_sent, a_sums = named(
        "conv_a", run, 0, 4, later, row=1, steps=steps - 1, sums_out=True, vmem=56,
        layout=layout((0, 0, all_rows - top_rows), (0, top_rows, near_rows)))
    a_got = send_far("a", a_sent)
    run = functools.partial(conv_frames, frames, after(halo, a_sums), weight, clip_ids, parts)
    ahead, = named("conv_hist0", run, 2, 2, [], [(4, [(0, 0), (1, 1)], ())], vmem=56)
    first_add = named("hist0", passed_along, ahead, "tm", 1)
    run = functools.partial(conv_frames, frames, after(halo, ahead), weight, clip_ids, parts)
    own = named("conv_own", run, 0, 2, [], [(0, [(0, 2)], ()), (1, [(0, 1), (1, 2)], ())],
                exact=True, weigh=20, vmem=56)
    run = functools.partial(conv_frames, frames, after(halo, ahead, *own), weight, clip_ids, parts)
    kept = {flip: a_sent[flip] for flip in range(parts) if flip not in far}
    t_sent = named(
        "conv_top", run, 0, 4, later, steps=1, sums=(a_sums,), kept=kept, weigh=20, vmem=56,
        layout=layout((0, STAT_ROWS, top_rows), (0, STAT_ROWS, near_rows)))
    t_got = send_far("t", t_sent)
    run = functools.partial(conv_frames, frames, after(halo, t_sent[0]), weight, clip_ids, parts)
    onward, = named("conv_hist1", run, 3, 1, [], [(5, [(0, 0)], ())], weigh=20, vmem=56)
    second_add = named("hist1", passed_along, after(onward, first_add, *a_got.values()), "tm", 1)
    kept = {flip: t_sent[flip] for flip in range(parts) if flip not in far}
    b_sent = named(
        "add_b", run, 0, 0, [(0, [], (0, 1))], addends=(own[0], after(first_add, a_sums)), kept=kept,
        weigh=20, vmem=56,
        layout=layout((0, STAT_ROWS, one_rows), (all_rows, all_rows + STAT_ROWS, near_rows)))
    b_got = send_far("b", b_sent)
    b_got.update(send_near("tb", b_sent, False, b_sent[0]))
    c_sent = named(
        "add_c", run, 0, 0, [(1, [], (0, 1))], addends=(own[1], after(second_add, a_sums)),
        weigh=20, vmem=56, layout=[(0, STAT_ROWS, one_rows)] * parts)
    c_got = send_far("c", c_sent)
    c_got.update(send_near("c", c_sent, False))
    both = whole(b_sent, b_got)
    tops = [t_got[flip] if flip in far else both[flip] for flip in range(parts)]
    out, _ = named("norm_a", norm_frames, tops, gain, bias, 2, 2, shape, top_first=True, rest=a_got, vmem=20)
    out, _ = named("norm_b", norm_frames, both, gain, bias, 0, 1, shape, base=out, vmem=20,
                   bases=layout(0, all_rows))
    out, _ = named("norm_c", norm_frames, whole(c_sent, c_got), gain, bias, 1, 1, shape, base=out, vmem=20)
    return out.reshape(count, parts * steps, shape[3], co)


def solution(mesh):
    in_specs = (P("tm", "rows", None, None), P(), P(), P(), P())
    out_specs = P("tm", None, "rows", None)
    return jax.shard_map(
        on_device, mesh=mesh, in_specs=in_specs, out_specs=out_specs, check_vma=False
    )
```

```python
import functools

import jax
import jax.numpy as jnp
from jax import lax
from jax.experimental import pallas as pl
from jax.experimental.pallas import tpu as pltpu
from jax.sharding import PartitionSpec as P

GROUPS = 32
EPS = 1e-05
STAT_ROWS = 16


def passed_along(array, axis, by):
    length = lax.axis_size(axis)
    pairs = [(i, i + by) for i in range(length) if 0 <= i + by < length]
    return lax.ppermute(array, axis, pairs)


def exchanged(array, axis, flip):
    length = lax.axis_size(axis)
    return lax.ppermute(array, axis, [(i, i ^ flip) for i in range(length)])


def after(array, *earlier):
    return lax.optimization_barrier((array, *earlier))[0]


def rounded_up(rows):
    return -(-rows // 16) * 16


def split_columns(row_ref, slab_ref):
    width, ci = row_ref.shape
    half = width // 2
    slab_ref[:, 0:ci] = row_ref[pl.ds(0, half, stride=2), :]
    slab_ref[:, ci:] = row_ref[pl.ds(1, half, stride=2), :]


def split_three(total):
    high = total.astype(jnp.bfloat16).astype(jnp.float32)
    rest = total - high
    middle = rest.astype(jnp.bfloat16).astype(jnp.float32)
    return [high, middle, rest - middle]


def conv_kernel(plan, clip_ref, *refs):
    jobs, plains, parts, part_rows, part_width = (
        plan["jobs"], plan["plains"], plan["parts"], plan["part_rows"], plan["part_width"])
    layout, steps, sources, taps = plan["layout"], plan["steps"], plan["sources"], plan["taps"]

    def take(number):
        nonlocal refs
        some, refs = refs[:number], refs[number:]
        return some

    x_refs, above_refs, w_refs = take(sources), take(sources), take(len(taps))
    add_refs = take(plan["addends"])
    sums_refs = take(plan["sums_in"])
    take(plan["kept"])
    out_refs = take(parts)
    plain_refs = take(len(plains))
    sums_out = take(1 if plan["sums_out"] else 0)
    works = jobs + plains
    slab_refs, main_refs, left_refs = take(sources), take(len(works)), take(len(works))
    part_ref, stat_ref, closing_ref, part_sem, tail_sem = refs
    step = pl.program_id(0)
    ci = plan["ci"]
    half, co = plan["half"], plan["co"]
    above = lax.rem(step + 1, 2)
    below = lax.rem(step, 2)
    start = lax.axis_index("tm") * plan["count"]
    last = clip_ref.shape[0] - 1

    @pl.when(step == 0)
    def _():
        for source in range(sources):
            split_columns(above_refs[source].at[0, 0], slab_refs[source].at[1])
        for left_ref in left_refs:
            left_ref[0:8] = jnp.zeros((8, co), jnp.float32)
        stat_ref[...] = jnp.zeros_like(stat_ref)

    def piece_copies(at, slot, step):
        mine = lax.axis_index("rows")
        place = (at * steps + step) * part_rows
        return [
            pltpu.make_async_copy(
                part_ref.at[slot, at, mine ^ flip],
                out.at[pl.ds(pl.multiple_of(layout[flip][1] + place, 16), part_rows)],
                part_sem.at[slot, at, flip])
            for flip, out in enumerate(out_refs)
        ]

    def products(source, tap):
        slab_ref, w_ref = slab_refs[source], w_refs[taps.index(tap)]
        rows = [slab_ref[above], slab_ref[2], slab_ref[below]]
        main = jnp.dot(
            jnp.concatenate(rows, axis=1),
            jnp.concatenate([w_ref[0, (3 * a + 1) * ci : (3 * a + 3) * ci] for a in range(3)], axis=0),
            preferred_element_type=jnp.float32)
        left = jnp.dot(
            jnp.concatenate([row[:, ci:] for row in rows], axis=1),
            jnp.concatenate([w_ref[0, 3 * a * ci : (3 * a + 1) * ci] for a in range(3)], axis=0),
            preferred_element_type=jnp.float32)
        return main, left

    empty = [True] * len(works)
    for source in range(sources):
        split_columns(x_refs[source].at[0, 0], slab_refs[source].at[2])
        split_columns(x_refs[source].at[0, 1], slab_refs[source].at[below])
        frame = plan["first"] + source
        for at, (target, pairs, _) in enumerate(works):
            for tap in [tap for other, tap in pairs if other == source]:
                main, left = products(source, tap)
                if frame != target:
                    same = clip_ref[start + frame] == clip_ref[jnp.minimum(start + target, last)]
                    same = same.astype(jnp.float32)
                    main, left = main * same, left * same
                if empty[at]:
                    main_refs[at][...] = main
                    left_refs[at][8:] = left
                else:
                    main_refs[at][...] += main
                    left_refs[at][8:] += left
                empty[at] = False

    for at, (_, pairs, added) in enumerate(works):
        total = main_refs[at][...] + left_refs[at][7 : 7 + half] if pairs else 0.0
        for addend in added:
            total = total + add_refs[addend][0].astype(jnp.float32)
        if at >= len(jobs):
            plain_refs[at - len(jobs)][0] = total.astype(plain_refs[0].dtype)
            continue
        rounded = total.astype(jnp.bfloat16).astype(jnp.float32)
        tiles = rounded.reshape(half // 8, 8, co)
        stat_ref[2 * at] += jnp.sum(tiles, axis=0)
        stat_ref[2 * at + 1] += jnp.sum(tiles * tiles, axis=0)
        slot = lax.rem(step, 2)

        @pl.when(step >= 2)
        def _(at=at, slot=slot):
            for copy in piece_copies(at, slot, step):
                copy.wait()

        for part in range(parts):
            piece = rounded[part * part_width : (part + 1) * part_width]
            part_ref[slot, at, part, 0:part_width] = piece.astype(jnp.bfloat16)
        for copy in piece_copies(at, slot, step):
            copy.start()

    if not jobs:
        return

    @pl.when(step == steps - 1)
    def _():
        closing = []
        if sums_out:
            sums_out[0][...] = stat_ref[...]
        else:
            rows = []
            for at in range(2 * len(jobs)):
                total = stat_ref[at]
                for ref in sums_refs:
                    total = total + ref[at]
                rows += split_three(jnp.sum(total, axis=0, keepdims=True))
            blank = jnp.zeros((STAT_ROWS - len(rows), co), jnp.float32)
            closing_ref[...] = jnp.concatenate(rows + [blank], axis=0).astype(jnp.bfloat16)
            closing = [
                pltpu.make_async_copy(
                    closing_ref, out.at[layout[flip][0] : layout[flip][0] + STAT_ROWS], tail_sem.at[flip])
                for flip, out in enumerate(out_refs)
            ]
        for copy in closing:
            copy.start()
        for at in range(len(jobs)):
            for back in range(min(steps, 2)):
                for copy in piece_copies(at, lax.rem(step - back, 2), step - back):
                    copy.wait()
        for copy in closing:
            copy.wait()


def conv_frames(frames, halo, weight, clip_ids, parts, first, sources, jobs, plains=(), row=0,
                steps=None, addends=(), sums=(), sums_out=False, layout=None, kept=None, exact=False,
                weigh=1, vmem=56):
    _, band, width, ci = frames.shape
    co = weight.shape[2]
    half = width // 2
    steps = steps or band // 2
    part_width = half // parts
    part_rows = rounded_up(part_width)
    works = list(jobs) + list(plains)
    kept = kept or {}
    messages = parts if jobs else 0
    taps = sorted({tap for _, pairs, _ in works for _, tap in pairs})
    plan = dict(jobs=list(jobs), plains=list(plains), addends=len(addends), parts=messages,
                part_rows=part_rows, layout=layout, part_width=part_width, first=first,
                steps=steps, kept=len(kept), sums_in=len(sums), sums_out=sums_out, sources=sources, taps=taps,
                count=frames.shape[0],
                half=half, co=co, ci=ci)
    above, above_row = (frames, 2 * row - 1) if row else (halo, 0)
    plain_spec = pl.BlockSpec((1, None, half, co), lambda i, *_: (0, row + i, 0, 0))
    frame_spec = lambda source: pl.BlockSpec((1, 2, width, ci), lambda i, *_: (source, row + i, 0, 0))
    above_spec = lambda source: pl.BlockSpec((1, 1, width, ci), lambda i, *_: (source, above_row, 0, 0))
    tap_spec = lambda tap: pl.BlockSpec((1, 9 * ci, co), lambda i, *_: (tap, 0, 0))
    in_specs = [frame_spec(first + source) for source in range(sources)]
    in_specs += [above_spec(first + source) for source in range(sources)]
    in_specs += [tap_spec(tap) for tap in taps]
    in_specs += [plain_spec for _ in addends]
    in_specs += [pl.BlockSpec(a.shape, lambda i, *_: (0, 0, 0)) for a in sums]
    in_specs += [pl.BlockSpec(memory_space=pl.ANY) for _ in kept]
    operands = [clip_ids, *[frames] * sources, *[above] * sources, *[weight] * len(taps),
                *addends, *sums, *kept.values()]
    aliases = {len(operands) - len(kept) + at: flip for at, flip in enumerate(kept)}
    out_shape = [jax.ShapeDtypeStruct((layout[flip][2], co), jnp.bfloat16) for flip in range(messages)]
    out_specs = [pl.BlockSpec(memory_space=pl.ANY) for _ in range(messages)]
    plain_type = jnp.float32 if exact else jnp.bfloat16
    out_shape += [jax.ShapeDtypeStruct((1, band // 2, half, co), plain_type) for _ in plains]
    out_specs += [plain_spec for _ in plains]
    if sums_out:
        shape = (2 * len(jobs), 8, co)
        out_shape.append(jax.ShapeDtypeStruct(shape, jnp.float32))
        out_specs.append(pl.BlockSpec(shape, lambda i, *_: (0, 0, 0)))
    products = sum(len(pairs) for _, pairs, _ in works)
    return pl.pallas_call(
        functools.partial(conv_kernel, plan),
        out_shape=out_shape,
        grid_spec=pltpu.PrefetchScalarGridSpec(
            num_scalar_prefetch=1,
            grid=(steps,),
            in_specs=in_specs,
            out_specs=out_specs,
            scratch_shapes=[
                *[pltpu.VMEM((3, half, 2 * ci), jnp.bfloat16) for _ in range(sources)],
                *[pltpu.VMEM((half, co), jnp.float32) for _ in works],
                *[pltpu.VMEM((8 + half, co), jnp.float32) for _ in works],
                pltpu.VMEM((2, max(len(jobs), 1), parts, part_rows, co), jnp.bfloat16),
                pltpu.VMEM((2 * max(len(jobs), 1), 8, co), jnp.float32),
                pltpu.VMEM((STAT_ROWS, co), jnp.bfloat16),
                pltpu.SemaphoreType.DMA((2, max(len(jobs), 1), parts)),
                pltpu.SemaphoreType.DMA((parts,)),
            ],
        ),
        input_output_aliases=aliases,
        cost_estimate=pl.CostEstimate(
            flops=2 * weigh * products * steps * half * 9 * ci * co,
            bytes_accessed=weigh * (4 * sources * steps * width * ci + 2 * len(works) * steps * half * co),
            transcendentals=0,
        ),
        compiler_params=pltpu.CompilerParams(vmem_limit_bytes=vmem * 1024 * 1024),
    )(*operands)


def norm_kernel(plan, *refs):
    parts, jobs, steps, rows = plan["parts"], plan["jobs"], plan["steps"], plan["rows"]
    part_rows, apart, bases = plan["part_rows"], plan["apart"], plan["bases"]
    data_refs, rest_refs = refs[:parts], refs[parts : parts + len(apart)]
    gain_ref, bias_ref = refs[parts + len(apart) : parts + len(apart) + 2]
    out_ref, done_ref, scale_ref = refs[-3:]
    frame, step = pl.program_id(0), pl.program_id(1)
    part_width, co = out_ref.shape[-2:]

    @pl.when((frame == 0) & (step == 0))
    def _():
        scale_ref[...] = jnp.zeros_like(scale_ref)
        total = 0.0
        for flip, base in enumerate(bases):
            total = total + data_refs[flip][base : base + STAT_ROWS].astype(jnp.float32)
        size = co // GROUPS
        same = (lax.broadcasted_iota(jnp.int32, (co, co), 0) // size
                == lax.broadcasted_iota(jnp.int32, (co, co), 1) // size).astype(jnp.float32)
        grouped = jnp.dot(total, same, precision=lax.Precision.HIGHEST,
                          preferred_element_type=jnp.float32)
        for at in range(jobs):
            def taken(which):
                base = 6 * at + 3 * which
                return grouped[base : base + 1] + grouped[base + 1 : base + 2] + grouped[base + 2 : base + 3]
            mean = taken(0) / plan["entries"]
            variance = taken(1) / plan["entries"] - mean * mean
            scale_ref[at, 0:1] = mean
            scale_ref[at, 1:2] = lax.rsqrt(variance + EPS) * gain_ref[...]

    done_ref[...] = scale_ref[0]
    mean = scale_ref[frame, 0:1]
    scale = scale_ref[frame, 1:2]
    bias = bias_ref[...]
    mine = lax.axis_index("rows")
    top_rows = STAT_ROWS + jobs * part_rows

    def write(flip, at, ref, offset):
        values = ref[pl.ds(pl.multiple_of(offset, 16), part_rows)][0:part_width].astype(jnp.float32)
        value = 0.5 * ((values - mean) * scale + bias)
        out_ref[0, mine ^ flip, at] = (value + value * jnp.tanh(value)).astype(jnp.bfloat16)

    for at in range(rows):
        row = step * rows + at
        for flip in range(parts):
            if not plan["top_first"]:
                write(flip, at, data_refs[flip], bases[flip] + STAT_ROWS + (frame * steps + row) * part_rows)
                continue
            rest, base = data_refs[flip], top_rows
            if flip in apart:
                rest, base = rest_refs[apart.index(flip)], 0
            below = base + (frame * (steps - 1) + row - 1) * part_rows
            if at > 0:
                write(flip, at, rest, below)
                continue

            @pl.when(row == 0)
            def _(flip=flip):
                write(flip, 0, data_refs[flip], STAT_ROWS + frame * part_rows)

            @pl.when(row > 0)
            def _(flip=flip, rest=rest, below=below):
                write(flip, 0, rest, below)


def norm_frames(messages, gain, bias, first, jobs, shape, top_first=False, rest=None, bases=None,
                base=None, vmem=20):
    frames, parts, steps, part_width, co = shape
    rows = 2 if steps % 2 == 0 else 1
    rest = rest or {}
    plan = dict(parts=parts, jobs=jobs, steps=steps, rows=rows, apart=list(rest),
                bases=bases or [0] * parts,
                part_rows=rounded_up(part_width), top_first=top_first,
                entries=float(parts * steps * part_width * parts * (co // GROUPS)))
    in_specs = (
        [pl.BlockSpec(message.shape, lambda f, i, *_: (0, 0)) for message in [*messages, *rest.values()]]
        + [pl.BlockSpec((1, co), lambda f, i, *_: (0, 0))] * 2
    )
    operands = [*messages, *rest.values(), gain, bias]
    aliases = {}
    if base is not None:
        in_specs.append(pl.BlockSpec(memory_space=pl.ANY))
        aliases = {len(operands): 0}
        operands.append(base)
    return pl.pallas_call(
        functools.partial(norm_kernel, plan),
        out_shape=[jax.ShapeDtypeStruct(shape, jnp.bfloat16), jax.ShapeDtypeStruct((8, co), jnp.float32)],
        grid_spec=pltpu.PrefetchScalarGridSpec(
            num_scalar_prefetch=0,
            grid=(jobs, steps // rows),
            in_specs=in_specs,
            out_specs=[
                pl.BlockSpec((1, parts, rows, part_width, co), lambda f, i, *_: (first + f, 0, i, 0, 0)),
                pl.BlockSpec((8, co), lambda f, i, *_: (0, 0)),
            ],
            scratch_shapes=[pltpu.VMEM((jobs, 8, co), jnp.float32)],
        ),
        input_output_aliases=aliases,
        cost_estimate=pl.CostEstimate(
            flops=8 * jobs * parts * steps * part_width * co,
            bytes_accessed=4 * jobs * parts * steps * part_width * co,
            transcendentals=jobs * parts * steps * part_width * co,
        ),
        compiler_params=pltpu.CompilerParams(vmem_limit_bytes=vmem * 1024 * 1024),
    )(*operands)


def on_device(frames, clip_ids, conv_weight, norm_gain, norm_bias):
    count, band, width, ci = frames.shape
    co = conv_weight.shape[4]
    parts = lax.axis_size("rows")
    weight = conv_weight.reshape(3, 9 * ci, co)
    gain, bias = norm_gain.reshape(1, co), norm_bias.reshape(1, co)
    steps = band // 2
    shape = (count, parts, steps, width // 2 // parts, co)
    part_rows = rounded_up(shape[3])
    top_rows = STAT_ROWS + 2 * part_rows
    all_rows = top_rows + 2 * (steps - 1) * part_rows
    one_rows = STAT_ROWS + steps * part_rows

    def named(name, function, *args, **keywords):
        with jax.named_scope(name):
            return function(*args, **keywords)

    def whole(sent, got):
        return [sent[0]] + [got[flip] for flip in range(1, parts)]

    near = [flip for flip in range(1, parts) if 2 * flip < parts]
    far = [flip for flip in range(parts - 1, 0, -1) if 2 * flip >= parts]
    chain = []

    def send_far(name, sent):
        got = {}
        for flip in far:
            before = chain[-3:][:1] if len(chain) >= 3 else []
            got[flip] = named(f"{name}{flip}", exchanged, after(sent[flip], *before), "rows", flip)
            chain.append(got[flip])
        return got

    def send_near(name, sent, single, *earlier):
        got = {}
        for flip in near:
            got[flip] = named(f"{name}{flip}", exchanged, after(sent[flip], *earlier), "rows", flip)
            if single:
                earlier = (got[flip],)
        return got

    def layout(far_one, near_one):
        return [far_one if flip in far else near_one for flip in range(parts)]

    halo = named("halo", passed_along, frames[:, -1:], "rows", 1)
    run = functools.partial(conv_frames, frames, halo, weight, clip_ids, parts)
    later = [(2, [(0, 0), (1, 1), (2, 2)], ()), (3, [(1, 0), (2, 1), (3, 2)], ())]
    near_rows = top_rows + one_rows
    *a_sent, a_sums = named(
        "conv_a", run, 0, 4, later, row=1, steps=steps - 1, sums_out=True, vmem=56,
        layout=[(0, 0, all_rows - top_rows)] * parts)
    held = {}
    a_got = {}

    def send_one(got, name, sent, flip, *earlier):
        got[flip] = named(f"{name}{flip}", exchanged, after(sent[flip], *earlier), "rows", flip)

    for flip in far[:3]:
        send_one(a_got, "a", a_sent, flip)
    send_one(a_got, "a", a_sent, near[0])
    run = functools.partial(conv_frames, frames, after(halo, a_sums), weight, clip_ids, parts)
    ahead, = named("conv_hist0", run, 2, 2, [], [(4, [(0, 0), (1, 1)], ())], weigh=1, vmem=56)
    send_one(a_got, "a", a_sent, near[1], ahead, a_got[near[0]])
    first_add = named("hist0", passed_along, ahead, "tm", 1)
    run = functools.partial(conv_frames, frames, after(halo, ahead, a_got[near[0]]), weight, clip_ids, parts)
    own = named("conv_own", run, 0, 2, [], [(0, [(0, 2)], ()), (1, [(0, 1), (1, 2)], ())],
                exact=True, weigh=20, vmem=56)
    for at, flip in enumerate(near[2:]):
        send_one(a_got, "a", a_sent, flip, own[0], a_got[near[at + 1]])
    for at, flip in enumerate(far[3:]):
        send_one(a_got, "a", a_sent, flip, own[0], a_got[far[at]])
    chain += [a_got[flip] for flip in far]
    run = functools.partial(conv_frames, frames, after(halo, *own, a_got[near[1]]), weight, clip_ids, parts)
    t_sent = named(
        "conv_top", run, 0, 4, later, steps=1, sums=(a_sums,), weigh=20, vmem=56,
        layout=layout((0, STAT_ROWS, top_rows), (0, STAT_ROWS, near_rows)))
    t_got = send_far("t", t_sent)
    run = functools.partial(conv_frames, frames, after(halo, t_sent[0], a_got[near[2]]), weight, clip_ids, parts)
    onward, = named("conv_hist1", run, 3, 1, [], [(5, [(0, 0)], ())], weigh=20, vmem=56)
    second_add = named("hist1", passed_along, after(onward, first_add, *[a_got[flip] for flip in far]), "tm", 1)
    kept = {flip: t_sent[flip] for flip in range(parts) if flip not in far}
    b_sent = named(
        "add_b", run, 0, 0, [(0, [], (0, 1))], addends=(own[0], after(first_add, t_got[far[0]], t_got[far[1]], t_got[far[2]])), kept=kept,
        weigh=20, vmem=56,
        layout=layout((0, STAT_ROWS, one_rows), (top_rows, top_rows + STAT_ROWS, near_rows)))
    b_got = send_far("b", b_sent)
    b_got.update(send_near("tb", b_sent, False, t_got[far[-1]]))
    c_sent = named(
        "add_c", run, 0, 0, [(1, [], (0, 1))], addends=(own[1], after(second_add, b_got[near[0]], b_got[near[1]])),
        weigh=20, vmem=56, layout=[(0, STAT_ROWS, one_rows)] * parts)
    c_got = send_far("c", c_sent)
    c_got.update(send_near("c", c_sent, False))
    both = whole(b_sent, b_got)
    tops = [t_got[flip] if flip in far else both[flip] for flip in range(parts)]
    out, _ = named("norm_a", norm_frames, tops, gain, bias, 2, 2, shape, top_first=True, rest=dict(enumerate(whole(a_sent, a_got))), vmem=20)
    out, _ = named("norm_b", norm_frames, both, gain, bias, 0, 1, shape, base=out, vmem=20,
                   bases=layout(0, top_rows))
    out, _ = named("norm_c", norm_frames, whole(c_sent, c_got), gain, bias, 1, 1, shape, base=out, vmem=20)
    return out.reshape(count, parts * steps, shape[3], co)


def solution(mesh):
    in_specs = (P("tm", "rows", None, None), P(), P(), P(), P())
    out_specs = P("tm", None, "rows", None)
    return jax.shard_map(
        on_device, mesh=mesh, in_specs=in_specs, out_specs=out_specs, check_vma=False
    )
```

```python
import functools

import jax
import jax.numpy as jnp
from jax import lax
from jax.experimental import pallas as pl
from jax.experimental.pallas import tpu as pltpu
from jax.sharding import PartitionSpec as P

GROUPS = 32
EPS = 1e-05
STAT_ROWS = 16


def passed_along(array, axis, by):
    length = lax.axis_size(axis)
    pairs = [(i, i + by) for i in range(length) if 0 <= i + by < length]
    return lax.ppermute(array, axis, pairs)


def exchanged(array, axis, flip):
    length = lax.axis_size(axis)
    return lax.ppermute(array, axis, [(i, i ^ flip) for i in range(length)])


def after(array, *earlier):
    return lax.optimization_barrier((array, *earlier))[0]


def rounded_up(rows):
    return -(-rows // 16) * 16


def split_columns(row_ref, slab_ref):
    width, ci = row_ref.shape
    half = width // 2
    slab_ref[:, 0:ci] = row_ref[pl.ds(0, half, stride=2), :]
    slab_ref[:, ci:] = row_ref[pl.ds(1, half, stride=2), :]


def split_three(total):
    high = total.astype(jnp.bfloat16).astype(jnp.float32)
    rest = total - high
    middle = rest.astype(jnp.bfloat16).astype(jnp.float32)
    return [high, middle, rest - middle]


def conv_kernel(plan, clip_ref, *refs):
    jobs, plains, parts, part_rows, part_width = (
        plan["jobs"], plan["plains"], plan["parts"], plan["part_rows"], plan["part_width"])
    layout, steps, sources, taps = plan["layout"], plan["steps"], plan["sources"], plan["taps"]

    def take(number):
        nonlocal refs
        some, refs = refs[:number], refs[number:]
        return some

    x_refs, above_refs, w_refs = take(sources), take(sources), take(len(taps))
    add_refs = take(plan["addends"])
    sums_refs = take(plan["sums_in"])
    take(plan["kept"])
    out_refs = take(parts)
    plain_refs = take(len(plains))
    sums_out = take(1 if plan["sums_out"] else 0)
    works = jobs + plains
    slab_refs, main_refs, left_refs = take(sources), take(len(works)), take(len(works))
    part_ref, stat_ref, closing_ref, part_sem, tail_sem = refs
    step = pl.program_id(0)
    ci = plan["ci"]
    half, co = plan["half"], plan["co"]
    above = lax.rem(step + 1, 2)
    below = lax.rem(step, 2)
    start = lax.axis_index("tm") * plan["count"]
    last = clip_ref.shape[0] - 1

    @pl.when(step == 0)
    def _():
        for source in range(sources):
            split_columns(above_refs[source].at[0, 0], slab_refs[source].at[1])
        for left_ref in left_refs:
            left_ref[0:8] = jnp.zeros((8, co), jnp.float32)
        stat_ref[...] = jnp.zeros_like(stat_ref)

    def piece_copies(at, slot, step):
        mine = lax.axis_index("rows")
        place = (at * steps + step) * part_rows
        return [
            pltpu.make_async_copy(
                part_ref.at[slot, at, mine ^ flip],
                out.at[pl.ds(pl.multiple_of(layout[flip][1] + place, 16), part_rows)],
                part_sem.at[slot, at, flip])
            for flip, out in enumerate(out_refs)
        ]

    def products(source, tap):
        slab_ref, w_ref = slab_refs[source], w_refs[taps.index(tap)]
        rows = [slab_ref[above], slab_ref[2], slab_ref[below]]
        main = jnp.dot(
            jnp.concatenate(rows, axis=1),
            jnp.concatenate([w_ref[0, (3 * a + 1) * ci : (3 * a + 3) * ci] for a in range(3)], axis=0),
            preferred_element_type=jnp.float32)
        left = jnp.dot(
            jnp.concatenate([row[:, ci:] for row in rows], axis=1),
            jnp.concatenate([w_ref[0, 3 * a * ci : (3 * a + 1) * ci] for a in range(3)], axis=0),
            preferred_element_type=jnp.float32)
        return main, left

    empty = [True] * len(works)
    for source in range(sources):
        split_columns(x_refs[source].at[0, 0], slab_refs[source].at[2])
        split_columns(x_refs[source].at[0, 1], slab_refs[source].at[below])
        frame = plan["first"] + source
        for at, (target, pairs, _) in enumerate(works):
            for tap in [tap for other, tap in pairs if other == source]:
                main, left = products(source, tap)
                if frame != target:
                    same = clip_ref[start + frame] == clip_ref[jnp.minimum(start + target, last)]
                    same = same.astype(jnp.float32)
                    main, left = main * same, left * same
                if empty[at]:
                    main_refs[at][...] = main
                    left_refs[at][8:] = left
                else:
                    main_refs[at][...] += main
                    left_refs[at][8:] += left
                empty[at] = False

    for at, (_, pairs, added) in enumerate(works):
        total = main_refs[at][...] + left_refs[at][7 : 7 + half] if pairs else 0.0
        for addend in added:
            total = total + add_refs[addend][0].astype(jnp.float32)
        if at >= len(jobs):
            plain_refs[at - len(jobs)][0] = total.astype(plain_refs[0].dtype)
            continue
        rounded = total.astype(jnp.bfloat16).astype(jnp.float32)
        tiles = rounded.reshape(half // 8, 8, co)
        stat_ref[2 * at] += jnp.sum(tiles, axis=0)
        stat_ref[2 * at + 1] += jnp.sum(tiles * tiles, axis=0)
        slot = lax.rem(step, 2)

        @pl.when(step >= 2)
        def _(at=at, slot=slot):
            for copy in piece_copies(at, slot, step):
                copy.wait()

        for part in range(parts):
            piece = rounded[part * part_width : (part + 1) * part_width]
            part_ref[slot, at, part, 0:part_width] = piece.astype(jnp.bfloat16)
        for copy in piece_copies(at, slot, step):
            copy.start()

    if not jobs:
        return

    @pl.when(step == steps - 1)
    def _():
        closing = []
        if sums_out:
            sums_out[0][...] = stat_ref[...]
        else:
            rows = []
            for at in range(2 * len(jobs)):
                total = stat_ref[at]
                for ref in sums_refs:
                    total = total + ref[at]
                rows += split_three(jnp.sum(total, axis=0, keepdims=True))
            blank = jnp.zeros((STAT_ROWS - len(rows), co), jnp.float32)
            closing_ref[...] = jnp.concatenate(rows + [blank], axis=0).astype(jnp.bfloat16)
            closing = [
                pltpu.make_async_copy(
                    closing_ref, out.at[layout[flip][0] : layout[flip][0] + STAT_ROWS], tail_sem.at[flip])
                for flip, out in enumerate(out_refs)
            ]
        for copy in closing:
            copy.start()
        for at in range(len(jobs)):
            for back in range(min(steps, 2)):
                for copy in piece_copies(at, lax.rem(step - back, 2), step - back):
                    copy.wait()
        for copy in closing:
            copy.wait()


def conv_frames(frames, halo, weight, clip_ids, parts, first, sources, jobs, plains=(), row=0,
                steps=None, addends=(), sums=(), sums_out=False, layout=None, kept=None, exact=False,
                weigh=1, vmem=56):
    _, band, width, ci = frames.shape
    co = weight.shape[2]
    half = width // 2
    steps = steps or band // 2
    part_width = half // parts
    part_rows = rounded_up(part_width)
    works = list(jobs) + list(plains)
    kept = kept or {}
    messages = parts if jobs else 0
    taps = sorted({tap for _, pairs, _ in works for _, tap in pairs})
    plan = dict(jobs=list(jobs), plains=list(plains), addends=len(addends), parts=messages,
                part_rows=part_rows, layout=layout, part_width=part_width, first=first,
                steps=steps, kept=len(kept), sums_in=len(sums), sums_out=sums_out, sources=sources, taps=taps,
                count=frames.shape[0],
                half=half, co=co, ci=ci)
    above, above_row = (frames, 2 * row - 1) if row else (halo, 0)
    plain_spec = pl.BlockSpec((1, None, half, co), lambda i, *_: (0, row + i, 0, 0))
    frame_spec = lambda source: pl.BlockSpec((1, 2, width, ci), lambda i, *_: (source, row + i, 0, 0))
    above_spec = lambda source: pl.BlockSpec((1, 1, width, ci), lambda i, *_: (source, above_row, 0, 0))
    tap_spec = lambda tap: pl.BlockSpec((1, 9 * ci, co), lambda i, *_: (tap, 0, 0))
    in_specs = [frame_spec(first + source) for source in range(sources)]
    in_specs += [above_spec(first + source) for source in range(sources)]
    in_specs += [tap_spec(tap) for tap in taps]
    in_specs += [plain_spec for _ in addends]
    in_specs += [pl.BlockSpec(a.shape, lambda i, *_: (0, 0, 0)) for a in sums]
    in_specs += [pl.BlockSpec(memory_space=pl.ANY) for _ in kept]
    operands = [clip_ids, *[frames] * sources, *[above] * sources, *[weight] * len(taps),
                *addends, *sums, *kept.values()]
    aliases = {len(operands) - len(kept) + at: flip for at, flip in enumerate(kept)}
    out_shape = [jax.ShapeDtypeStruct((layout[flip][2], co), jnp.bfloat16) for flip in range(messages)]
    out_specs = [pl.BlockSpec(memory_space=pl.ANY) for _ in range(messages)]
    plain_type = jnp.float32 if exact else jnp.bfloat16
    out_shape += [jax.ShapeDtypeStruct((1, band // 2, half, co), plain_type) for _ in plains]
    out_specs += [plain_spec for _ in plains]
    if sums_out:
        shape = (2 * len(jobs), 8, co)
        out_shape.append(jax.ShapeDtypeStruct(shape, jnp.float32))
        out_specs.append(pl.BlockSpec(shape, lambda i, *_: (0, 0, 0)))
    products = sum(len(pairs) for _, pairs, _ in works)
    return pl.pallas_call(
        functools.partial(conv_kernel, plan),
        out_shape=out_shape,
        grid_spec=pltpu.PrefetchScalarGridSpec(
            num_scalar_prefetch=1,
            grid=(steps,),
            in_specs=in_specs,
            out_specs=out_specs,
            scratch_shapes=[
                *[pltpu.VMEM((3, half, 2 * ci), jnp.bfloat16) for _ in range(sources)],
                *[pltpu.VMEM((half, co), jnp.float32) for _ in works],
                *[pltpu.VMEM((8 + half, co), jnp.float32) for _ in works],
                pltpu.VMEM((2, max(len(jobs), 1), parts, part_rows, co), jnp.bfloat16),
                pltpu.VMEM((2 * max(len(jobs), 1), 8, co), jnp.float32),
                pltpu.VMEM((STAT_ROWS, co), jnp.bfloat16),
                pltpu.SemaphoreType.DMA((2, max(len(jobs), 1), parts)),
                pltpu.SemaphoreType.DMA((parts,)),
            ],
        ),
        input_output_aliases=aliases,
        cost_estimate=pl.CostEstimate(
            flops=2 * weigh * products * steps * half * 9 * ci * co,
            bytes_accessed=weigh * (4 * sources * steps * width * ci + 2 * len(works) * steps * half * co),
            transcendentals=0,
        ),
        compiler_params=pltpu.CompilerParams(vmem_limit_bytes=vmem * 1024 * 1024),
    )(*operands)


def norm_kernel(plan, *refs):
    parts, jobs, steps, rows = plan["parts"], plan["jobs"], plan["steps"], plan["rows"]
    part_rows, apart, bases = plan["part_rows"], plan["apart"], plan["bases"]
    data_refs, rest_refs = refs[:parts], refs[parts : parts + len(apart)]
    gain_ref, bias_ref = refs[parts + len(apart) : parts + len(apart) + 2]
    out_ref, done_ref, scale_ref = refs[-3:]
    frame, step = pl.program_id(0), pl.program_id(1)
    part_width, co = out_ref.shape[-2:]

    @pl.when((frame == 0) & (step == 0))
    def _():
        scale_ref[...] = jnp.zeros_like(scale_ref)
        total = 0.0
        for flip, base in enumerate(bases):
            total = total + data_refs[flip][base : base + STAT_ROWS].astype(jnp.float32)
        size = co // GROUPS
        same = (lax.broadcasted_iota(jnp.int32, (co, co), 0) // size
                == lax.broadcasted_iota(jnp.int32, (co, co), 1) // size).astype(jnp.float32)
        grouped = jnp.dot(total, same, precision=lax.Precision.HIGHEST,
                          preferred_element_type=jnp.float32)
        for at in range(jobs):
            def taken(which):
                base = 6 * at + 3 * which
                return grouped[base : base + 1] + grouped[base + 1 : base + 2] + grouped[base + 2 : base + 3]
            mean = taken(0) / plan["entries"]
            variance = taken(1) / plan["entries"] - mean * mean
            scale_ref[at, 0:1] = mean
            scale_ref[at, 1:2] = lax.rsqrt(variance + EPS) * gain_ref[...]

    done_ref[...] = scale_ref[0]
    mean = scale_ref[frame, 0:1]
    scale = scale_ref[frame, 1:2]
    bias = bias_ref[...]
    mine = lax.axis_index("rows")
    top_rows = STAT_ROWS + jobs * part_rows

    def write(flip, at, ref, offset):
        values = ref[pl.ds(pl.multiple_of(offset, 16), part_rows)][0:part_width].astype(jnp.float32)
        value = 0.5 * ((values - mean) * scale + bias)
        out_ref[0, mine ^ flip, at] = (value + value * jnp.tanh(value)).astype(jnp.bfloat16)

    for at in range(rows):
        row = step * rows + at
        for flip in range(parts):
            if not plan["top_first"]:
                write(flip, at, data_refs[flip], bases[flip] + STAT_ROWS + (frame * steps + row) * part_rows)
                continue
            rest, base = data_refs[flip], top_rows
            if flip in apart:
                rest, base = rest_refs[apart.index(flip)], 0
            below = base + (frame * (steps - 1) + row - 1) * part_rows
            if at > 0:
                write(flip, at, rest, below)
                continue

            @pl.when(row == 0)
            def _(flip=flip):
                write(flip, 0, data_refs[flip], STAT_ROWS + frame * part_rows)

            @pl.when(row > 0)
            def _(flip=flip, rest=rest, below=below):
                write(flip, 0, rest, below)


def norm_frames(messages, gain, bias, first, jobs, shape, top_first=False, rest=None, bases=None,
                base=None, vmem=20):
    frames, parts, steps, part_width, co = shape
    rows = 2 if steps % 2 == 0 else 1
    rest = rest or {}
    plan = dict(parts=parts, jobs=jobs, steps=steps, rows=rows, apart=list(rest),
                bases=bases or [0] * parts,
                part_rows=rounded_up(part_width), top_first=top_first,
                entries=float(parts * steps * part_width * parts * (co // GROUPS)))
    in_specs = (
        [pl.BlockSpec(message.shape, lambda f, i, *_: (0, 0)) for message in [*messages, *rest.values()]]
        + [pl.BlockSpec((1, co), lambda f, i, *_: (0, 0))] * 2
    )
    operands = [*messages, *rest.values(), gain, bias]
    aliases = {}
    if base is not None:
        in_specs.append(pl.BlockSpec(memory_space=pl.ANY))
        aliases = {len(operands): 0}
        operands.append(base)
    return pl.pallas_call(
        functools.partial(norm_kernel, plan),
        out_shape=[jax.ShapeDtypeStruct(shape, jnp.bfloat16), jax.ShapeDtypeStruct((8, co), jnp.float32)],
        grid_spec=pltpu.PrefetchScalarGridSpec(
            num_scalar_prefetch=0,
            grid=(jobs, steps // rows),
            in_specs=in_specs,
            out_specs=[
                pl.BlockSpec((1, parts, rows, part_width, co), lambda f, i, *_: (first + f, 0, i, 0, 0)),
                pl.BlockSpec((8, co), lambda f, i, *_: (0, 0)),
            ],
            scratch_shapes=[pltpu.VMEM((jobs, 8, co), jnp.float32)],
        ),
        input_output_aliases=aliases,
        cost_estimate=pl.CostEstimate(
            flops=8 * jobs * parts * steps * part_width * co,
            bytes_accessed=4 * jobs * parts * steps * part_width * co,
            transcendentals=jobs * parts * steps * part_width * co,
        ),
        compiler_params=pltpu.CompilerParams(vmem_limit_bytes=vmem * 1024 * 1024),
    )(*operands)


def on_device(frames, clip_ids, conv_weight, norm_gain, norm_bias):
    count, band, width, ci = frames.shape
    co = conv_weight.shape[4]
    parts = lax.axis_size("rows")
    weight = conv_weight.reshape(3, 9 * ci, co)
    gain, bias = norm_gain.reshape(1, co), norm_bias.reshape(1, co)
    steps = band // 2
    shape = (count, parts, steps, width // 2 // parts, co)
    part_rows = rounded_up(shape[3])
    top_rows = STAT_ROWS + 2 * part_rows
    all_rows = top_rows + 2 * (steps - 1) * part_rows
    one_rows = STAT_ROWS + steps * part_rows

    def named(name, function, *args, **keywords):
        with jax.named_scope(name):
            return function(*args, **keywords)

    def whole(sent, got):
        return [sent[0]] + [got[flip] for flip in range(1, parts)]

    near = [flip for flip in range(1, parts) if 2 * flip < parts]
    far = [flip for flip in range(parts - 1, 0, -1) if 2 * flip >= parts]
    chain = []

    def send_far(name, sent):
        got = {}
        for flip in far:
            before = chain[-3:][:1] if len(chain) >= 3 else []
            got[flip] = named(f"{name}{flip}", exchanged, after(sent[flip], *before), "rows", flip)
            chain.append(got[flip])
        return got

    def send_near(name, sent, single, *earlier):
        got = {}
        for flip in near:
            got[flip] = named(f"{name}{flip}", exchanged, after(sent[flip], *earlier), "rows", flip)
            if single:
                earlier = (got[flip],)
        return got

    def layout(far_one, near_one):
        return [far_one if flip in far else near_one for flip in range(parts)]

    halo = named("halo", passed_along, frames[:, -1:], "rows", 1)
    run = functools.partial(conv_frames, frames, halo, weight, clip_ids, parts)
    later = [(2, [(0, 0), (1, 1), (2, 2)], ()), (3, [(1, 0), (2, 1), (3, 2)], ())]
    near_rows = top_rows + one_rows
    *a_sent, a_sums = named(
        "conv_a", run, 0, 4, later, row=1, steps=steps - 1, sums_out=True, vmem=56,
        layout=[(0, 0, all_rows - top_rows)] * parts)
    held = {}
    a_got = {}

    def send_one(got, name, sent, flip, *earlier):
        got[flip] = named(f"{name}{flip}", exchanged, after(sent[flip], *earlier), "rows", flip)

    for flip in far[:3]:
        send_one(a_got, "a", a_sent, flip)
    send_one(a_got, "a", a_sent, near[0])
    run = functools.partial(conv_frames, frames, after(halo, a_sums), weight, clip_ids, parts)
    ahead, = named("conv_hist0", run, 2, 2, [], [(4, [(0, 0), (1, 1)], ())], weigh=1, vmem=56)
    send_one(a_got, "a", a_sent, near[1], ahead, a_got[near[0]])
    first_add = named("hist0", passed_along, ahead, "tm", 1)
    run = functools.partial(conv_frames, frames, after(halo, ahead, a_got[near[0]]), weight, clip_ids, parts)
    own = named("conv_own", run, 0, 2, [], [(0, [(0, 2)], ()), (1, [(0, 1), (1, 2)], ())],
                exact=True, weigh=20, vmem=56)
    for at, flip in enumerate(near[2:]):
        send_one(a_got, "a", a_sent, flip, own[0], a_got[near[at + 1]])
    for at, flip in enumerate(far[3:]):
        send_one(a_got, "a", a_sent, flip, own[0], a_got[far[at]])
    chain += [a_got[flip] for flip in far]
    run = functools.partial(conv_frames, frames, after(halo, *own, a_got[near[1]]), weight, clip_ids, parts)
    t_sent = named(
        "conv_top", run, 0, 4, later, steps=1, sums=(a_sums,), weigh=20, vmem=56,
        layout=layout((0, STAT_ROWS, top_rows), (0, STAT_ROWS, near_rows)))
    t_got = send_far("t", t_sent)
    run = functools.partial(conv_frames, frames, after(halo, t_sent[0], a_sums), weight, clip_ids, parts)
    onward, = named("conv_hist1", run, 3, 1, [], [(5, [(0, 0)], ())], weigh=20, vmem=56)
    second_add = named("hist1", passed_along, after(onward, first_add, *[a_got[flip] for flip in far]), "tm", 1)
    kept = {flip: t_sent[flip] for flip in range(parts) if flip not in far}
    b_sent = named(
        "add_b", run, 0, 0, [(0, [], (0, 1))], addends=(own[0], after(first_add, a_sums)), kept=kept,
        weigh=20, vmem=56,
        layout=layout((0, STAT_ROWS, one_rows), (top_rows, top_rows + STAT_ROWS, near_rows)))
    b_got = send_far("b", b_sent)
    b_got.update(send_near("tb", b_sent, False, t_got[far[-1]]))
    c_sent = named(
        "add_c", run, 0, 0, [(1, [], (0, 1))], addends=(own[1], after(second_add, b_got[near[0]], b_got[near[1]])),
        weigh=20, vmem=56, layout=[(0, STAT_ROWS, one_rows)] * parts)
    c_got = send_far("c", c_sent)
    c_got.update(send_near("c", c_sent, False))
    both = whole(b_sent, b_got)
    tops = [t_got[flip] if flip in far else both[flip] for flip in range(parts)]
    out, _ = named("norm_a", norm_frames, tops, gain, bias, 2, 2, shape, top_first=True, rest=dict(enumerate(whole(a_sent, a_got))), vmem=20)
    out, _ = named("norm_b", norm_frames, both, gain, bias, 0, 1, shape, base=out, vmem=20,
                   bases=layout(0, top_rows))
    out, _ = named("norm_c", norm_frames, whole(c_sent, c_got), gain, bias, 1, 1, shape, base=out, vmem=20)
    return out.reshape(count, parts * steps, shape[3], co)


def solution(mesh):
    in_specs = (P("tm", "rows", None, None), P(), P(), P(), P())
    out_specs = P("tm", None, "rows", None)
    return jax.shard_map(
        on_device, mesh=mesh, in_specs=in_specs, out_specs=out_specs, check_vma=False
    )
```

```python
import functools

import jax
import jax.numpy as jnp
from jax import lax
from jax.experimental import pallas as pl
from jax.experimental.pallas import tpu as pltpu
from jax.sharding import PartitionSpec as P

GROUPS = 32
EPS = 1e-05
STAT_ROWS = 16


def passed_along(array, axis, by):
    length = lax.axis_size(axis)
    pairs = [(i, i + by) for i in range(length) if 0 <= i + by < length]
    return lax.ppermute(array, axis, pairs)


def exchanged(array, axis, flip):
    length = lax.axis_size(axis)
    return lax.ppermute(array, axis, [(i, i ^ flip) for i in range(length)])


def after(array, *earlier):
    return lax.optimization_barrier((array, *earlier))[0]


def rounded_up(rows):
    return -(-rows // 16) * 16


def split_columns(row_ref, slab_ref):
    width, ci = row_ref.shape
    half = width // 2
    slab_ref[:, 0:ci] = row_ref[pl.ds(0, half, stride=2), :]
    slab_ref[:, ci:] = row_ref[pl.ds(1, half, stride=2), :]


def split_three(total):
    high = total.astype(jnp.bfloat16).astype(jnp.float32)
    rest = total - high
    middle = rest.astype(jnp.bfloat16).astype(jnp.float32)
    return [high, middle, rest - middle]


def conv_kernel(plan, clip_ref, *refs):
    jobs, plains, parts, part_rows, part_width = (
        plan["jobs"], plan["plains"], plan["parts"], plan["part_rows"], plan["part_width"])
    layout, steps, sources, taps = plan["layout"], plan["steps"], plan["sources"], plan["taps"]

    def take(number):
        nonlocal refs
        some, refs = refs[:number], refs[number:]
        return some

    x_refs, above_refs, w_refs = take(sources), take(sources), take(len(taps))
    add_refs = take(plan["addends"])
    sums_refs = take(plan["sums_in"])
    take(plan["kept"])
    out_refs = take(parts)
    plain_refs = take(len(plains))
    sums_out = take(1 if plan["sums_out"] else 0)
    works = jobs + plains
    slab_refs, main_refs, left_refs = take(sources), take(len(works)), take(len(works))
    part_ref, stat_ref, closing_ref, part_sem, tail_sem = refs
    step = pl.program_id(0)
    ci = plan["ci"]
    half, co = plan["half"], plan["co"]
    above = lax.rem(step + 1, 2)
    below = lax.rem(step, 2)
    start = lax.axis_index("tm") * plan["count"]
    last = clip_ref.shape[0] - 1

    @pl.when(step == 0)
    def _():
        for source in range(sources):
            split_columns(above_refs[source].at[0, 0], slab_refs[source].at[1])
        for left_ref in left_refs:
            left_ref[0:8] = jnp.zeros((8, co), jnp.float32)
        stat_ref[...] = jnp.zeros_like(stat_ref)

    def piece_copies(at, slot, step):
        mine = lax.axis_index("rows")
        place = (at * steps + step) * part_rows
        return [
            pltpu.make_async_copy(
                part_ref.at[slot, at, mine ^ flip],
                out.at[pl.ds(pl.multiple_of(layout[flip][1] + place, 16), part_rows)],
                part_sem.at[slot, at, flip])
            for flip, out in enumerate(out_refs)
        ]

    def products(source, tap):
        slab_ref, w_ref = slab_refs[source], w_refs[taps.index(tap)]
        rows = [slab_ref[above], slab_ref[2], slab_ref[below]]
        main = jnp.dot(
            jnp.concatenate(rows, axis=1),
            jnp.concatenate([w_ref[0, (3 * a + 1) * ci : (3 * a + 3) * ci] for a in range(3)], axis=0),
            preferred_element_type=jnp.float32)
        left = jnp.dot(
            jnp.concatenate([row[:, ci:] for row in rows], axis=1),
            jnp.concatenate([w_ref[0, 3 * a * ci : (3 * a + 1) * ci] for a in range(3)], axis=0),
            preferred_element_type=jnp.float32)
        return main, left

    empty = [True] * len(works)
    for source in range(sources):
        split_columns(x_refs[source].at[0, 0], slab_refs[source].at[2])
        split_columns(x_refs[source].at[0, 1], slab_refs[source].at[below])
        frame = plan["first"] + source
        for at, (target, pairs, _) in enumerate(works):
            for tap in [tap for other, tap in pairs if other == source]:
                main, left = products(source, tap)
                if frame != target:
                    same = clip_ref[start + frame] == clip_ref[jnp.minimum(start + target, last)]
                    same = same.astype(jnp.float32)
                    main, left = main * same, left * same
                if empty[at]:
                    main_refs[at][...] = main
                    left_refs[at][8:] = left
                else:
                    main_refs[at][...] += main
                    left_refs[at][8:] += left
                empty[at] = False

    for at, (_, pairs, added) in enumerate(works):
        total = main_refs[at][...] + left_refs[at][7 : 7 + half] if pairs else 0.0
        for addend in added:
            total = total + add_refs[addend][0].astype(jnp.float32)
        if at >= len(jobs):
            plain_refs[at - len(jobs)][0] = total.astype(plain_refs[0].dtype)
            continue
        rounded = total.astype(jnp.bfloat16).astype(jnp.float32)
        tiles = rounded.reshape(half // 8, 8, co)
        stat_ref[2 * at] += jnp.sum(tiles, axis=0)
        stat_ref[2 * at + 1] += jnp.sum(tiles * tiles, axis=0)
        slot = lax.rem(step, 2)

        @pl.when(step >= 2)
        def _(at=at, slot=slot):
            for copy in piece_copies(at, slot, step):
                copy.wait()

        for part in range(parts):
            piece = rounded[part * part_width : (part + 1) * part_width]
            part_ref[slot, at, part, 0:part_width] = piece.astype(jnp.bfloat16)
        for copy in piece_copies(at, slot, step):
            copy.start()

    if not jobs:
        return

    @pl.when(step == steps - 1)
    def _():
        closing = []
        if sums_out:
            sums_out[0][...] = stat_ref[...]
        else:
            rows = []
            for at in range(2 * len(jobs)):
                total = stat_ref[at]
                for ref in sums_refs:
                    total = total + ref[at]
                rows += split_three(jnp.sum(total, axis=0, keepdims=True))
            blank = jnp.zeros((STAT_ROWS - len(rows), co), jnp.float32)
            closing_ref[...] = jnp.concatenate(rows + [blank], axis=0).astype(jnp.bfloat16)
            closing = [
                pltpu.make_async_copy(
                    closing_ref, out.at[layout[flip][0] : layout[flip][0] + STAT_ROWS], tail_sem.at[flip])
                for flip, out in enumerate(out_refs)
            ]
        for copy in closing:
            copy.start()
        for at in range(len(jobs)):
            for back in range(min(steps, 2)):
                for copy in piece_copies(at, lax.rem(step - back, 2), step - back):
                    copy.wait()
        for copy in closing:
            copy.wait()


def conv_frames(frames, halo, weight, clip_ids, parts, first, sources, jobs, plains=(), row=0,
                steps=None, addends=(), sums=(), sums_out=False, layout=None, kept=None, exact=False,
                weigh=1, vmem=56):
    _, band, width, ci = frames.shape
    co = weight.shape[2]
    half = width // 2
    steps = steps or band // 2
    part_width = half // parts
    part_rows = rounded_up(part_width)
    works = list(jobs) + list(plains)
    kept = kept or {}
    messages = parts if jobs else 0
    taps = sorted({tap for _, pairs, _ in works for _, tap in pairs})
    plan = dict(jobs=list(jobs), plains=list(plains), addends=len(addends), parts=messages,
                part_rows=part_rows, layout=layout, part_width=part_width, first=first,
                steps=steps, kept=len(kept), sums_in=len(sums), sums_out=sums_out, sources=sources, taps=taps,
                count=frames.shape[0],
                half=half, co=co, ci=ci)
    above, above_row = (frames, 2 * row - 1) if row else (halo, 0)
    plain_spec = pl.BlockSpec((1, None, half, co), lambda i, *_: (0, row + i, 0, 0))
    frame_spec = lambda source: pl.BlockSpec((1, 2, width, ci), lambda i, *_: (source, row + i, 0, 0))
    above_spec = lambda source: pl.BlockSpec((1, 1, width, ci), lambda i, *_: (source, above_row, 0, 0))
    tap_spec = lambda tap: pl.BlockSpec((1, 9 * ci, co), lambda i, *_: (tap, 0, 0))
    in_specs = [frame_spec(first + source) for source in range(sources)]
    in_specs += [above_spec(first + source) for source in range(sources)]
    in_specs += [tap_spec(tap) for tap in taps]
    in_specs += [plain_spec for _ in addends]
    in_specs += [pl.BlockSpec(a.shape, lambda i, *_: (0, 0, 0)) for a in sums]
    in_specs += [pl.BlockSpec(memory_space=pl.ANY) for _ in kept]
    operands = [clip_ids, *[frames] * sources, *[above] * sources, *[weight] * len(taps),
                *addends, *sums, *kept.values()]
    aliases = {len(operands) - len(kept) + at: flip for at, flip in enumerate(kept)}
    out_shape = [jax.ShapeDtypeStruct((layout[flip][2], co), jnp.bfloat16) for flip in range(messages)]
    out_specs = [pl.BlockSpec(memory_space=pl.ANY) for _ in range(messages)]
    plain_type = jnp.float32 if exact else jnp.bfloat16
    out_shape += [jax.ShapeDtypeStruct((1, band // 2, half, co), plain_type) for _ in plains]
    out_specs += [plain_spec for _ in plains]
    if sums_out:
        shape = (2 * len(jobs), 8, co)
        out_shape.append(jax.ShapeDtypeStruct(shape, jnp.float32))
        out_specs.append(pl.BlockSpec(shape, lambda i, *_: (0, 0, 0)))
    products = sum(len(pairs) for _, pairs, _ in works)
    return pl.pallas_call(
        functools.partial(conv_kernel, plan),
        out_shape=out_shape,
        grid_spec=pltpu.PrefetchScalarGridSpec(
            num_scalar_prefetch=1,
            grid=(steps,),
            in_specs=in_specs,
            out_specs=out_specs,
            scratch_shapes=[
                *[pltpu.VMEM((3, half, 2 * ci), jnp.bfloat16) for _ in range(sources)],
                *[pltpu.VMEM((half, co), jnp.float32) for _ in works],
                *[pltpu.VMEM((8 + half, co), jnp.float32) for _ in works],
                pltpu.VMEM((2, max(len(jobs), 1), parts, part_rows, co), jnp.bfloat16),
                pltpu.VMEM((2 * max(len(jobs), 1), 8, co), jnp.float32),
                pltpu.VMEM((STAT_ROWS, co), jnp.bfloat16),
                pltpu.SemaphoreType.DMA((2, max(len(jobs), 1), parts)),
                pltpu.SemaphoreType.DMA((parts,)),
            ],
        ),
        input_output_aliases=aliases,
        cost_estimate=pl.CostEstimate(
            flops=2 * weigh * products * steps * half * 9 * ci * co,
            bytes_accessed=weigh * (4 * sources * steps * width * ci + 2 * len(works) * steps * half * co),
            transcendentals=0,
        ),
        compiler_params=pltpu.CompilerParams(vmem_limit_bytes=vmem * 1024 * 1024),
    )(*operands)


def norm_kernel(plan, *refs):
    parts, jobs, steps, rows = plan["parts"], plan["jobs"], plan["steps"], plan["rows"]
    part_rows, apart, bases = plan["part_rows"], plan["apart"], plan["bases"]
    data_refs, rest_refs = refs[:parts], refs[parts : parts + len(apart)]
    gain_ref, bias_ref = refs[parts + len(apart) : parts + len(apart) + 2]
    out_ref, done_ref, scale_ref = refs[-3:]
    frame, step = pl.program_id(0), pl.program_id(1)
    part_width, co = out_ref.shape[-2:]

    @pl.when((frame == 0) & (step == 0))
    def _():
        scale_ref[...] = jnp.zeros_like(scale_ref)
        total = 0.0
        for flip, base in enumerate(bases):
            total = total + data_refs[flip][base : base + STAT_ROWS].astype(jnp.float32)
        size = co // GROUPS
        same = (lax.broadcasted_iota(jnp.int32, (co, co), 0) // size
                == lax.broadcasted_iota(jnp.int32, (co, co), 1) // size).astype(jnp.float32)
        grouped = jnp.dot(total, same, precision=lax.Precision.HIGHEST,
                          preferred_element_type=jnp.float32)
        for at in range(jobs):
            def taken(which):
                base = 6 * at + 3 * which
                return grouped[base : base + 1] + grouped[base + 1 : base + 2] + grouped[base + 2 : base + 3]
            mean = taken(0) / plan["entries"]
            variance = taken(1) / plan["entries"] - mean * mean
            scale_ref[at, 0:1] = mean
            scale_ref[at, 1:2] = lax.rsqrt(variance + EPS) * gain_ref[...]

    done_ref[...] = scale_ref[0]
    mean = scale_ref[frame, 0:1]
    scale = scale_ref[frame, 1:2]
    bias = bias_ref[...]
    mine = lax.axis_index("rows")
    top_rows = STAT_ROWS + jobs * part_rows

    def write(flip, at, ref, offset):
        values = ref[pl.ds(pl.multiple_of(offset, 16), part_rows)][0:part_width].astype(jnp.float32)
        value = 0.5 * ((values - mean) * scale + bias)
        out_ref[0, mine ^ flip, at] = (value + value * jnp.tanh(value)).astype(jnp.bfloat16)

    for at in range(rows):
        row = step * rows + at
        for flip in range(parts):
            if not plan["top_first"]:
                write(flip, at, data_refs[flip], bases[flip] + STAT_ROWS + (frame * steps + row) * part_rows)
                continue
            rest, base = data_refs[flip], top_rows
            if flip in apart:
                rest, base = rest_refs[apart.index(flip)], 0
            below = base + (frame * (steps - 1) + row - 1) * part_rows
            if at > 0:
                write(flip, at, rest, below)
                continue

            @pl.when(row == 0)
            def _(flip=flip):
                write(flip, 0, data_refs[flip], STAT_ROWS + frame * part_rows)

            @pl.when(row > 0)
            def _(flip=flip, rest=rest, below=below):
                write(flip, 0, rest, below)


def norm_frames(messages, gain, bias, first, jobs, shape, top_first=False, rest=None, bases=None,
                base=None, vmem=20):
    frames, parts, steps, part_width, co = shape
    rows = 2 if steps % 2 == 0 else 1
    rest = rest or {}
    plan = dict(parts=parts, jobs=jobs, steps=steps, rows=rows, apart=list(rest),
                bases=bases or [0] * parts,
                part_rows=rounded_up(part_width), top_first=top_first,
                entries=float(parts * steps * part_width * parts * (co // GROUPS)))
    in_specs = (
        [pl.BlockSpec(message.shape, lambda f, i, *_: (0, 0)) for message in [*messages, *rest.values()]]
        + [pl.BlockSpec((1, co), lambda f, i, *_: (0, 0))] * 2
    )
    operands = [*messages, *rest.values(), gain, bias]
    aliases = {}
    if base is not None:
        in_specs.append(pl.BlockSpec(memory_space=pl.ANY))
        aliases = {len(operands): 0}
        operands.append(base)
    return pl.pallas_call(
        functools.partial(norm_kernel, plan),
        out_shape=[jax.ShapeDtypeStruct(shape, jnp.bfloat16), jax.ShapeDtypeStruct((8, co), jnp.float32)],
        grid_spec=pltpu.PrefetchScalarGridSpec(
            num_scalar_prefetch=0,
            grid=(jobs, steps // rows),
            in_specs=in_specs,
            out_specs=[
                pl.BlockSpec((1, parts, rows, part_width, co), lambda f, i, *_: (first + f, 0, i, 0, 0)),
                pl.BlockSpec((8, co), lambda f, i, *_: (0, 0)),
            ],
            scratch_shapes=[pltpu.VMEM((jobs, 8, co), jnp.float32)],
        ),
        input_output_aliases=aliases,
        cost_estimate=pl.CostEstimate(
            flops=8 * jobs * parts * steps * part_width * co,
            bytes_accessed=4 * jobs * parts * steps * part_width * co,
            transcendentals=jobs * parts * steps * part_width * co,
        ),
        compiler_params=pltpu.CompilerParams(vmem_limit_bytes=vmem * 1024 * 1024),
    )(*operands)


def on_device(frames, clip_ids, conv_weight, norm_gain, norm_bias):
    count, band, width, ci = frames.shape
    co = conv_weight.shape[4]
    parts = lax.axis_size("rows")
    weight = conv_weight.reshape(3, 9 * ci, co)
    gain, bias = norm_gain.reshape(1, co), norm_bias.reshape(1, co)
    steps = band // 2
    shape = (count, parts, steps, width // 2 // parts, co)
    part_rows = rounded_up(shape[3])
    top_rows = STAT_ROWS + 2 * part_rows
    all_rows = top_rows + 2 * (steps - 1) * part_rows
    one_rows = STAT_ROWS + steps * part_rows

    def named(name, function, *args, **keywords):
        with jax.named_scope(name):
            return function(*args, **keywords)

    def whole(sent, got):
        return [sent[0]] + [got[flip] for flip in range(1, parts)]

    near = [flip for flip in range(1, parts) if 2 * flip < parts]
    far = [flip for flip in range(parts - 1, 0, -1) if 2 * flip >= parts]
    chain = []

    def send_far(name, sent, deep=3):
        got = {}
        for flip in far:
            before = chain[-deep:][:1] if len(chain) >= deep else []
            got[flip] = named(f"{name}{flip}", exchanged, after(sent[flip], *before), "rows", flip)
            chain.append(got[flip])
        return got

    def send_near(name, sent, single, *earlier):
        got = {}
        for flip in near:
            got[flip] = named(f"{name}{flip}", exchanged, after(sent[flip], *earlier), "rows", flip)
            if single:
                earlier = (got[flip],)
        return got

    def layout(far_one, near_one):
        return [far_one if flip in far else near_one for flip in range(parts)]

    halo = named("halo", passed_along, frames[:, -1:], "rows", 1)
    run = functools.partial(conv_frames, frames, halo, weight, clip_ids, parts)
    later = [(2, [(0, 0), (1, 1), (2, 2)], ()), (3, [(1, 0), (2, 1), (3, 2)], ())]
    near_rows = top_rows + one_rows
    *a_sent, a_sums = named(
        "conv_a", run, 0, 4, later, row=1, steps=steps - 1, sums_out=True, vmem=56,
        layout=[(0, 0, all_rows - top_rows)] * parts)
    held = {}
    a_got = {}

    def send_one(got, name, sent, flip, *earlier):
        got[flip] = named(f"{name}{flip}", exchanged, after(sent[flip], *earlier), "rows", flip)

    for flip in far[:3]:
        send_one(a_got, "a", a_sent, flip)
    send_one(a_got, "a", a_sent, near[0])
    run = functools.partial(conv_frames, frames, after(halo, a_sums), weight, clip_ids, parts)
    ahead, = named("conv_hist0", run, 2, 2, [], [(4, [(0, 0), (1, 1)], ())], weigh=1, vmem=56)
    send_one(a_got, "a", a_sent, near[1], ahead, a_got[near[0]])
    first_add = named("hist0", passed_along, ahead, "tm", 1)
    run = functools.partial(conv_frames, frames, after(halo, ahead, a_got[near[0]]), weight, clip_ids, parts)
    own = named("conv_own", run, 0, 2, [], [(0, [(0, 2)], ()), (1, [(0, 1), (1, 2)], ())],
                exact=True, weigh=20, vmem=56)
    for at, flip in enumerate(near[2:]):
        send_one(a_got, "a", a_sent, flip, own[0], a_got[near[at + 1]])
    for at, flip in enumerate(far[3:]):
        send_one(a_got, "a", a_sent, flip, own[0], a_got[far[at]])
    chain += [a_got[flip] for flip in far]
    run = functools.partial(conv_frames, frames, after(halo, *own, a_got[near[1]]), weight, clip_ids, parts)
    t_sent = named(
        "conv_top", run, 0, 4, later, steps=1, sums=(a_sums,), weigh=20, vmem=56,
        layout=layout((0, STAT_ROWS, top_rows), (0, STAT_ROWS, near_rows)))
    t_got = send_far("t", t_sent)
    run = functools.partial(conv_frames, frames, after(halo, t_sent[0], a_sums), weight, clip_ids, parts)
    onward, = named("conv_hist1", run, 3, 1, [], [(5, [(0, 0)], ())], weigh=20, vmem=56)
    second_add = named("hist1", passed_along, after(onward, first_add, *[a_got[flip] for flip in far]), "tm", 1)
    kept = {flip: t_sent[flip] for flip in range(parts) if flip not in far}
    b_sent = named(
        "add_b", run, 0, 0, [(0, [], (0, 1))], addends=(own[0], after(first_add, a_sums)), kept=kept,
        weigh=20, vmem=56,
        layout=layout((0, STAT_ROWS, one_rows), (top_rows, top_rows + STAT_ROWS, near_rows)))
    b_got = send_far("b", b_sent, 4)
    b_got.update(send_near("tb", b_sent, False, b_got[far[0]]))
    c_sent = named(
        "add_c", run, 0, 0, [(1, [], (0, 1))], addends=(own[1], after(second_add, b_got[near[0]], b_got[near[1]])),
        weigh=20, vmem=56, layout=[(0, STAT_ROWS, one_rows)] * parts)
    c_got = send_far("c", c_sent)
    c_got.update(send_near("c", c_sent, False))
    both = whole(b_sent, b_got)
    tops = [t_got[flip] if flip in far else both[flip] for flip in range(parts)]
    out, _ = named("norm_a", norm_frames, tops, gain, bias, 2, 2, shape, top_first=True, rest=dict(enumerate(whole(a_sent, a_got))), vmem=20)
    out, _ = named("norm_b", norm_frames, both, gain, bias, 0, 1, shape, base=out, vmem=20,
                   bases=layout(0, top_rows))
    out, _ = named("norm_c", norm_frames, whole(c_sent, c_got), gain, bias, 1, 1, shape, base=out, vmem=20)
    return out.reshape(count, parts * steps, shape[3], co)


def solution(mesh):
    in_specs = (P("tm", "rows", None, None), P(), P(), P(), P())
    out_specs = P("tm", None, "rows", None)
    return jax.shard_map(
        on_device, mesh=mesh, in_specs=in_specs, out_specs=out_specs, check_vma=False
    )
```
